32 devices in a mesh: wide: 16 (over z, y, core), narrow: 2 (over x).
Axes of the slice: x: 2, y: 2, z: 4, core: 2. Of those that a mesh axis runs over, the one named last changes fastest.
Arguments:
- tokens: bfloat16 [128, 8192], P('wide', 'narrow'), may hold values from -6 to 6
- cotangent: bfloat16 [128, 8192], P('wide', 'narrow'), may hold values from -2.390625 to 2.390625
- gate_vals: bfloat16 [2, 16, 192, 128, 128], P('narrow', 'wide'), may hold values from -0.125 to 0.125
- up_vals: bfloat16 [2, 16, 192, 128, 128], P('narrow', 'wide'), may hold values from -0.125 to 0.125
- gu_index: int32 [2, 16, 192], P('narrow', 'wide'), may hold values from 0 to 255, as said below
- gu_count: int32 [2, 16], P('narrow', 'wide'), may hold values from 1 to 192, as said below
- down_vals: bfloat16 [16, 2, 192, 128, 128], P('wide', 'narrow'), may hold values from -0.09375 to 0.09375
- down_index: int32 [16, 2, 192], P('wide', 'narrow'), may hold values from 0 to 255, as said below
- down_count: int32 [16, 2], P('wide', 'narrow'), may hold values from 1 to 192, as said below
Outputs:
- d_tokens: bfloat16 [128, 8192], P('wide', 'narrow')
- gate_grad: bfloat16 [2, 16, 192, 128, 128], P('narrow', 'wide')
- up_grad: bfloat16 [2, 16, 192, 128, 128], P('narrow', 'wide')
- down_grad: bfloat16 [16, 2, 192, 128, 128], P('wide', 'narrow')
The draws below stay inside these ranges and needn't reach their ends.
Inputs may be any that keep to these rules, and one draw needn't show every extreme that they name: `gu_index`: within each tile all 192 entries are different. `gu_count`: some tile has exactly 192 live slots. `down_index`: within each tile all 192 entries are different. `down_count`: some tile has exactly 192 live slots.
All inputs are finite; a program needn't handle non-finite values.
Results may differ from the reference program's by a relative error of at most 0.005.
Values may be sent and summed in bfloat16 or wider, within the bound.
No kernel may reach another device: no remote copies, remote signals or barrier semaphores. Data moves between devices by JAX's collectives and lax.ppermute only.
A program may use at most 192 MiB of HBM per device.

```python
import jax
import jax.numpy as jnp
from jax import lax

D = 8192
FF = 16384
BLOCK = 128
TOKENS = 128
D_SPLIT = 2
F_SPLIT = 16
D_BLOCKS = 32
F_BLOCKS = 8
SLOTS = 192


def tile_indices(key, tiles_a, tiles_b):
    keys = jax.random.split(key, tiles_a * tiles_b)
    perms = jax.vmap(lambda single: jax.random.permutation(single, D_BLOCKS * F_BLOCKS)[:SLOTS])(keys)
    return perms.reshape(tiles_a, tiles_b, SLOTS).astype(jnp.int32)


def tile_counts(key, tiles_a, tiles_b):
    total = tiles_a * tiles_b
    counts = jax.random.randint(key, (total,), 1, 2 * (D_BLOCKS * F_BLOCKS // 4), dtype=jnp.int32)
    fullest = jax.random.randint(jax.random.fold_in(key, 5), (), 0, total, dtype=jnp.int32)
    counts = jnp.where(jnp.arange(total, dtype=jnp.int32) == fullest, SLOTS, counts)
    return counts.reshape(tiles_a, tiles_b).astype(jnp.int32)


def draw_gu_index(key, part):
    return tile_indices(jax.random.fold_in(key, 11), D_SPLIT, F_SPLIT)


def draw_gu_count(key, part):
    return tile_counts(jax.random.fold_in(key, 23), D_SPLIT, F_SPLIT)


def draw_down_index(key, part):
    return tile_indices(jax.random.fold_in(key, 37), F_SPLIT, D_SPLIT)


def draw_down_count(key, part):
    return tile_counts(jax.random.fold_in(key, 41), F_SPLIT, D_SPLIT)


def level_of(stream_key, dims, shards, least, top_value):
    def one(axis_at, parts):
        draws = jax.random.uniform(jax.random.fold_in(jax.random.fold_in(stream_key, 6), axis_at), (parts,), jnp.float32, least / len(shards), top_value / len(shards))
        return jnp.repeat(jnp.exp(draws), dims[axis_at] // parts).reshape((-1,) + (1,) * (len(dims) - axis_at - 1))

    factor_of = one(*shards[0])
    for cut in shards[1:]:
        factor_of = factor_of * one(*cut)
    return factor_of


def centred(rng, shape, spread, reach, pieces=(), held_as=jnp.bfloat16):
    values = jax.random.normal(rng, shape, jnp.float32) * spread
    if len(pieces) > 0:
        values = level_of(rng, shape, pieces, -0.22, 0.18) * values
    return jnp.clip(values, min=-reach, max=reach).astype(held_as)


def setup_inputs(seed: int = 0) -> dict:
    arg_keys = jax.random.split(jax.random.key(seed), 10)
    return {
        "tokens": centred(arg_keys[0], (TOKENS, D), 1.0, 6.0, ((0, 16), (1, 2))),
        "cotangent": centred(arg_keys[1], (TOKENS, D), 0.4, 2.390625, ((0, 16), (1, 2))),
        "gate_vals": centred(arg_keys[2], (D_SPLIT, F_SPLIT, SLOTS, BLOCK, BLOCK), (D // 4) ** -0.5, 0.125, ((0, 2), (1, 16))),
        "up_vals": centred(arg_keys[3], (D_SPLIT, F_SPLIT, SLOTS, BLOCK, BLOCK), (D // 4) ** -0.5, 0.125, ((0, 2), (1, 16))),
        "gu_index": draw_gu_index(jax.random.fold_in(arg_keys[9], 71), 0),
        "gu_count": draw_gu_count(jax.random.fold_in(arg_keys[9], 71), 0),
        "down_vals": centred(arg_keys[6], (F_SPLIT, D_SPLIT, SLOTS, BLOCK, BLOCK), (FF // 4) ** -0.5, 0.09375, ((0, 16), (1, 2))),
        "down_index": draw_down_index(jax.random.fold_in(arg_keys[9], 71), 0),
        "down_count": draw_down_count(jax.random.fold_in(arg_keys[9], 71), 0),
    }


def place_table(slot_ids, live_count, blocks_total):
    slots_total = slot_ids.shape[2]
    alive = (jnp.arange(slots_total, dtype=jnp.int32)[None, None, :] < live_count[:, :, None]).astype(jnp.float32)
    table = (slot_ids[:, :, :, None] == jnp.arange(blocks_total, dtype=jnp.int32)[None, None, None, :]).astype(jnp.float32)
    return table * alive[:, :, :, None]


def unpack_tiles(tile_values, slot_ids, live_count, row_blocks, col_blocks):
    tiles_a = tile_values.shape[0]
    tiles_b = tile_values.shape[1]
    block_size = tile_values.shape[3]
    placer = place_table(slot_ids, live_count, row_blocks * col_blocks)
    blocks = jnp.einsum("abst,absij->abtij", placer, tile_values.astype(jnp.float32), precision=lax.Precision.HIGHEST)
    blocks = blocks.reshape(tiles_a, tiles_b, row_blocks, col_blocks, block_size, block_size)
    dense = blocks.transpose(0, 2, 4, 1, 3, 5).reshape(tiles_a * row_blocks * block_size, tiles_b * col_blocks * block_size)
    return dense.astype(jnp.bfloat16)


def pack_tiles(dense, slot_ids, live_count, row_blocks, col_blocks, block_size):
    tiles_a = slot_ids.shape[0]
    tiles_b = slot_ids.shape[1]
    blocks = dense.reshape(tiles_a, row_blocks, block_size, tiles_b, col_blocks, block_size).transpose(0, 3, 1, 4, 2, 5)
    blocks = blocks.reshape(tiles_a, tiles_b, row_blocks * col_blocks, block_size, block_size)
    placer = place_table(slot_ids, live_count, row_blocks * col_blocks)
    picked = jnp.einsum("abst,abtij->absij", placer, blocks, precision=lax.Precision.HIGHEST)
    return picked.astype(jnp.bfloat16)


def reference(tokens, cotangent, gate_vals, up_vals, gu_index, gu_count, down_vals, down_index, down_count):
    block_size = gate_vals.shape[-1]
    gate_weight = unpack_tiles(gate_vals, gu_index, gu_count, D_BLOCKS, F_BLOCKS)
    up_weight = unpack_tiles(up_vals, gu_index, gu_count, D_BLOCKS, F_BLOCKS)
    down_weight = unpack_tiles(down_vals, down_index, down_count, F_BLOCKS, D_BLOCKS)
    gate_out = jnp.dot(tokens, gate_weight, preferred_element_type=jnp.float32)
    up_out = jnp.dot(tokens, up_weight, preferred_element_type=jnp.float32)
    sigmoid_g = jax.nn.sigmoid(gate_out)
    hidden = (gate_out * sigmoid_g * up_out).astype(jnp.bfloat16)
    d_hidden = jnp.dot(cotangent, down_weight.T, preferred_element_type=jnp.float32)
    d_gate = (d_hidden * up_out * sigmoid_g * (1.0 + gate_out * (1.0 - sigmoid_g))).astype(jnp.bfloat16)
    d_up = (d_hidden * gate_out * sigmoid_g).astype(jnp.bfloat16)
    d_tokens = jnp.dot(d_gate, gate_weight.T, preferred_element_type=jnp.float32) + jnp.dot(d_up, up_weight.T, preferred_element_type=jnp.float32)
    d_tokens = d_tokens.astype(jnp.bfloat16)
    gate_dense = jnp.dot(tokens.T, d_gate, preferred_element_type=jnp.float32)
    gate_grad = pack_tiles(gate_dense, gu_index, gu_count, D_BLOCKS, F_BLOCKS, block_size)
    up_dense = jnp.dot(tokens.T, d_up, preferred_element_type=jnp.float32)
    up_grad = pack_tiles(up_dense, gu_index, gu_count, D_BLOCKS, F_BLOCKS, block_size)
    down_dense = jnp.dot(hidden.T, cotangent, preferred_element_type=jnp.float32)
    down_grad = pack_tiles(down_dense, down_index, down_count, F_BLOCKS, D_BLOCKS, block_size)
    return (d_tokens, gate_grad, up_grad, down_grad)
```

```python
import functools

import jax
import jax.numpy as jnp
from jax import lax
from jax.experimental import pallas as pl
from jax.experimental.pallas import tpu as pltpu
from jax.sharding import PartitionSpec as P

FF = 16384
F32 = jnp.float32
BF16 = jnp.bfloat16
VMEM_LIMIT = 24 * 1024 * 1024

WHOLE = pl.BlockSpec(memory_space=pltpu.VMEM)
SCALARS = pl.BlockSpec(memory_space=pltpu.SMEM)
ANYWHERE = pl.BlockSpec(memory_space=pl.ANY)


def params():
    return pltpu.CompilerParams(vmem_limit_bytes=VMEM_LIMIT)


def cost(flops, bytes_accessed):
    return pl.CostEstimate(flops=int(flops), bytes_accessed=int(bytes_accessed), transcendentals=0)


def resident(array):
    return pltpu.with_memory_space_constraint(array, pltpu.VMEM)


def swap(array, axis, size, flip):
    return lax.ppermute(array, axis, [(i, i ^ flip) for i in range(size)])


def fill_body(gu_index, gu_count, down_index, down_count, gate, up, down, gate_w, up_w, down_w, sem):
    f_blocks, d_blocks = gate_w.shape[:2]
    zeros = jnp.zeros(gate_w.shape[1:], gate_w.dtype)

    def clear(ref):
        @pl.loop(0, f_blocks)
        def _(c):
            ref[c] = zeros

    def gu_copies(s):
        place = gu_index[s]
        row, col = place // f_blocks, place % f_blocks
        return (
            pltpu.make_async_copy(gate.at[s], gate_w.at[col, row], sem.at[0]),
            pltpu.make_async_copy(up.at[s], up_w.at[col, row], sem.at[0]),
        )

    def down_copy(s):
        place = down_index[s]
        return pltpu.make_async_copy(
            down.at[s], down_w.at[place // d_blocks, place % d_blocks], sem.at[1]
        )

    clear(gate_w)
    clear(up_w)

    @pl.loop(0, gu_count[0])
    def _(s):
        for copy in gu_copies(s):
            copy.start()

    clear(down_w)

    @pl.loop(0, down_count[0])
    def _(s):
        down_copy(s).start()

    @pl.loop(0, gu_count[0])
    def _(s):
        for copy in gu_copies(s):
            copy.wait()

    @pl.loop(0, down_count[0])
    def _(s):
        down_copy(s).wait()


def fill(gu_index, gu_count, down_index, down_count, gate, up, down, f_blocks, d_blocks):
    block = gate.shape[-1]
    dense = pltpu.VMEM((f_blocks, d_blocks, block, block), BF16)
    return pl.pallas_call(
        fill_body,
        out_shape=(dense,) * 3,
        in_specs=[SCALARS] * 4 + [ANYWHERE] * 3,
        out_specs=(WHOLE,) * 3,
        scratch_shapes=[pltpu.SemaphoreType.DMA((2,))],
        compiler_params=params(),
        cost_estimate=cost(0, 3 * gate.size * 2),
        name="fill",
    )(gu_index, gu_count, down_index, down_count, gate, up, down)


def gate_up_body(mine, other, gate_w, up_w, own, send):
    f_blocks, d_blocks, block, _ = gate_w.shape
    x = jnp.concatenate([mine[...], other[...]], axis=0)

    @pl.loop(0, f_blocks)
    def _(c):
        weights = jnp.concatenate(
            [
                gate_w[c].reshape(d_blocks * block, block),
                up_w[c].reshape(d_blocks * block, block),
            ],
            axis=1,
        )
        result = jnp.dot(x, weights, preferred_element_type=F32)
        own[c] = result
        send[c] = result.astype(BF16)


def gate_up(mine, other, gate_w, up_w):
    f_blocks, d_blocks, block, _ = gate_w.shape
    tokens = 2 * mine.shape[0]
    shape = (f_blocks, tokens, 2 * block)
    return pl.pallas_call(
        gate_up_body,
        out_shape=(jax.ShapeDtypeStruct(shape, F32), jax.ShapeDtypeStruct(shape, BF16)),
        in_specs=[WHOLE] * 4,
        out_specs=(WHOLE,) * 2,
        compiler_params=params(),
        cost_estimate=cost(4 * tokens * gate_w.size, 4 * gate_w.size),
        name="gate_up",
    )(mine, other, resident(gate_w), resident(up_w))


def d_hidden_body(mine, other, down_w, own, send):
    f_blocks, d_blocks, block, _ = down_w.shape
    y = jnp.concatenate([mine[...], other[...]], axis=0)

    @pl.loop(0, f_blocks // 2)
    def _(pair):
        weights = jnp.concatenate(
            [
                down_w[pl.ds(2 * pair, 2), d].reshape(2 * block, block)
                for d in range(d_blocks)
            ],
            axis=1,
        )
        result = lax.dot_general(
            y, weights, (((1,), (1,)), ((), ())), preferred_element_type=F32
        )
        for half in range(2):
            part = result[:, half * block : (half + 1) * block]
            own[2 * pair + half] = part
            send[2 * pair + half] = part.astype(BF16)


def d_hidden(mine, other, down_w):
    f_blocks, d_blocks, block, _ = down_w.shape
    tokens = 2 * mine.shape[0]
    shape = (f_blocks, tokens, block)
    return pl.pallas_call(
        d_hidden_body,
        out_shape=(jax.ShapeDtypeStruct(shape, F32), jax.ShapeDtypeStruct(shape, BF16)),
        in_specs=[WHOLE] * 3,
        out_specs=(WHOLE,) * 2,
        compiler_params=params(),
        cost_estimate=cost(2 * tokens * down_w.size, 2 * down_w.size),
        name="d_hidden",
    )(mine, other, resident(down_w))


def d_tokens_body(others, *refs):
    gu_own, dh_own = refs[:2]
    gu_recv = refs[2 : 2 + others]
    dh_recv = refs[2 + others : 2 + 2 * others]
    gate_w, up_w, own, send, d_pair, hidden, packed = refs[2 + 2 * others :]
    f_blocks, d_blocks, block, _ = gate_w.shape
    half = own.shape[0]
    for c in range(f_blocks):
        gu = gu_own[c]
        dh = dh_own[c]
        for k in range(others):
            gu = gu + gu_recv[k][c].astype(F32)
            dh = dh + dh_recv[k][c].astype(F32)
        gate, up = gu[:, :block], gu[:, block:]
        sig = jax.nn.sigmoid(gate)
        silu = gate * sig
        hidden[c] = (silu * up).astype(BF16)
        d_gate = (dh * up * sig * (1.0 + gate * (1.0 - sig))).astype(BF16)
        d_up = (dh * silu).astype(BF16)
        both = jnp.concatenate([d_gate, d_up], axis=1)
        d_pair[c] = both
        packed[:, 2 * block * c : 2 * block * (c + 1)] = both
    grads = packed[...]

    @pl.loop(0, d_blocks // 2)
    def _(pair):
        rows = pl.ds(2 * pair, 2)
        weights = jnp.concatenate(
            [
                ref[c, rows].reshape(2 * block, block)
                for c in range(f_blocks)
                for ref in (gate_w, up_w)
            ],
            axis=1,
        )
        result = lax.dot_general(
            grads, weights, (((1,), (1,)), ((), ())), preferred_element_type=F32
        )
        columns = pl.ds(pl.multiple_of(pair * 2 * block, 2 * block), 2 * block)
        own[:, columns] = result[:half]
        send[:, columns] = result[half:].astype(BF16)


def d_tokens_part(gu_own, dh_own, gu_recv, dh_recv, gate_w, up_w):
    f_blocks, d_blocks, block, _ = gate_w.shape
    tokens = gu_own.shape[1]
    width = d_blocks * block
    others = len(gu_recv)
    return pl.pallas_call(
        functools.partial(d_tokens_body, others),
        out_shape=(
            jax.ShapeDtypeStruct((tokens // 2, width), F32),
            jax.ShapeDtypeStruct((tokens // 2, width), BF16),
            jax.ShapeDtypeStruct((f_blocks, tokens, 2 * block), BF16),
            jax.ShapeDtypeStruct((f_blocks, tokens, block), BF16),
        ),
        in_specs=[WHOLE] * (4 + 2 * others),
        out_specs=(WHOLE,) * 4,
        scratch_shapes=[pltpu.VMEM((tokens, f_blocks * 2 * block), BF16)],
        compiler_params=params(),
        cost_estimate=cost(4 * tokens * gate_w.size, 4 * gate_w.size),
        name="d_tokens",
    )(gu_own, dh_own, *gu_recv, *dh_recv, resident(gate_w), resident(up_w))


def step_slots(slots):
    return max(n for n in range(1, 17) if slots % n == 0)


def gu_grad_body(index, count, mine, other, d_pair, gate_out, up_out, turned):
    f_blocks = d_pair.shape[0]
    d_blocks, block, _ = turned.shape
    step = pl.program_id(0)

    @pl.when(step == 0)
    def _():
        for d in range(d_blocks):
            columns = slice(d * block, (d + 1) * block)
            x = jnp.concatenate([mine[:, columns], other[:, columns]], axis=0)
            turned[d] = x.T

    for j in range(gate_out.shape[0]):
        slot = step * gate_out.shape[0] + j
        place = index[slot]
        result = jnp.dot(
            turned[place // f_blocks], d_pair[place % f_blocks], preferred_element_type=F32
        )
        result = jnp.where(slot < count[0], result, 0.0).astype(BF16)
        gate_out[j] = result[:, :block]
        up_out[j] = result[:, block:]


def gu_grads(index, count, mine, other, d_pair, slots):
    f_blocks, tokens, pair = d_pair.shape
    block = pair // 2
    d_blocks = mine.shape[1] // block
    chunk = step_slots(slots)
    shape = jax.ShapeDtypeStruct((slots, block, block), BF16)
    out = pl.BlockSpec((chunk, block, block), lambda i, *_: (i, 0, 0))
    return pl.pallas_call(
        gu_grad_body,
        out_shape=(shape,) * 2,
        grid_spec=pltpu.PrefetchScalarGridSpec(
            num_scalar_prefetch=2,
            grid=(slots // chunk,),
            in_specs=[WHOLE] * 3,
            out_specs=(out,) * 2,
            scratch_shapes=[pltpu.VMEM((d_blocks, block, tokens), BF16)],
        ),
        compiler_params=params(),
        cost_estimate=cost(4 * slots * block * block * tokens, 4 * slots * block * block),
        name="gu_grads",
    )(index, count, mine, other, d_pair)


def down_grad_body(index, count, mine, other, hidden, out, turned, columns):
    f_blocks = hidden.shape[0]
    d_blocks = columns.shape[0]
    block = hidden.shape[2]
    step = pl.program_id(0)

    @pl.when(step == 0)
    def _():
        for f in range(f_blocks):
            turned[f] = hidden[f].T
        for d in range(d_blocks):
            at = slice(d * block, (d + 1) * block)
            columns[d] = jnp.concatenate([mine[:, at], other[:, at]], axis=0)

    for j in range(out.shape[0]):
        slot = step * out.shape[0] + j
        place = index[slot]
        result = jnp.dot(
            turned[place // d_blocks], columns[place % d_blocks], preferred_element_type=F32
        )
        out[j] = jnp.where(slot < count[0], result, 0.0).astype(BF16)


def down_grads(index, count, mine, other, hidden, slots):
    f_blocks, tokens, block = hidden.shape
    d_blocks = mine.shape[1] // block
    chunk = step_slots(slots)
    return pl.pallas_call(
        down_grad_body,
        out_shape=jax.ShapeDtypeStruct((slots, block, block), BF16),
        grid_spec=pltpu.PrefetchScalarGridSpec(
            num_scalar_prefetch=2,
            grid=(slots // chunk,),
            in_specs=[WHOLE] * 3,
            out_specs=pl.BlockSpec((chunk, block, block), lambda i, *_: (i, 0, 0)),
            scratch_shapes=[
                pltpu.VMEM((f_blocks, block, tokens), BF16),
                pltpu.VMEM((d_blocks, tokens, block), BF16),
            ],
        ),
        compiler_params=params(),
        cost_estimate=cost(2 * slots * block * block * tokens, 2 * slots * block * block),
        name="down_grads",
    )(index, count, mine, other, hidden)


def on_device(
    tokens, cotangent, gate_vals, up_vals, gu_index, gu_count, down_vals, down_index, down_count
):
    block = gate_vals.shape[-1]
    slots = gate_vals.shape[2]
    wide = lax.axis_size("wide")
    narrow = lax.axis_size("narrow")
    chips = wide // 2
    rows = tokens.shape[0]
    d_blocks = tokens.shape[1] // block
    f_blocks = FF // (block * wide)
    gu_index, down_index = gu_index[0, 0], down_index[0, 0]
    gu_count, down_count = gu_count[0], down_count[0]

    def gather(piece):
        pieces = [piece] + [swap(piece, "wide", wide, 2 * k) for k in range(1, chips)]
        return pieces

    def share(pieces):
        mine = jnp.concatenate(pieces, axis=0)
        return mine, swap(mine, "wide", wide, 1)

    def exchange(array):
        return [swap(array, "narrow", narrow, k) for k in range(1, narrow)]

    x_pieces = gather(tokens)
    gate_w, up_w, down_w = fill(
        gu_index, gu_count, down_index, down_count,
        gate_vals[0, 0], up_vals[0, 0], down_vals[0, 0], f_blocks, d_blocks,
    )
    x_pieces, cotangent = lax.optimization_barrier((x_pieces, cotangent))
    y_pieces = gather(cotangent)
    x_mine, x_other = share(x_pieces)
    gu_own, gu_send = gate_up(x_mine, x_other, gate_w, up_w)
    gu_recv = exchange(gu_send)
    y_mine, y_other = share(y_pieces)
    dh_own, dh_send = d_hidden(y_mine, y_other, down_w)
    dh_recv = exchange(dh_send)
    own, send, d_pair, hidden = d_tokens_part(gu_own, dh_own, gu_recv, dh_recv, gate_w, up_w)
    own = own + swap(send, "wide", wide, 1).astype(F32)
    down_grad = down_grads(down_index, down_count, y_mine, y_other, hidden, slots)
    parts = [own[k * rows : (k + 1) * rows] for k in range(chips)]
    sends = [part.astype(BF16) for part in parts[1:]]
    sends, d_pair = lax.optimization_barrier((sends, d_pair))
    gate_grad, up_grad = gu_grads(gu_index, gu_count, x_mine, x_other, d_pair, slots)
    total = parts[0]
    for k in range(1, chips):
        total = total + swap(sends[k - 1], "wide", wide, 2 * k).astype(F32)
    return (
        total.astype(BF16),
        gate_grad[None, None],
        up_grad[None, None],
        down_grad[None, None],
    )


def solution(mesh):
    in_specs = (
        P("wide", "narrow"),
        P("wide", "narrow"),
        P("narrow", "wide", None, None, None),
        P("narrow", "wide", None, None, None),
        P("narrow", "wide", None),
        P("narrow", "wide"),
        P("wide", "narrow", None, None, None),
        P("wide", "narrow", None),
        P("wide", "narrow"),
    )
    out_specs = (
        P("wide", "narrow"),
        P("narrow", "wide", None, None, None),
        P("narrow", "wide", None, None, None),
        P("wide", "narrow", None, None, None),
    )
    return jax.shard_map(
        on_device, mesh=mesh, in_specs=in_specs, out_specs=out_specs, check_vma=False
    )
```

```python
import functools

import jax
import jax.numpy as jnp
from jax import lax
from jax.experimental import pallas as pl
from jax.experimental.pallas import tpu as pltpu
from jax.sharding import PartitionSpec as P

FF = 16384
F32 = jnp.float32
BF16 = jnp.bfloat16
VMEM_LIMIT = 8 * 1024 * 1024

WHOLE = pl.BlockSpec(memory_space=pltpu.VMEM)
SCALARS = pl.BlockSpec(memory_space=pltpu.SMEM)


def params():
    return pltpu.CompilerParams(vmem_limit_bytes=VMEM_LIMIT)


def cost(flops, bytes_accessed):
    return pl.CostEstimate(flops=int(flops), bytes_accessed=int(bytes_accessed), transcendentals=0)


def resident(array):
    return pltpu.with_memory_space_constraint(array, pltpu.VMEM)


def in_hbm(array):
    return pltpu.with_memory_space_constraint(array, pltpu.HBM)


def swap(array, axis, size, flip):
    return lax.ppermute(array, axis, [(i, i ^ flip) for i in range(size)])


def fill_body(gu_index, gu_count, down_index, down_count, gate, up, down, gate_w, up_w, down_w, sem):
    f_blocks, d_blocks = gate_w.shape[:2]
    zeros = jnp.zeros(gate_w.shape[1:], gate_w.dtype)

    def clear(ref):
        @pl.loop(0, f_blocks)
        def _(c):
            ref[c] = zeros

    def gu_copies(s):
        place = gu_index[s]
        row, col = place // f_blocks, place % f_blocks
        return (
            pltpu.make_async_copy(gate.at[s], gate_w.at[col, row], sem.at[0]),
            pltpu.make_async_copy(up.at[s], up_w.at[col, row], sem.at[0]),
        )

    def down_copy(s):
        place = down_index[s]
        return pltpu.make_async_copy(
            down.at[s], down_w.at[place // d_blocks, place % d_blocks], sem.at[1]
        )

    clear(gate_w)
    clear(up_w)

    @pl.loop(0, gu_count[0])
    def _(s):
        for copy in gu_copies(s):
            copy.start()

    clear(down_w)

    @pl.loop(0, down_count[0])
    def _(s):
        down_copy(s).start()

    @pl.loop(0, gu_count[0])
    def _(s):
        for copy in gu_copies(s):
            copy.wait()

    @pl.loop(0, down_count[0])
    def _(s):
        down_copy(s).wait()


def fill(gu_index, gu_count, down_index, down_count, gate, up, down, f_blocks, d_blocks):
    block = gate.shape[-1]
    dense = pltpu.VMEM((f_blocks, d_blocks, block, block), BF16)
    return pl.pallas_call(
        fill_body,
        out_shape=(dense,) * 3,
        in_specs=[SCALARS] * 4 + [pl.BlockSpec(memory_space=pltpu.HBM)] * 3,
        out_specs=(WHOLE,) * 3,
        scratch_shapes=[pltpu.SemaphoreType.DMA((2,))],
        compiler_params=params(),
        cost_estimate=cost(0, 3 * gate.size * 2),
        name="fill",
    )(gu_index, gu_count, down_index, down_count, in_hbm(gate), in_hbm(up), in_hbm(down))


def gate_up_body(mine, other, gate_w, up_w, own, send):
    f_blocks, d_blocks, block, _ = gate_w.shape
    x = jnp.concatenate([mine[...], other[...]], axis=0)

    @pl.loop(0, f_blocks)
    def _(c):
        weights = jnp.concatenate(
            [
                gate_w[c].reshape(d_blocks * block, block),
                up_w[c].reshape(d_blocks * block, block),
            ],
            axis=1,
        )
        result = jnp.dot(x, weights, preferred_element_type=F32)
        own[c] = result
        send[c] = result.astype(BF16)


def gate_up(mine, other, gate_w, up_w):
    f_blocks, d_blocks, block, _ = gate_w.shape
    tokens = 2 * mine.shape[0]
    shape = (f_blocks, tokens, 2 * block)
    return pl.pallas_call(
        gate_up_body,
        out_shape=(jax.ShapeDtypeStruct(shape, F32), jax.ShapeDtypeStruct(shape, BF16)),
        in_specs=[WHOLE] * 4,
        out_specs=(WHOLE,) * 2,
        compiler_params=params(),
        cost_estimate=cost(4 * tokens * gate_w.size, 4 * gate_w.size),
        name="gate_up",
    )(mine, other, resident(gate_w), resident(up_w))


def d_hidden_body(mine, other, down_w, own, send):
    f_blocks, d_blocks, block, _ = down_w.shape
    y = jnp.concatenate([mine[...], other[...]], axis=0)

    @pl.loop(0, f_blocks // 2)
    def _(pair):
        weights = jnp.concatenate(
            [
                down_w[pl.ds(2 * pair, 2), d].reshape(2 * block, block)
                for d in range(d_blocks)
            ],
            axis=1,
        )
        result = lax.dot_general(
            y, weights, (((1,), (1,)), ((), ())), preferred_element_type=F32
        )
        for half in range(2):
            part = result[:, half * block : (half + 1) * block]
            own[2 * pair + half] = part
            send[2 * pair + half] = part.astype(BF16)


def d_hidden(mine, other, down_w):
    f_blocks, d_blocks, block, _ = down_w.shape
    tokens = 2 * mine.shape[0]
    shape = (f_blocks, tokens, block)
    return pl.pallas_call(
        d_hidden_body,
        out_shape=(jax.ShapeDtypeStruct(shape, F32), jax.ShapeDtypeStruct(shape, BF16)),
        in_specs=[WHOLE] * 3,
        out_specs=(WHOLE,) * 2,
        compiler_params=params(),
        cost_estimate=cost(2 * tokens * down_w.size, 2 * down_w.size),
        name="d_hidden",
    )(mine, other, resident(down_w))


def d_tokens_body(others, *refs):
    gu_own, dh_own = refs[:2]
    gu_recv = refs[2 : 2 + others]
    dh_recv = refs[2 + others : 2 + 2 * others]
    gate_w, up_w, own, send, d_pair, hidden, packed = refs[2 + 2 * others :]
    f_blocks, d_blocks, block, _ = gate_w.shape
    half = own.shape[0]
    for c in range(f_blocks):
        gu = gu_own[c]
        dh = dh_own[c]
        for k in range(others):
            gu = gu + gu_recv[k][c].astype(F32)
            dh = dh + dh_recv[k][c].astype(F32)
        gate, up = gu[:, :block], gu[:, block:]
        sig = jax.nn.sigmoid(gate)
        silu = gate * sig
        hidden[c] = (silu * up).astype(BF16)
        d_gate = (dh * up * sig * (1.0 + gate * (1.0 - sig))).astype(BF16)
        d_up = (dh * silu).astype(BF16)
        both = jnp.concatenate([d_gate, d_up], axis=1)
        d_pair[c] = both
        packed[:, 2 * block * c : 2 * block * (c + 1)] = both
    grads = packed[...]

    @pl.loop(0, d_blocks // 2)
    def _(pair):
        rows = pl.ds(2 * pair, 2)
        weights = jnp.concatenate(
            [
                ref[c, rows].reshape(2 * block, block)
                for c in range(f_blocks)
                for ref in (gate_w, up_w)
            ],
            axis=1,
        )
        result = lax.dot_general(
            grads, weights, (((1,), (1,)), ((), ())), preferred_element_type=F32
        )
        columns = pl.ds(pl.multiple_of(pair * 2 * block, 2 * block), 2 * block)
        own[:, columns] = result[:half]
        send[:, columns] = result[half:].astype(BF16)


def d_tokens_part(gu_own, dh_own, gu_recv, dh_recv, gate_w, up_w):
    f_blocks, d_blocks, block, _ = gate_w.shape
    tokens = gu_own.shape[1]
    width = d_blocks * block
    others = len(gu_recv)
    return pl.pallas_call(
        functools.partial(d_tokens_body, others),
        out_shape=(
            jax.ShapeDtypeStruct((tokens // 2, width), F32),
            jax.ShapeDtypeStruct((tokens // 2, width), BF16),
            jax.ShapeDtypeStruct((f_blocks, tokens, 2 * block), BF16),
            jax.ShapeDtypeStruct((f_blocks, tokens, block), BF16),
        ),
        in_specs=[WHOLE] * (4 + 2 * others),
        out_specs=(WHOLE,) * 4,
        scratch_shapes=[pltpu.VMEM((tokens, f_blocks * 2 * block), BF16)],
        compiler_params=params(),
        cost_estimate=cost(4 * tokens * gate_w.size, 4 * gate_w.size),
        name="d_tokens",
    )(gu_own, dh_own, *gu_recv, *dh_recv, resident(gate_w), resident(up_w))


def step_slots(slots):
    return max(n for n in range(1, 17) if slots % n == 0)


def gu_grad_body(index, count, mine, other, d_pair, gate_out, up_out, turned):
    f_blocks = d_pair.shape[0]
    d_blocks, block, _ = turned.shape
    step = pl.program_id(0)

    @pl.when(step == 0)
    def _():
        for d in range(d_blocks):
            columns = slice(d * block, (d + 1) * block)
            x = jnp.concatenate([mine[:, columns], other[:, columns]], axis=0)
            turned[d] = x.T

    for j in range(gate_out.shape[0]):
        slot = step * gate_out.shape[0] + j
        place = index[slot]
        result = jnp.dot(
            turned[place // f_blocks], d_pair[place % f_blocks], preferred_element_type=F32
        )
        result = jnp.where(slot < count[0], result, 0.0).astype(BF16)
        gate_out[j] = result[:, :block]
        up_out[j] = result[:, block:]


def gu_grads(index, count, mine, other, d_pair, slots):
    f_blocks, tokens, pair = d_pair.shape
    block = pair // 2
    d_blocks = mine.shape[1] // block
    chunk = step_slots(slots)
    shape = jax.ShapeDtypeStruct((slots, block, block), BF16)
    out = pl.BlockSpec((chunk, block, block), lambda i, *_: (i, 0, 0))
    return pl.pallas_call(
        gu_grad_body,
        out_shape=(shape,) * 2,
        grid_spec=pltpu.PrefetchScalarGridSpec(
            num_scalar_prefetch=2,
            grid=(slots // chunk,),
            in_specs=[WHOLE] * 3,
            out_specs=(out,) * 2,
            scratch_shapes=[pltpu.VMEM((d_blocks, block, tokens), BF16)],
        ),
        compiler_params=params(),
        cost_estimate=cost(4 * slots * block * block * tokens, 4 * slots * block * block),
        name="gu_grads",
    )(index, count, mine, other, d_pair)


def down_grad_body(index, count, mine, other, hidden, out, turned, columns):
    f_blocks = hidden.shape[0]
    d_blocks = columns.shape[0]
    block = hidden.shape[2]
    step = pl.program_id(0)

    @pl.when(step == 0)
    def _():
        for f in range(f_blocks):
            turned[f] = hidden[f].T
        for d in range(d_blocks):
            at = slice(d * block, (d + 1) * block)
            columns[d] = jnp.concatenate([mine[:, at], other[:, at]], axis=0)

    for j in range(out.shape[0]):
        slot = step * out.shape[0] + j
        place = index[slot]
        result = jnp.dot(
            turned[place // d_blocks], columns[place % d_blocks], preferred_element_type=F32
        )
        out[j] = jnp.where(slot < count[0], result, 0.0).astype(BF16)


def down_grads(index, count, mine, other, hidden, slots):
    f_blocks, tokens, block = hidden.shape
    d_blocks = mine.shape[1] // block
    chunk = step_slots(slots)
    return pl.pallas_call(
        down_grad_body,
        out_shape=jax.ShapeDtypeStruct((slots, block, block), BF16),
        grid_spec=pltpu.PrefetchScalarGridSpec(
            num_scalar_prefetch=2,
            grid=(slots // chunk,),
            in_specs=[WHOLE] * 3,
            out_specs=pl.BlockSpec((chunk, block, block), lambda i, *_: (i, 0, 0)),
            scratch_shapes=[
                pltpu.VMEM((f_blocks, block, tokens), BF16),
                pltpu.VMEM((d_blocks, tokens, block), BF16),
            ],
        ),
        compiler_params=params(),
        cost_estimate=cost(2 * slots * block * block * tokens, 2 * slots * block * block),
        name="down_grads",
    )(index, count, mine, other, hidden)


def on_device(
    tokens, cotangent, gate_vals, up_vals, gu_index, gu_count, down_vals, down_index, down_count
):
    block = gate_vals.shape[-1]
    slots = gate_vals.shape[2]
    wide = lax.axis_size("wide")
    narrow = lax.axis_size("narrow")
    chips = wide // 2
    rows = tokens.shape[0]
    d_blocks = tokens.shape[1] // block
    f_blocks = FF // (block * wide)
    gu_index, down_index = gu_index[0, 0], down_index[0, 0]
    gu_count, down_count = gu_count[0], down_count[0]

    same_core = [[2 * chip + core for chip in range(chips)] for core in range(2)]

    def scatter(array):
        return lax.all_to_all(
            array, "wide", split_axis=0, concat_axis=0, axis_index_groups=same_core, tiled=True
        )

    def gather(piece):
        return scatter(jnp.tile(piece, (chips, 1)))

    def share(mine):
        return mine, swap(mine, "wide", wide, 1)

    def exchange(array):
        return [swap(array, "narrow", narrow, k) for k in range(1, narrow)]

    x_mine = gather(tokens)
    gate_w, up_w, down_w = fill(
        gu_index, gu_count, down_index, down_count,
        gate_vals[0, 0], up_vals[0, 0], down_vals[0, 0], f_blocks, d_blocks,
    )
    x_mine, cotangent = lax.optimization_barrier((x_mine, cotangent))
    y_mine = gather(cotangent)
    x_mine, x_other = share(x_mine)
    gu_own, gu_send = gate_up(x_mine, x_other, gate_w, up_w)
    gu_recv = exchange(gu_send)
    y_mine, y_other = share(y_mine)
    dh_own, dh_send = d_hidden(y_mine, y_other, down_w)
    dh_recv = exchange(dh_send)
    own, send, d_pair, hidden = d_tokens_part(gu_own, dh_own, gu_recv, dh_recv, gate_w, up_w)
    own = own + swap(send, "wide", wide, 1).astype(F32)
    down_grad = down_grads(down_index, down_count, y_mine, y_other, hidden, slots)
    sends, d_pair = lax.optimization_barrier((own.astype(BF16), d_pair))
    gate_grad, up_grad = gu_grads(gu_index, gu_count, x_mine, x_other, d_pair, slots)
    parts = scatter(sends).reshape(chips, rows, -1)
    total = jnp.sum(parts.astype(F32), axis=0)
    return (
        total.astype(BF16),
        gate_grad[None, None],
        up_grad[None, None],
        down_grad[None, None],
    )


def solution(mesh):
    in_specs = (
        P("wide", "narrow"),
        P("wide", "narrow"),
        P("narrow", "wide", None, None, None),
        P("narrow", "wide", None, None, None),
        P("narrow", "wide", None),
        P("narrow", "wide"),
        P("wide", "narrow", None, None, None),
        P("wide", "narrow", None),
        P("wide", "narrow"),
    )
    out_specs = (
        P("wide", "narrow"),
        P("narrow", "wide", None, None, None),
        P("narrow", "wide", None, None, None),
        P("wide", "narrow", None, None, None),
    )
    return jax.shard_map(
        on_device, mesh=mesh, in_specs=in_specs, out_specs=out_specs, check_vma=False
    )
```

```python
import functools

import jax
import jax.numpy as jnp
from jax import lax
from jax.experimental import pallas as pl
from jax.experimental.pallas import tpu as pltpu
from jax.sharding import PartitionSpec as P

FF = 16384
F32 = jnp.float32
BF16 = jnp.bfloat16
VMEM_LIMIT = 8 * 1024 * 1024

WHOLE = pl.BlockSpec(memory_space=pltpu.VMEM)
SCALARS = pl.BlockSpec(memory_space=pltpu.SMEM)


def params():
    return pltpu.CompilerParams(vmem_limit_bytes=VMEM_LIMIT)


def cost(flops, bytes_accessed):
    return pl.CostEstimate(flops=int(flops), bytes_accessed=int(bytes_accessed), transcendentals=0)


def resident(array):
    return pltpu.with_memory_space_constraint(array, pltpu.VMEM)


def in_hbm(array):
    return pltpu.with_memory_space_constraint(array, pltpu.HBM)


def swap(array, axis, size, flip):
    return lax.ppermute(array, axis, [(i, i ^ flip) for i in range(size)])


def reverse_bits(number, size):
    return sum(size >> (bit + 1) for bit in range(size.bit_length() - 1) if number >> bit & 1)


def fill_body(hidden_first, index, count, slots, rows, dense, rows_out, sem):
    f_blocks, d_blocks = dense.shape[:2]

    def slot_copy(s):
        place = index[0, 0, s]
        if hidden_first:
            target = dense.at[place // d_blocks, place % d_blocks]
        else:
            target = dense.at[place % f_blocks, place // f_blocks]
        return pltpu.make_async_copy(slots.at[0, 0, s], target, sem)

    rows_out[...] = rows[...]

    @pl.loop(0, f_blocks)
    def _(c):
        dense[c] = jnp.zeros(dense.shape[1:], dense.dtype)

    @pl.loop(0, count[0, 0])
    def _(s):
        slot_copy(s).start()

    @pl.loop(0, count[0, 0])
    def _(s):
        slot_copy(s).wait()


def fill(index, count, slots, rows, f_blocks, d_blocks, hidden_first):
    block = slots.shape[-1]
    return pl.pallas_call(
        functools.partial(fill_body, hidden_first),
        out_shape=(
            pltpu.VMEM((f_blocks, d_blocks, block, block), BF16),
            jax.ShapeDtypeStruct(rows.shape, rows.dtype),
        ),
        in_specs=[SCALARS] * 2 + [pl.BlockSpec(memory_space=pltpu.HBM), WHOLE],
        out_specs=(WHOLE,) * 2,
        scratch_shapes=[pltpu.SemaphoreType.DMA],
        compiler_params=params(),
        cost_estimate=cost(0, slots.size * 2),
        name="fill",
    )(index, count, in_hbm(slots), rows)


def stack(pieces):
    return jnp.concatenate([piece[...] for piece in pieces], axis=0)


def gate_up_body(*refs):
    *pieces, gate_w, up_w, own, send = refs
    f_blocks, d_blocks, block, _ = gate_w.shape
    x = stack(pieces)

    @pl.loop(0, f_blocks)
    def _(c):
        weights = jnp.concatenate(
            [
                gate_w[c].reshape(d_blocks * block, block),
                up_w[c].reshape(d_blocks * block, block),
            ],
            axis=1,
        )
        result = jnp.dot(x, weights, preferred_element_type=F32)
        own[c] = result
        send[c] = result.astype(BF16)


def gate_up(pieces, gate_w, up_w):
    f_blocks, d_blocks, block, _ = gate_w.shape
    tokens = sum(piece.shape[0] for piece in pieces)
    shape = (f_blocks, tokens, 2 * block)
    return pl.pallas_call(
        gate_up_body,
        out_shape=(jax.ShapeDtypeStruct(shape, F32), jax.ShapeDtypeStruct(shape, BF16)),
        in_specs=[WHOLE] * (len(pieces) + 2),
        out_specs=(WHOLE,) * 2,
        compiler_params=params(),
        cost_estimate=cost(4 * tokens * gate_w.size, 4 * gate_w.size),
        name="gate_up",
    )(*pieces, resident(gate_w), resident(up_w))


def d_hidden_body(*refs):
    *pieces, down_w, own, send = refs
    f_blocks, d_blocks, block, _ = down_w.shape
    y = stack(pieces)

    @pl.loop(0, f_blocks // 2)
    def _(pair):
        weights = jnp.concatenate(
            [
                down_w[pl.ds(2 * pair, 2), d].reshape(2 * block, block)
                for d in range(d_blocks)
            ],
            axis=1,
        )
        result = lax.dot_general(
            y, weights, (((1,), (1,)), ((), ())), preferred_element_type=F32
        )
        for half in range(2):
            part = result[:, half * block : (half + 1) * block]
            own[2 * pair + half] = part
            send[2 * pair + half] = part.astype(BF16)


def d_hidden(pieces, down_w):
    f_blocks, d_blocks, block, _ = down_w.shape
    tokens = sum(piece.shape[0] for piece in pieces)
    shape = (f_blocks, tokens, block)
    return pl.pallas_call(
        d_hidden_body,
        out_shape=(jax.ShapeDtypeStruct(shape, F32), jax.ShapeDtypeStruct(shape, BF16)),
        in_specs=[WHOLE] * (len(pieces) + 1),
        out_specs=(WHOLE,) * 2,
        compiler_params=params(),
        cost_estimate=cost(2 * tokens * down_w.size, 2 * down_w.size),
        name="d_hidden",
    )(*pieces, resident(down_w))


def d_tokens_body(*refs):
    coef, dh_own, *dh_recv, gate_w, up_w, own, send, d_pair, packed = refs
    f_blocks, d_blocks, block, _ = gate_w.shape
    half = own.shape[0]
    for c in range(f_blocks):
        dh = dh_own[c]
        for part in dh_recv:
            dh = dh + part[c].astype(F32)
        both = (jnp.concatenate([dh, dh], axis=1) * coef[c]).astype(BF16)
        d_pair[c] = both
        packed[:, 2 * block * c : 2 * block * (c + 1)] = both
    grads = packed[...]

    @pl.loop(0, d_blocks // 2)
    def _(pair):
        rows = pl.ds(2 * pair, 2)
        weights = jnp.concatenate(
            [
                ref[c, rows].reshape(2 * block, block)
                for c in range(f_blocks)
                for ref in (gate_w, up_w)
            ],
            axis=1,
        )
        result = lax.dot_general(
            grads, weights, (((1,), (1,)), ((), ())), preferred_element_type=F32
        )
        columns = pl.ds(pl.multiple_of(pair * 2 * block, 2 * block), 2 * block)
        own[:, columns] = result[:half]
        send[:, columns] = result[half:].astype(BF16)


def d_tokens_part(coef, dh_own, dh_recv, gate_w, up_w):
    f_blocks, d_blocks, block, _ = gate_w.shape
    tokens = dh_own.shape[1]
    width = d_blocks * block
    return pl.pallas_call(
        d_tokens_body,
        out_shape=(
            jax.ShapeDtypeStruct((tokens // 2, width), F32),
            jax.ShapeDtypeStruct((tokens // 2, width), BF16),
            jax.ShapeDtypeStruct((f_blocks, tokens, 2 * block), BF16),
        ),
        in_specs=[WHOLE] * (4 + len(dh_recv)),
        out_specs=(WHOLE,) * 3,
        scratch_shapes=[pltpu.VMEM((tokens, f_blocks * 2 * block), BF16)],
        compiler_params=params(),
        cost_estimate=cost(4 * tokens * gate_w.size, 4 * gate_w.size),
        name="d_tokens",
    )(coef, dh_own, *dh_recv, resident(gate_w), resident(up_w))


def merge_body(here, own, recv, out):
    chips = out.shape[0]
    bits = chips.bit_length() - 1
    place = sum(((here[0] >> bit) & 1) << (bits - 1 - bit) for bit in range(bits))
    for chip in range(chips):
        at = reverse_bits(chip, chips) ^ place
        out[chip] = (own[at] + recv[at].astype(F32)).astype(BF16)


def merge(chip, own, recv):
    return pl.pallas_call(
        merge_body,
        out_shape=jax.ShapeDtypeStruct(own.shape, BF16),
        in_specs=[SCALARS] + [WHOLE] * 2,
        out_specs=WHOLE,
        compiler_params=params(),
        cost_estimate=cost(own.size, 8 * own.size),
        name="merge",
    )(chip, own, recv)


def step_slots(slots):
    return max(n for n in range(1, 17) if slots % n == 0)


def gu_grad_body(index, count, *refs):
    *pieces, d_pair, gate_out, up_out, turned = refs
    f_blocks = d_pair.shape[0]
    d_blocks, block, _ = turned.shape
    step = pl.program_id(0)

    @pl.when(step == 0)
    def _():
        for d in range(d_blocks):
            columns = slice(d * block, (d + 1) * block)
            turned[d] = jnp.concatenate([piece[:, columns] for piece in pieces], axis=0).T

    for j in range(gate_out.shape[0]):
        slot = step * gate_out.shape[0] + j
        place = index[0, 0, slot]
        result = jnp.dot(
            turned[place // f_blocks], d_pair[place % f_blocks], preferred_element_type=F32
        )
        result = jnp.where(slot < count[0, 0], result, 0.0).astype(BF16)
        gate_out[j] = result[:, :block]
        up_out[j] = result[:, block:]


def gu_grads(index, count, pieces, d_pair, slots):
    f_blocks, tokens, pair = d_pair.shape
    block = pair // 2
    d_blocks = pieces[0].shape[1] // block
    chunk = step_slots(slots)
    shape = jax.ShapeDtypeStruct((slots, block, block), BF16)
    out = pl.BlockSpec((chunk, block, block), lambda i, *_: (i, 0, 0))
    return pl.pallas_call(
        gu_grad_body,
        out_shape=(shape,) * 2,
        grid_spec=pltpu.PrefetchScalarGridSpec(
            num_scalar_prefetch=2,
            grid=(slots // chunk,),
            in_specs=[WHOLE] * (len(pieces) + 1),
            out_specs=(out,) * 2,
            scratch_shapes=[pltpu.VMEM((d_blocks, block, tokens), BF16)],
        ),
        compiler_params=params(),
        cost_estimate=cost(4 * slots * block * block * tokens, 4 * slots * block * block),
        name="gu_grads",
    )(index, count, *pieces, d_pair)


def down_grad_body(pieces_count, index, count, *refs):
    pieces, gu = refs[:pieces_count], refs[pieces_count:-4]
    out, coef, turned, columns = refs[-4:]
    f_blocks = turned.shape[0]
    d_blocks, _, block = columns.shape
    step = pl.program_id(0)

    @pl.when(step == 0)
    def _():
        for f in range(f_blocks):
            both = gu[0][f]
            for part in gu[1:]:
                both = both + part[f].astype(F32)
            gate, up = both[:, :block], both[:, block:]
            sig = jax.nn.sigmoid(gate)
            silu = gate * sig
            turned[f] = (silu * up).astype(BF16).T
            coef[f, :, :block] = up * sig * (1.0 + gate * (1.0 - sig))
            coef[f, :, block:] = silu
        for d in range(d_blocks):
            at = slice(d * block, (d + 1) * block)
            columns[d] = jnp.concatenate([piece[:, at] for piece in pieces], axis=0)

    for j in range(out.shape[0]):
        slot = step * out.shape[0] + j
        place = index[0, 0, slot]
        result = jnp.dot(
            turned[place // d_blocks], columns[place % d_blocks], preferred_element_type=F32
        )
        out[j] = jnp.where(slot < count[0, 0], result, 0.0).astype(BF16)


def down_grads(index, count, pieces, gu_own, gu_recv, slots):
    f_blocks, tokens, pair = gu_own.shape
    block = pair // 2
    d_blocks = pieces[0].shape[1] // block
    chunk = step_slots(slots)
    return pl.pallas_call(
        functools.partial(down_grad_body, len(pieces)),
        out_shape=(
            jax.ShapeDtypeStruct((slots, block, block), BF16),
            jax.ShapeDtypeStruct(gu_own.shape, F32),
        ),
        grid_spec=pltpu.PrefetchScalarGridSpec(
            num_scalar_prefetch=2,
            grid=(slots // chunk,),
            in_specs=[WHOLE] * (len(pieces) + 1 + len(gu_recv)),
            out_specs=(pl.BlockSpec((chunk, block, block), lambda i, *_: (i, 0, 0)), WHOLE),
            scratch_shapes=[
                pltpu.VMEM((f_blocks, block, tokens), BF16),
                pltpu.VMEM((d_blocks, tokens, block), BF16),
            ],
        ),
        compiler_params=params(),
        cost_estimate=cost(2 * slots * block * block * tokens, 2 * slots * block * block),
        name="down_grads",
    )(index, count, *pieces, gu_own, *gu_recv)


def on_device(
    tokens, cotangent, gate_vals, up_vals, gu_index, gu_count, down_vals, down_index, down_count
):
    block = gate_vals.shape[-1]
    slots = gate_vals.shape[2]
    wide = lax.axis_size("wide")
    narrow = lax.axis_size("narrow")
    chips = wide // 2
    rows = tokens.shape[0]
    d_blocks = tokens.shape[1] // block
    f_blocks = FF // (block * wide)

    def exchange(array):
        return [swap(array, "narrow", narrow, k) for k in range(1, narrow)]

    fills = [
        functools.partial(fill, gu_index, gu_count, gate_vals, hidden_first=False),
        functools.partial(fill, gu_index, gu_count, up_vals, hidden_first=False),
        functools.partial(fill, down_index, down_count, down_vals, hidden_first=True),
    ]
    weights = []

    x, y = tokens, cotangent
    flips = [chips >> hop for hop in range(1, chips.bit_length())]
    for hop, flip in enumerate(flips):
        if hop > 0:
            x = jnp.concatenate([x, x_recv], axis=0)
            y = jnp.concatenate([y, y_recv], axis=0)
        x_recv = swap(x, "wide", wide, 2 * flip)
        y_recv = swap(y, "wide", wide, 2 * flip)
        last = hop == len(flips) - 1
        if last:
            x_across = swap(x, "wide", wide, 1)
            y_across = swap(y, "wide", wide, 1)
        while len(weights) < len(fills) and (last or len(weights) <= hop):
            dense, x = fills[len(weights)](rows=x, f_blocks=f_blocks, d_blocks=d_blocks)
            weights.append(dense)
    x_pieces = [x, x_recv, x_across, swap(x_recv, "wide", wide, 1)]
    y_pieces = [y, y_recv, y_across, swap(y_recv, "wide", wide, 1)]
    gate_w, up_w, down_w = weights

    gu_own, gu_send = gate_up(x_pieces, gate_w, up_w)
    gu_recv = exchange(gu_send)
    dh_own, dh_send = d_hidden(y_pieces, down_w)
    dh_recv = exchange(dh_send)
    down_grad, coef = down_grads(down_index, down_count, y_pieces, gu_own, gu_recv, slots)
    own, send, d_pair = d_tokens_part(coef, dh_own, dh_recv, gate_w, up_w)
    across = swap(send, "wide", wide, 1)
    chip = lax.shift_right_logical(lax.axis_index("wide"), 1)[None]
    split = (chips, rows, tokens.shape[1])
    merged = merge(chip, own.reshape(split), across.reshape(split))
    merged, d_pair = lax.optimization_barrier((merged, d_pair))
    gate_grad, up_grad = gu_grads(gu_index, gu_count, x_pieces, d_pair, slots)
    same_core = [[2 * chip + core for chip in range(chips)] for core in range(2)]
    parts = lax.all_to_all(
        merged, "wide", split_axis=0, concat_axis=0, axis_index_groups=same_core, tiled=True
    )
    total = jnp.sum(parts.astype(F32), axis=0)
    return (
        total.astype(BF16),
        gate_grad[None, None],
        up_grad[None, None],
        down_grad[None, None],
    )


def solution(mesh):
    in_specs = (
        P("wide", "narrow"),
        P("wide", "narrow"),
        P("narrow", "wide", None, None, None),
        P("narrow", "wide", None, None, None),
        P("narrow", "wide", None),
        P("narrow", "wide"),
        P("wide", "narrow", None, None, None),
        P("wide", "narrow", None),
        P("wide", "narrow"),
    )
    out_specs = (
        P("wide", "narrow"),
        P("narrow", "wide", None, None, None),
        P("narrow", "wide", None, None, None),
        P("wide", "narrow", None, None, None),
    )
    return jax.shard_map(
        on_device, mesh=mesh, in_specs=in_specs, out_specs=out_specs, check_vma=False
    )
```

```python
import functools

import jax
import jax.numpy as jnp
from jax import lax
from jax.experimental import pallas as pl
from jax.experimental.pallas import tpu as pltpu
from jax.sharding import PartitionSpec as P

FF = 16384
F32 = jnp.float32
BF16 = jnp.bfloat16
VMEM_LIMIT = 8 * 1024 * 1024

WHOLE = pl.BlockSpec(memory_space=pltpu.VMEM)
SCALARS = pl.BlockSpec(memory_space=pltpu.SMEM)


def params():
    return pltpu.CompilerParams(vmem_limit_bytes=VMEM_LIMIT)


def cost(flops, bytes_accessed):
    return pl.CostEstimate(flops=int(flops), bytes_accessed=int(bytes_accessed), transcendentals=0)


def resident(array):
    return pltpu.with_memory_space_constraint(array, pltpu.VMEM)


def in_hbm(array):
    return pltpu.with_memory_space_constraint(array, pltpu.HBM)


def swap(array, axis, size, flip):
    return lax.ppermute(array, axis, [(i, i ^ flip) for i in range(size)])


def split_index(number, size):
    if size & (size - 1):
        return number // size, number % size
    return number >> (size.bit_length() - 1), number & (size - 1)


def reverse_bits(number, size):
    return sum(size >> (bit + 1) for bit in range(size.bit_length() - 1) if number >> bit & 1)


def fill_body(index, count, slots, dense, seen, sem):
    outer, inner = dense.shape[:2]
    live = count[0, 0]
    chunk = min(inner, 8)

    @pl.loop(0, outer * inner, unroll=8)
    def _(place):
        seen[place] = 0

    @pl.loop(0, live)
    def _(s):
        place = index[0, 0, s]
        seen[place] = 1
        high, low = split_index(place, inner)
        pltpu.make_async_copy(slots.at[0, 0, s], dense.at[high, low], sem).start()

    @pl.loop(0, outer)
    def _(high):
        for low in range(inner):

            @pl.when(seen[high * inner + low] == 0)
            def _():
                dense[high, low] = jnp.zeros(dense.shape[2:], dense.dtype)

    many, few = split_index(live, chunk)

    @pl.loop(0, many)
    def _(_):
        blocks = pl.ds(0, chunk)
        pltpu.make_async_copy(slots.at[0, 0, blocks], dense.at[0, blocks], sem).wait()

    @pl.loop(0, few)
    def _(_):
        pltpu.make_async_copy(slots.at[0, 0, 0], dense.at[0, 0], sem).wait()


def fill(index, count, slots, outer, inner):
    block = slots.shape[-1]
    return pl.pallas_call(
        fill_body,
        out_shape=pltpu.VMEM((outer, inner, block, block), BF16),
        in_specs=[SCALARS] * 2 + [pl.BlockSpec(memory_space=pltpu.HBM)],
        out_specs=WHOLE,
        scratch_shapes=[pltpu.SMEM((outer * inner,), jnp.int32), pltpu.SemaphoreType.DMA],
        compiler_params=params(),
        cost_estimate=cost(0, slots.size * 2),
        name="fill",
    )(index, count, in_hbm(slots))


def stack(pieces):
    return jnp.concatenate([piece[...] for piece in pieces], axis=0)


def gate_up_body(*refs):
    *pieces, gate_w, up_w, own, send = refs
    d_blocks, f_blocks, block, _ = gate_w.shape
    x = stack(pieces)

    @pl.loop(0, f_blocks)
    def _(c):
        weights = jnp.concatenate(
            [
                gate_w[:, c].reshape(d_blocks * block, block),
                up_w[:, c].reshape(d_blocks * block, block),
            ],
            axis=1,
        )
        result = jnp.dot(x, weights, preferred_element_type=F32)
        own[c] = result
        send[c] = result.astype(BF16)


def gate_up(pieces, gate_w, up_w):
    d_blocks, f_blocks, block, _ = gate_w.shape
    tokens = sum(piece.shape[0] for piece in pieces)
    shape = (f_blocks, tokens, 2 * block)
    return pl.pallas_call(
        gate_up_body,
        out_shape=(jax.ShapeDtypeStruct(shape, F32), jax.ShapeDtypeStruct(shape, BF16)),
        in_specs=[WHOLE] * (len(pieces) + 2),
        out_specs=(WHOLE,) * 2,
        compiler_params=params(),
        cost_estimate=cost(4 * tokens * gate_w.size, 4 * gate_w.size),
        name="gate_up",
    )(*pieces, resident(gate_w), resident(up_w))


def d_hidden_body(pieces_count, *refs):
    y_pieces, x_pieces = refs[:pieces_count], refs[pieces_count : 2 * pieces_count]
    down_w, own, send, turned = refs[2 * pieces_count :]
    f_blocks, d_blocks, block, _ = down_w.shape
    y = stack(y_pieces)

    @pl.loop(0, f_blocks // 2)
    def _(pair):
        weights = jnp.concatenate(
            [
                down_w[pl.ds(2 * pair, 2), d].reshape(2 * block, block)
                for d in range(d_blocks)
            ],
            axis=1,
        )
        result = lax.dot_general(
            y, weights, (((1,), (1,)), ((), ())), preferred_element_type=F32
        )
        for half in range(2):
            part = result[:, half * block : (half + 1) * block]
            own[2 * pair + half] = part
            send[2 * pair + half] = part.astype(BF16)

    for d in range(d_blocks):
        columns = slice(d * block, (d + 1) * block)
        turned[d] = jnp.concatenate([piece[:, columns] for piece in x_pieces], axis=0).T


def d_hidden(y_pieces, x_pieces, down_w):
    f_blocks, d_blocks, block, _ = down_w.shape
    tokens = sum(piece.shape[0] for piece in y_pieces)
    shape = (f_blocks, tokens, block)
    return pl.pallas_call(
        functools.partial(d_hidden_body, len(y_pieces)),
        out_shape=(
            jax.ShapeDtypeStruct(shape, F32),
            jax.ShapeDtypeStruct(shape, BF16),
            jax.ShapeDtypeStruct((d_blocks, block, tokens), BF16),
        ),
        in_specs=[WHOLE] * (2 * len(y_pieces) + 1),
        out_specs=(WHOLE,) * 3,
        compiler_params=params(),
        cost_estimate=cost(2 * tokens * down_w.size, 2 * down_w.size),
        name="d_hidden",
    )(*y_pieces, *x_pieces, resident(down_w))


def d_tokens_body(group, *refs):
    coef, dh_own, *dh_recv, gate_w, up_w, own, send, d_pair, turned = refs
    d_blocks, f_blocks, block, _ = gate_w.shape
    half = own.shape[0]
    for c in range(f_blocks):
        dh = dh_own[c]
        for part in dh_recv:
            dh = dh + part[c].astype(F32)
        both = (jnp.concatenate([dh, dh], axis=1) * coef[c]).astype(BF16)
        d_pair[c] = both
        for side in range(2):
            turned[pl.ds((2 * c + side) * block, block), :] = both[
                :, side * block : (side + 1) * block
            ].T
    grads = turned[...]

    @pl.loop(0, d_blocks // group)
    def _(at):
        rows = pl.ds(at * group, group)
        weights = jnp.concatenate(
            [
                ref[rows, c].reshape(group * block, block)
                for c in range(f_blocks)
                for ref in (gate_w, up_w)
            ],
            axis=1,
        )
        result = jnp.dot(weights, grads, preferred_element_type=F32).T
        columns = pl.ds(pl.multiple_of(at * group * block, group * block), group * block)
        own[:, columns] = result[:half]
        send[:, columns] = result[half:].astype(BF16)


def d_tokens_part(coef, dh_own, dh_recv, gate_w, up_w):
    d_blocks, f_blocks, block, _ = gate_w.shape
    tokens = dh_own.shape[1]
    width = d_blocks * block
    group = max(n for n in (1, 2, 4) if d_blocks % n == 0)
    return pl.pallas_call(
        functools.partial(d_tokens_body, group),
        out_shape=(
            jax.ShapeDtypeStruct((tokens // 2, width), F32),
            jax.ShapeDtypeStruct((tokens // 2, width), BF16),
            jax.ShapeDtypeStruct((f_blocks, tokens, 2 * block), BF16),
        ),
        in_specs=[WHOLE] * (4 + len(dh_recv)),
        out_specs=(WHOLE,) * 3,
        scratch_shapes=[pltpu.VMEM((f_blocks * 2 * block, tokens), BF16)],
        compiler_params=params(),
        cost_estimate=cost(4 * tokens * gate_w.size, 4 * gate_w.size),
        name="d_tokens",
    )(coef, dh_own, *dh_recv, resident(gate_w), resident(up_w))


def step_slots(slots):
    return max(n for n in range(1, 17) if slots % n == 0)


def gu_grad_body(first, index, count, d_pair, turned, *refs):
    gate_out, up_out = refs[-2:]
    f_blocks = d_pair.shape[0]
    block = turned.shape[1]
    step = pl.program_id(0) + first

    for j in range(gate_out.shape[0]):
        slot = step * gate_out.shape[0] + j
        d, f = split_index(index[0, 0, slot], f_blocks)
        result = jnp.dot(turned[d], d_pair[f], preferred_element_type=F32)
        result = jnp.where(slot < count[0, 0], result, 0.0).astype(BF16)
        gate_out[j] = result[:, :block]
        up_out[j] = result[:, block:]


def gu_grads(index, count, d_pair, turned, slots, part, parts, before):
    block, tokens = turned.shape[1:]
    chunk = step_slots(slots // parts)
    steps = slots // parts // chunk
    first = part * steps
    shape = jax.ShapeDtypeStruct((slots, block, block), BF16)
    out = pl.BlockSpec((chunk, block, block), lambda i, *_: (i + first, 0, 0))
    flops = 4 * slots * block * block * tokens
    return pl.pallas_call(
        functools.partial(gu_grad_body, first),
        out_shape=(shape,) * 2,
        grid_spec=pltpu.PrefetchScalarGridSpec(
            num_scalar_prefetch=2,
            grid=(steps,),
            in_specs=[WHOLE] * 2 + [pl.BlockSpec(memory_space=pl.ANY)] * len(before),
            out_specs=(out,) * 2,
        ),
        input_output_aliases={4 + at: at for at in range(len(before))},
        compiler_params=params(),
        cost_estimate=cost(flops // parts, 4 * slots * block * block // parts),
        name="gu_grads",
    )(index, count, d_pair, turned, *before)


def down_grad_body(pieces_count, index, count, *refs):
    pieces, gu = refs[:pieces_count], refs[pieces_count:-4]
    out, coef, turned, columns = refs[-4:]
    f_blocks = turned.shape[0]
    d_blocks, _, block = columns.shape
    step = pl.program_id(0)

    @pl.when(step == 0)
    def _():
        for f in range(f_blocks):
            both = gu[0][f]
            for part in gu[1:]:
                both = both + part[f].astype(F32)
            gate, up = both[:, :block], both[:, block:]
            sig = jax.nn.sigmoid(gate)
            silu = gate * sig
            turned[f] = (silu * up).astype(BF16).T
            coef[f, :, :block] = up * sig * (1.0 + gate * (1.0 - sig))
            coef[f, :, block:] = silu
        for d in range(d_blocks):
            at = slice(d * block, (d + 1) * block)
            columns[d] = jnp.concatenate([piece[:, at] for piece in pieces], axis=0)

    for j in range(out.shape[0]):
        slot = step * out.shape[0] + j
        f, d = split_index(index[0, 0, slot], d_blocks)
        result = jnp.dot(turned[f], columns[d], preferred_element_type=F32)
        out[j] = jnp.where(slot < count[0, 0], result, 0.0).astype(BF16)


def down_grads(index, count, pieces, gu_own, gu_recv, slots):
    f_blocks, tokens, pair = gu_own.shape
    block = pair // 2
    d_blocks = pieces[0].shape[1] // block
    chunk = step_slots(slots)
    return pl.pallas_call(
        functools.partial(down_grad_body, len(pieces)),
        out_shape=(
            jax.ShapeDtypeStruct((slots, block, block), BF16),
            jax.ShapeDtypeStruct(gu_own.shape, F32),
        ),
        grid_spec=pltpu.PrefetchScalarGridSpec(
            num_scalar_prefetch=2,
            grid=(slots // chunk,),
            in_specs=[WHOLE] * (len(pieces) + 1 + len(gu_recv)),
            out_specs=(pl.BlockSpec((chunk, block, block), lambda i, *_: (i, 0, 0)), WHOLE),
            scratch_shapes=[
                pltpu.VMEM((f_blocks, block, tokens), BF16),
                pltpu.VMEM((d_blocks, tokens, block), BF16),
            ],
        ),
        compiler_params=params(),
        cost_estimate=cost(2 * slots * block * block * tokens, 2 * slots * block * block),
        name="down_grads",
    )(index, count, *pieces, gu_own, *gu_recv)


def on_device(
    tokens, cotangent, gate_vals, up_vals, gu_index, gu_count, down_vals, down_index, down_count
):
    block = gate_vals.shape[-1]
    slots = gate_vals.shape[2]
    wide = lax.axis_size("wide")
    narrow = lax.axis_size("narrow")
    chips = wide // 2
    rows = tokens.shape[0]
    d_blocks = tokens.shape[1] // block
    f_blocks = FF // (block * wide)

    def exchange(array):
        return [swap(array, "narrow", narrow, k) for k in range(1, narrow)]

    x, y = tokens, cotangent
    weights = []
    index = gu_index
    flips = [chips >> hop for hop in range(1, chips.bit_length())]
    for hop, flip in enumerate(flips):
        if hop > 0:
            x = jnp.concatenate([x, x_recv], axis=0)
            y = jnp.concatenate([y, y_recv], axis=0)
            x, weights, index = lax.optimization_barrier((x, weights, index))
        x_recv = swap(x, "wide", wide, 2 * flip)
        if hop == len(flips) - 1:
            x_across = swap(x, "wide", wide, 1)
        if len(weights) < 2:
            slots_of = (gate_vals, up_vals)[hop]
            weights.append(fill(index, gu_count, slots_of, d_blocks, f_blocks))
        y, _ = lax.optimization_barrier((y, x_recv))
        y_recv = swap(y, "wide", wide, 2 * flip)
    x_pieces = [x, x_recv, x_across, swap(x_recv, "wide", wide, 1)]
    gate_w, up_w = weights

    gu_own, gu_send = gate_up(x_pieces, gate_w, up_w)
    gu_recv = exchange(gu_send)
    late_index, y, y_recv, _ = lax.optimization_barrier((down_index, y, y_recv, gu_send))
    y_across = swap(y, "wide", wide, 1)
    down_w = fill(late_index, down_count, down_vals, f_blocks, d_blocks)
    y_pieces = [y, y_recv, y_across, swap(y_recv, "wide", wide, 1)]
    dh_own, dh_send, turned = d_hidden(y_pieces, x_pieces, down_w)
    dh_recv = exchange(dh_send)
    down_grad, coef = down_grads(down_index, down_count, y_pieces, gu_own, gu_recv, slots)
    own, send, d_pair = d_tokens_part(coef, dh_own, dh_recv, gate_w, up_w)

    own = own + swap(send, "wide", wide, 1).astype(F32)
    kept = chips // 2 * rows
    far = own[kept:].astype(BF16)
    own = own[:kept]
    parts = 2 if slots % 2 == 0 else 1
    far, d_pair = lax.optimization_barrier((far, d_pair))
    grads = gu_grads(gu_index, gu_count, d_pair, turned, slots, 0, parts, ())
    own = own + swap(far, "wide", wide, 2).astype(F32)
    sends = [own[p * rows : (p + 1) * rows].astype(BF16) for p in range(1, chips // 2)]
    if parts == 2:
        sends, d_pair = lax.optimization_barrier((sends, d_pair))
        grads = gu_grads(gu_index, gu_count, d_pair, turned, slots, 1, parts, grads)
    gate_grad, up_grad = grads
    total = own[:rows]
    for p, part in enumerate(sends, 1):
        total = total + swap(part, "wide", wide, 2 * reverse_bits(p, chips)).astype(F32)
    return (
        total.astype(BF16),
        gate_grad[None, None],
        up_grad[None, None],
        down_grad[None, None],
    )


def solution(mesh):
    in_specs = (
        P("wide", "narrow"),
        P("wide", "narrow"),
        P("narrow", "wide", None, None, None),
        P("narrow", "wide", None, None, None),
        P("narrow", "wide", None),
        P("narrow", "wide"),
        P("wide", "narrow", None, None, None),
        P("wide", "narrow", None),
        P("wide", "narrow"),
    )
    out_specs = (
        P("wide", "narrow"),
        P("narrow", "wide", None, None, None),
        P("narrow", "wide", None, None, None),
        P("wide", "narrow", None, None, None),
    )
    return jax.shard_map(
        on_device, mesh=mesh, in_specs=in_specs, out_specs=out_specs, check_vma=False
    )
```

```python
import functools

import jax
import jax.numpy as jnp
from jax import lax
from jax.experimental import pallas as pl
from jax.experimental.pallas import tpu as pltpu
from jax.sharding import PartitionSpec as P

FF = 16384
F32 = jnp.float32
BF16 = jnp.bfloat16
VMEM_LIMIT = 8 * 1024 * 1024

WHOLE = pl.BlockSpec(memory_space=pltpu.VMEM)
SCALARS = pl.BlockSpec(memory_space=pltpu.SMEM)


def params():
    return pltpu.CompilerParams(vmem_limit_bytes=VMEM_LIMIT)


def cost(flops, bytes_accessed):
    return pl.CostEstimate(flops=int(flops), bytes_accessed=int(bytes_accessed), transcendentals=0)


def resident(array):
    return pltpu.with_memory_space_constraint(array, pltpu.VMEM)


def in_hbm(array):
    return pltpu.with_memory_space_constraint(array, pltpu.HBM)


def swap(array, axis, size, flip):
    return lax.ppermute(array, axis, [(i, i ^ flip) for i in range(size)])


def split_index(number, size):
    if size & (size - 1):
        return number // size, number % size
    return number >> (size.bit_length() - 1), number & (size - 1)


def reverse_bits(number, size):
    return sum(size >> (bit + 1) for bit in range(size.bit_length() - 1) if number >> bit & 1)


def fill_body(arrays, index, count, *refs):
    slots, dense, sem = refs[:arrays], refs[arrays : 2 * arrays], refs[2 * arrays]
    outer, inner = dense[0].shape[:2]
    live = count[0, 0]
    chunk = min(inner, 8)

    for source, target in zip(slots, dense):

        @pl.loop(0, outer)
        def _(high):
            target[high] = jnp.zeros(target.shape[1:], target.dtype)

        @pl.loop(0, live)
        def _(s):
            high, low = split_index(index[0, 0, s], inner)
            pltpu.make_async_copy(source.at[0, 0, s], target.at[high, low], sem).start()

    many, few = split_index(live, chunk)
    for source, target in zip(slots, dense):

        @pl.loop(0, many)
        def _(_):
            blocks = pl.ds(0, chunk)
            pltpu.make_async_copy(source.at[0, 0, blocks], target.at[0, blocks], sem).wait()

        @pl.loop(0, few)
        def _(_):
            pltpu.make_async_copy(source.at[0, 0, 0], target.at[0, 0], sem).wait()


def fill(index, count, slots, outer, inner):
    arrays = len(slots)
    block = slots[0].shape[-1]
    return pl.pallas_call(
        functools.partial(fill_body, arrays),
        out_shape=(pltpu.VMEM((outer, inner, block, block), BF16),) * arrays,
        in_specs=[SCALARS] * 2 + [pl.BlockSpec(memory_space=pltpu.HBM)] * arrays,
        out_specs=(WHOLE,) * arrays,
        scratch_shapes=[pltpu.SemaphoreType.DMA],
        compiler_params=params(),
        cost_estimate=cost(0, arrays * slots[0].size * 2),
        name="fill",
    )(index, count, *(in_hbm(array) for array in slots))


def stack(pieces):
    return jnp.concatenate([piece[...] for piece in pieces], axis=0)


def gate_up_body(*refs):
    *pieces, gate_w, up_w, own, send = refs
    d_blocks, f_blocks, block, _ = gate_w.shape
    x = stack(pieces)

    @pl.loop(0, f_blocks)
    def _(c):
        weights = jnp.concatenate(
            [
                gate_w[:, c].reshape(d_blocks * block, block),
                up_w[:, c].reshape(d_blocks * block, block),
            ],
            axis=1,
        )
        result = jnp.dot(x, weights, preferred_element_type=F32)
        own[c] = result
        send[c] = result.astype(BF16)


def gate_up(pieces, gate_w, up_w):
    d_blocks, f_blocks, block, _ = gate_w.shape
    tokens = sum(piece.shape[0] for piece in pieces)
    shape = (f_blocks, tokens, 2 * block)
    return pl.pallas_call(
        gate_up_body,
        out_shape=(jax.ShapeDtypeStruct(shape, F32), jax.ShapeDtypeStruct(shape, BF16)),
        in_specs=[WHOLE] * (len(pieces) + 2),
        out_specs=(WHOLE,) * 2,
        compiler_params=params(),
        cost_estimate=cost(4 * tokens * gate_w.size, 4 * gate_w.size),
        name="gate_up",
    )(*pieces, resident(gate_w), resident(up_w))


def d_hidden_body(pieces_count, *refs):
    y_pieces, x_pieces = refs[:pieces_count], refs[pieces_count : 2 * pieces_count]
    down_w, own, send, turned = refs[2 * pieces_count :]
    f_blocks, d_blocks, block, _ = down_w.shape
    y = stack(y_pieces)

    @pl.loop(0, f_blocks // 2)
    def _(pair):
        weights = jnp.concatenate(
            [
                down_w[pl.ds(2 * pair, 2), d].reshape(2 * block, block)
                for d in range(d_blocks)
            ],
            axis=1,
        )
        result = lax.dot_general(
            y, weights, (((1,), (1,)), ((), ())), preferred_element_type=F32
        )
        for half in range(2):
            part = result[:, half * block : (half + 1) * block]
            own[2 * pair + half] = part
            send[2 * pair + half] = part.astype(BF16)

    for d in range(d_blocks):
        columns = slice(d * block, (d + 1) * block)
        turned[d] = jnp.concatenate([piece[:, columns] for piece in x_pieces], axis=0).T


def d_hidden(y_pieces, x_pieces, down_w):
    f_blocks, d_blocks, block, _ = down_w.shape
    tokens = sum(piece.shape[0] for piece in y_pieces)
    shape = (f_blocks, tokens, block)
    return pl.pallas_call(
        functools.partial(d_hidden_body, len(y_pieces)),
        out_shape=(
            jax.ShapeDtypeStruct(shape, F32),
            jax.ShapeDtypeStruct(shape, BF16),
            jax.ShapeDtypeStruct((d_blocks, block, tokens), BF16),
        ),
        in_specs=[WHOLE] * (2 * len(y_pieces) + 1),
        out_specs=(WHOLE,) * 3,
        compiler_params=params(),
        cost_estimate=cost(2 * tokens * down_w.size, 2 * down_w.size),
        name="d_hidden",
    )(*y_pieces, *x_pieces, resident(down_w))


def d_tokens_body(group, *refs):
    coef, dh_own, *dh_recv, gate_w, up_w, own, send, d_pair, turned = refs
    d_blocks, f_blocks, block, _ = gate_w.shape
    piece = own.shape[0] // 2
    for c in range(f_blocks):
        dh = dh_own[c]
        for part in dh_recv:
            dh = dh + part[c].astype(F32)
        both = (jnp.concatenate([dh, dh], axis=1) * coef[c]).astype(BF16)
        d_pair[c] = both
        for side in range(2):
            turned[pl.ds((2 * c + side) * block, block), :] = both[
                :, side * block : (side + 1) * block
            ].T
    grads = turned[...]

    @pl.loop(0, d_blocks // group)
    def _(at):
        rows = pl.ds(at * group, group)
        weights = jnp.concatenate(
            [
                ref[rows, c].reshape(group * block, block)
                for c in range(f_blocks)
                for ref in (gate_w, up_w)
            ],
            axis=1,
        )
        result = jnp.dot(weights, grads, preferred_element_type=F32).T
        columns = pl.ds(pl.multiple_of(at * group * block, group * block), group * block)
        for at_piece in range(2):
            rows = slice(at_piece * piece, (at_piece + 1) * piece)
            start = 2 * at_piece * piece
            own[rows, columns] = result[start : start + piece]
            send[rows, columns] = result[start + piece : start + 2 * piece].astype(BF16)


def d_tokens_part(coef, dh_own, dh_recv, gate_w, up_w):
    d_blocks, f_blocks, block, _ = gate_w.shape
    tokens = dh_own.shape[1]
    width = d_blocks * block
    group = max(n for n in (1, 2, 4) if d_blocks % n == 0)
    return pl.pallas_call(
        functools.partial(d_tokens_body, group),
        out_shape=(
            jax.ShapeDtypeStruct((tokens // 2, width), F32),
            jax.ShapeDtypeStruct((tokens // 2, width), BF16),
            jax.ShapeDtypeStruct((f_blocks, tokens, 2 * block), BF16),
        ),
        in_specs=[WHOLE] * (4 + len(dh_recv)),
        out_specs=(WHOLE,) * 3,
        scratch_shapes=[pltpu.VMEM((f_blocks * 2 * block, tokens), BF16)],
        compiler_params=params(),
        cost_estimate=cost(4 * tokens * gate_w.size, 4 * gate_w.size),
        name="d_tokens",
    )(coef, dh_own, *dh_recv, resident(gate_w), resident(up_w))


def step_slots(slots):
    return max(n for n in range(1, 17) if slots % n == 0)


def gu_grad_body(first, index, count, d_pair, turned, *refs):
    gate_out, up_out = refs[-2:]
    f_blocks = d_pair.shape[0]
    block = turned.shape[1]
    step = pl.program_id(0) + first

    for j in range(gate_out.shape[0]):
        slot = step * gate_out.shape[0] + j
        d, f = split_index(index[0, 0, slot], f_blocks)
        result = jnp.dot(turned[d], d_pair[f], preferred_element_type=F32)
        result = jnp.where(slot < count[0, 0], result, 0.0).astype(BF16)
        gate_out[j] = result[:, :block]
        up_out[j] = result[:, block:]


def gu_grads(index, count, d_pair, turned, slots, part, parts, before):
    block, tokens = turned.shape[1:]
    chunk = step_slots(slots // parts)
    steps = slots // parts // chunk
    first = part * steps
    shape = jax.ShapeDtypeStruct((slots, block, block), BF16)
    out = pl.BlockSpec((chunk, block, block), lambda i, *_: (i + first, 0, 0))
    flops = 4 * slots * block * block * tokens
    return pl.pallas_call(
        functools.partial(gu_grad_body, first),
        out_shape=(shape,) * 2,
        grid_spec=pltpu.PrefetchScalarGridSpec(
            num_scalar_prefetch=2,
            grid=(steps,),
            in_specs=[WHOLE] * 2 + [pl.BlockSpec(memory_space=pl.ANY)] * len(before),
            out_specs=(out,) * 2,
        ),
        input_output_aliases={4 + at: at for at in range(len(before))},
        compiler_params=params(),
        cost_estimate=cost(flops // parts, 4 * slots * block * block // parts),
        name="gu_grads",
    )(index, count, d_pair, turned, *before)


def down_grad_body(pieces_count, index, count, *refs):
    pieces, gu = refs[:pieces_count], refs[pieces_count:-4]
    halves = gu[: len(gu) // 2], gu[len(gu) // 2 :]
    out, coef, turned, columns = refs[-4:]
    f_blocks = turned.shape[0]
    d_blocks, _, block = columns.shape
    step = pl.program_id(0)

    @pl.when(step == 0)
    def _():
        for f in range(f_blocks):
            both = jnp.concatenate(
                [
                    sum((part[f].astype(F32) for part in half[1:]), half[0][f])
                    for half in halves
                ],
                axis=0,
            )
            gate, up = both[:, :block], both[:, block:]
            sig = jax.nn.sigmoid(gate)
            silu = gate * sig
            turned[f] = (silu * up).astype(BF16).T
            coef[f, :, :block] = up * sig * (1.0 + gate * (1.0 - sig))
            coef[f, :, block:] = silu
        for d in range(d_blocks):
            at = slice(d * block, (d + 1) * block)
            columns[d] = jnp.concatenate([piece[:, at] for piece in pieces], axis=0)

    for j in range(out.shape[0]):
        slot = step * out.shape[0] + j
        f, d = split_index(index[0, 0, slot], d_blocks)
        result = jnp.dot(turned[f], columns[d], preferred_element_type=F32)
        out[j] = jnp.where(slot < count[0, 0], result, 0.0).astype(BF16)


def down_grads(index, count, pieces, halves, slots):
    f_blocks, half_tokens, pair = halves[0][0].shape
    tokens = 2 * half_tokens
    block = pair // 2
    d_blocks = pieces[0].shape[1] // block
    chunk = step_slots(slots)
    return pl.pallas_call(
        functools.partial(down_grad_body, len(pieces)),
        out_shape=(
            jax.ShapeDtypeStruct((slots, block, block), BF16),
            jax.ShapeDtypeStruct((f_blocks, tokens, pair), F32),
        ),
        grid_spec=pltpu.PrefetchScalarGridSpec(
            num_scalar_prefetch=2,
            grid=(slots // chunk,),
            in_specs=[WHOLE] * (len(pieces) + 2 * len(halves[0])),
            out_specs=(pl.BlockSpec((chunk, block, block), lambda i, *_: (i, 0, 0)), WHOLE),
            scratch_shapes=[
                pltpu.VMEM((f_blocks, block, tokens), BF16),
                pltpu.VMEM((d_blocks, tokens, block), BF16),
            ],
        ),
        compiler_params=params(),
        cost_estimate=cost(2 * slots * block * block * tokens, 2 * slots * block * block),
        name="down_grads",
    )(index, count, *pieces, *halves[0], *halves[1])


def on_device(
    tokens, cotangent, gate_vals, up_vals, gu_index, gu_count, down_vals, down_index, down_count
):
    block = gate_vals.shape[-1]
    slots = gate_vals.shape[2]
    wide = lax.axis_size("wide")
    narrow = lax.axis_size("narrow")
    chips = wide // 2
    rows = tokens.shape[0]
    d_blocks = tokens.shape[1] // block
    f_blocks = FF // (block * wide)

    def exchange(array):
        return [swap(array, "narrow", narrow, k) for k in range(1, narrow)]

    flips = [chips >> hop for hop in range(1, chips.bit_length())]
    x, y = tokens, cotangent
    x_recv = swap(x, "wide", wide, 2 * flips[0])
    gate_w, up_w = fill(gu_index, gu_count, (gate_vals, up_vals), d_blocks, f_blocks)
    y, _ = lax.optimization_barrier((y, x_recv))
    y_recv = swap(y, "wide", wide, 2 * flips[0])
    for hop, flip in enumerate(flips[1:-1]):
        x = jnp.concatenate([x, x_recv], axis=0)
        if hop == 0:
            x, gate_w, up_w, index = lax.optimization_barrier((x, gate_w, up_w, down_index))
            (down_w,) = fill(index, down_count, (down_vals,), f_blocks, d_blocks)
        x_recv = swap(x, "wide", wide, 2 * flip)
        y = jnp.concatenate([y, y_recv], axis=0)
        y, _ = lax.optimization_barrier((y, x_recv))
        y_recv = swap(y, "wide", wide, 2 * flip)
    x = jnp.concatenate([x, x_recv], axis=0)
    x, down_w = lax.optimization_barrier((x, down_w))

    x_near = [x, swap(x, "wide", wide, 1)]
    x_far = swap(x, "wide", wide, 2 * flips[-1])
    near_own, near_send = gate_up(x_near, gate_w, up_w)
    near_recv = exchange(near_send)
    y = jnp.concatenate([y, y_recv], axis=0)
    x_far, y, _ = lax.optimization_barrier((x_far, y, near_send))
    y_far = swap(y, "wide", wide, 2 * flips[-1])
    y_near = [y, swap(y, "wide", wide, 1)]
    x_far = [x_far, swap(x_far, "wide", wide, 1)]
    far_own, far_send = gate_up(x_far, gate_w, up_w)
    far_recv = exchange(far_send)
    y_far, _ = lax.optimization_barrier((y_far, far_send))
    y_far = [y_far, swap(y_far, "wide", wide, 1)]
    x_pieces = x_near + x_far
    y_pieces = y_near + y_far
    dh_own, dh_send, turned = d_hidden(y_pieces, x_pieces, down_w)
    dh_recv = exchange(dh_send)
    halves = (near_own, *near_recv), (far_own, *far_recv)
    down_grad, coef = down_grads(down_index, down_count, y_pieces, halves, slots)
    own, send, d_pair = d_tokens_part(coef, dh_own, dh_recv, gate_w, up_w)

    own = own + swap(send, "wide", wide, 1).astype(F32)
    kept = chips // 2 * rows
    far = own[kept:].astype(BF16)
    own = own[:kept]
    parts = 2 if slots % 2 == 0 else 1
    far, d_pair = lax.optimization_barrier((far, d_pair))
    grads = gu_grads(gu_index, gu_count, d_pair, turned, slots, 0, parts, ())
    own = own + swap(far, "wide", wide, 2).astype(F32)
    sends = [own[p * rows : (p + 1) * rows].astype(BF16) for p in range(1, chips // 2)]
    if parts == 2:
        sends, d_pair = lax.optimization_barrier((sends, d_pair))
        grads = gu_grads(gu_index, gu_count, d_pair, turned, slots, 1, parts, grads)
    gate_grad, up_grad = grads
    total = own[:rows]
    for p, part in enumerate(sends, 1):
        total = total + swap(part, "wide", wide, 2 * reverse_bits(p, chips)).astype(F32)
    return (
        total.astype(BF16),
        gate_grad[None, None],
        up_grad[None, None],
        down_grad[None, None],
    )


def solution(mesh):
    in_specs = (
        P("wide", "narrow"),
        P("wide", "narrow"),
        P("narrow", "wide", None, None, None),
        P("narrow", "wide", None, None, None),
        P("narrow", "wide", None),
        P("narrow", "wide"),
        P("wide", "narrow", None, None, None),
        P("wide", "narrow", None),
        P("wide", "narrow"),
    )
    out_specs = (
        P("wide", "narrow"),
        P("narrow", "wide", None, None, None),
        P("narrow", "wide", None, None, None),
        P("wide", "narrow", None, None, None),
    )
    return jax.shard_map(
        on_device, mesh=mesh, in_specs=in_specs, out_specs=out_specs, check_vma=False
    )
```

```python
import functools

import jax
import jax.numpy as jnp
from jax import lax
from jax.experimental import pallas as pl
from jax.experimental.pallas import tpu as pltpu
from jax.sharding import PartitionSpec as P

FF = 16384
F32 = jnp.float32
BF16 = jnp.bfloat16
VMEM_LIMIT = 8 * 1024 * 1024

WHOLE = pl.BlockSpec(memory_space=pltpu.VMEM)
SCALARS = pl.BlockSpec(memory_space=pltpu.SMEM)


def params(vmem=VMEM_LIMIT):
    return pltpu.CompilerParams(vmem_limit_bytes=vmem)


def cost(flops, bytes_accessed):
    return pl.CostEstimate(flops=int(flops), bytes_accessed=int(bytes_accessed), transcendentals=0)


def resident(array):
    return pltpu.with_memory_space_constraint(array, pltpu.VMEM)


def in_hbm(array):
    return pltpu.with_memory_space_constraint(array, pltpu.HBM)


def swap(array, axis, size, flip):
    return lax.ppermute(array, axis, [(i, i ^ flip) for i in range(size)])


def split_index(number, size):
    if size & (size - 1):
        return number // size, number % size
    return number >> (size.bit_length() - 1), number & (size - 1)


def reverse_bits(number, size):
    return sum(size >> (bit + 1) for bit in range(size.bit_length() - 1) if number >> bit & 1)


def fill_body(arrays, index, count, *refs):
    slots, dense, sem = refs[:arrays], refs[arrays : 2 * arrays], refs[2 * arrays]
    outer, inner = dense[0].shape[:2]
    live = count[0, 0]
    chunk = min(inner, 8)

    for source, target in zip(slots, dense):

        @pl.loop(0, outer)
        def _(high):
            target[high] = jnp.zeros(target.shape[1:], target.dtype)

        @pl.loop(0, live)
        def _(s):
            high, low = split_index(index[0, 0, s], inner)
            pltpu.make_async_copy(source.at[0, 0, s], target.at[high, low], sem).start()

    many, few = split_index(live, chunk)
    for source, target in zip(slots, dense):

        @pl.loop(0, many)
        def _(_):
            blocks = pl.ds(0, chunk)
            pltpu.make_async_copy(source.at[0, 0, blocks], target.at[0, blocks], sem).wait()

        @pl.loop(0, few)
        def _(_):
            pltpu.make_async_copy(source.at[0, 0, 0], target.at[0, 0], sem).wait()


def fill(index, count, slots, outer, inner):
    arrays = len(slots)
    block = slots[0].shape[-1]
    return pl.pallas_call(
        functools.partial(fill_body, arrays),
        out_shape=(pltpu.VMEM((outer, inner, block, block), BF16),) * arrays,
        in_specs=[SCALARS] * 2 + [pl.BlockSpec(memory_space=pltpu.HBM)] * arrays,
        out_specs=(WHOLE,) * arrays,
        scratch_shapes=[pltpu.SemaphoreType.DMA],
        compiler_params=params(),
        cost_estimate=cost(0, arrays * slots[0].size * 2),
        name="fill",
    )(index, count, *(in_hbm(array) for array in slots))


def stack(pieces):
    return jnp.concatenate([piece[...] for piece in pieces], axis=0)


def gate_up_body(*refs):
    *pieces, gate_w, up_w, own, send = refs
    d_blocks, f_blocks, block, _ = gate_w.shape
    x = stack(pieces)

    @pl.loop(0, f_blocks)
    def _(c):
        weights = jnp.concatenate(
            [
                gate_w[:, c].reshape(d_blocks * block, block),
                up_w[:, c].reshape(d_blocks * block, block),
            ],
            axis=1,
        )
        result = jnp.dot(x, weights, preferred_element_type=F32)
        own[c] = result
        send[c] = result.astype(BF16)


def gate_up(pieces, gate_w, up_w):
    d_blocks, f_blocks, block, _ = gate_w.shape
    tokens = sum(piece.shape[0] for piece in pieces)
    shape = (f_blocks, tokens, 2 * block)
    return pl.pallas_call(
        gate_up_body,
        out_shape=(jax.ShapeDtypeStruct(shape, F32), jax.ShapeDtypeStruct(shape, BF16)),
        in_specs=[WHOLE] * (len(pieces) + 2),
        out_specs=(WHOLE,) * 2,
        compiler_params=params(),
        cost_estimate=cost(4 * tokens * gate_w.size, 4 * gate_w.size),
        name="gate_up",
    )(*pieces, resident(gate_w), resident(up_w))


def d_hidden_body(pieces_count, *refs):
    y_pieces, x_pieces = refs[:pieces_count], refs[pieces_count : 2 * pieces_count]
    down_w, own, send, turned = refs[2 * pieces_count :]
    f_blocks, d_blocks, block, _ = down_w.shape
    y = stack(y_pieces)

    @pl.loop(0, f_blocks // 2)
    def _(pair):
        weights = jnp.concatenate(
            [
                down_w[pl.ds(2 * pair, 2), d].reshape(2 * block, block)
                for d in range(d_blocks)
            ],
            axis=1,
        )
        result = lax.dot_general(
            y, weights, (((1,), (1,)), ((), ())), preferred_element_type=F32
        )
        for half in range(2):
            part = result[:, half * block : (half + 1) * block]
            own[2 * pair + half] = part
            send[2 * pair + half] = part.astype(BF16)

    for d in range(d_blocks):
        columns = slice(d * block, (d + 1) * block)
        turned[d] = jnp.concatenate([piece[:, columns] for piece in x_pieces], axis=0).T


def d_hidden(y_pieces, x_pieces, down_w):
    f_blocks, d_blocks, block, _ = down_w.shape
    tokens = sum(piece.shape[0] for piece in y_pieces)
    shape = (f_blocks, tokens, block)
    return pl.pallas_call(
        functools.partial(d_hidden_body, len(y_pieces)),
        out_shape=(
            jax.ShapeDtypeStruct(shape, F32),
            jax.ShapeDtypeStruct(shape, BF16),
            jax.ShapeDtypeStruct((d_blocks, block, tokens), BF16),
        ),
        in_specs=[WHOLE] * (2 * len(y_pieces) + 1),
        out_specs=(WHOLE,) * 3,
        compiler_params=params(),
        cost_estimate=cost(2 * tokens * down_w.size, 2 * down_w.size),
        name="d_hidden",
    )(*y_pieces, *x_pieces, resident(down_w))


def d_tokens_body(group, *refs):
    near, far, dh_own, *dh_recv, gate_w, up_w, own, send, d_pair, turned = refs
    d_blocks, f_blocks, block, _ = gate_w.shape
    piece = own.shape[0] // 2
    for c in range(f_blocks):
        dh = dh_own[c]
        for part in dh_recv:
            dh = dh + part[c].astype(F32)
        coef = jnp.concatenate([near[c], far[c]], axis=0)
        both = (jnp.concatenate([dh, dh], axis=1) * coef).astype(BF16)
        d_pair[c] = both
        for side in range(2):
            turned[pl.ds((2 * c + side) * block, block), :] = both[
                :, side * block : (side + 1) * block
            ].T
    grads = turned[...]

    @pl.loop(0, d_blocks // group)
    def _(at):
        rows = pl.ds(at * group, group)
        weights = jnp.concatenate(
            [
                ref[rows, c].reshape(group * block, block)
                for c in range(f_blocks)
                for ref in (gate_w, up_w)
            ],
            axis=1,
        )
        result = jnp.dot(weights, grads, preferred_element_type=F32).T
        columns = pl.ds(pl.multiple_of(at * group * block, group * block), group * block)
        for at_piece in range(2):
            rows = slice(at_piece * piece, (at_piece + 1) * piece)
            start = 2 * at_piece * piece
            own[rows, columns] = result[start : start + piece]
            send[rows, columns] = result[start + piece : start + 2 * piece].astype(BF16)


def d_tokens_part(near, far, dh_own, dh_recv, gate_w, up_w):
    d_blocks, f_blocks, block, _ = gate_w.shape
    tokens = dh_own.shape[1]
    width = d_blocks * block
    group = max(n for n in (1, 2, 4) if d_blocks % n == 0)
    return pl.pallas_call(
        functools.partial(d_tokens_body, group),
        out_shape=(
            jax.ShapeDtypeStruct((tokens // 2, width), F32),
            jax.ShapeDtypeStruct((tokens // 2, width), BF16),
            jax.ShapeDtypeStruct((f_blocks, tokens, 2 * block), BF16),
        ),
        in_specs=[WHOLE] * (5 + len(dh_recv)),
        out_specs=(WHOLE,) * 3,
        scratch_shapes=[pltpu.VMEM((f_blocks * 2 * block, tokens), BF16)],
        compiler_params=params(),
        cost_estimate=cost(4 * tokens * gate_w.size, 4 * gate_w.size),
        name="d_tokens",
    )(near, far, dh_own, *dh_recv, resident(gate_w), resident(up_w))


def step_slots(slots):
    return max(n for n in range(1, 17) if slots % n == 0)


def gu_grad_body(first, index, count, d_pair, turned, *refs):
    gate_out, up_out = refs[-2:]
    f_blocks = d_pair.shape[0]
    block = turned.shape[1]
    step = pl.program_id(0) + first

    for j in range(gate_out.shape[0]):
        slot = step * gate_out.shape[0] + j
        d, f = split_index(index[0, 0, slot], f_blocks)
        result = jnp.dot(turned[d], d_pair[f], preferred_element_type=F32)
        result = jnp.where(slot < count[0, 0], result, 0.0).astype(BF16)
        gate_out[j] = result[:, :block]
        up_out[j] = result[:, block:]


def gu_grads(index, count, d_pair, turned, slots, part, parts, before):
    block, tokens = turned.shape[1:]
    chunk = step_slots(slots // parts)
    steps = slots // parts // chunk
    first = part * steps
    shape = jax.ShapeDtypeStruct((slots, block, block), BF16)
    out = pl.BlockSpec((chunk, block, block), lambda i, *_: (i + first, 0, 0))
    flops = 4 * slots * block * block * tokens
    return pl.pallas_call(
        functools.partial(gu_grad_body, first),
        out_shape=(shape,) * 2,
        grid_spec=pltpu.PrefetchScalarGridSpec(
            num_scalar_prefetch=2,
            grid=(steps,),
            in_specs=[WHOLE] * 2 + [pl.BlockSpec(memory_space=pl.ANY)] * len(before),
            out_specs=(out,) * 2,
        ),
        input_output_aliases={4 + at: at for at in range(len(before))},
        compiler_params=params(),
        cost_estimate=cost(flops // parts, 4 * slots * block * block // parts),
        name="gu_grads",
    )(index, count, d_pair, turned, *before)


def activate_body(*refs):
    own, *recv, hidden, coef = refs
    block = hidden.shape[2]
    for f in range(hidden.shape[0]):
        both = own[f]
        for part in recv:
            both = both + part[f].astype(F32)
        gate, up = both[:, :block], both[:, block:]
        sig = jax.nn.sigmoid(gate)
        silu = gate * sig
        hidden[f] = (silu * up).astype(BF16)
        coef[f, :, :block] = up * sig * (1.0 + gate * (1.0 - sig))
        coef[f, :, block:] = silu


def activate(own, recv):
    f_blocks, tokens, pair = own.shape
    return pl.pallas_call(
        activate_body,
        out_shape=(
            jax.ShapeDtypeStruct((f_blocks, tokens, pair // 2), BF16),
            jax.ShapeDtypeStruct(own.shape, F32),
        ),
        in_specs=[WHOLE] * (1 + len(recv)),
        out_specs=(WHOLE,) * 2,
        compiler_params=params(),
        cost_estimate=cost(20 * own.size, 8 * own.size),
        name="activate",
    )(own, *recv)


def down_grad_body(index, count, near, far, *refs):
    *pieces, out, turned, dense, zero, sem = refs
    f_blocks, d_blocks, block, _ = dense.shape
    live = count[0, 0]
    for f in range(f_blocks):
        turned[pl.ds(f * block, block), :] = jnp.concatenate([near[f], far[f]], axis=0).T
    zero[...] = jnp.zeros(zero.shape, zero.dtype)

    @pl.loop(live, out.shape[0])
    def _(s):
        pltpu.make_async_copy(zero, out.at[s], sem).start()

    @pl.loop(0, d_blocks // 2)
    def _(pair):
        columns = pl.ds(pl.multiple_of(pair * 2 * block, 2 * block), 2 * block)
        y = jnp.concatenate([piece[:, columns] for piece in pieces], axis=0)
        result = jnp.dot(turned[...], y, preferred_element_type=F32).astype(BF16)
        for side in range(2):
            part = result[:, side * block : (side + 1) * block]
            dense[:, 2 * pair + side] = part.reshape(f_blocks, block, block)

    @pl.loop(0, live)
    def _(s):
        f, d = split_index(index[0, 0, s], d_blocks)
        pltpu.make_async_copy(dense.at[f, d], out.at[s], sem).start()

    pltpu.make_async_copy(out, out, sem).wait()


def down_grads(index, count, pieces, near, far, slots):
    f_blocks, _, block = near.shape
    tokens = sum(piece.shape[0] for piece in pieces)
    d_blocks = pieces[0].shape[1] // block
    return pl.pallas_call(
        down_grad_body,
        out_shape=jax.ShapeDtypeStruct((slots, block, block), BF16),
        in_specs=[SCALARS] * 2 + [WHOLE] * (2 + len(pieces)),
        out_specs=pl.BlockSpec(memory_space=pltpu.HBM),
        scratch_shapes=[
            pltpu.VMEM((f_blocks * block, tokens), BF16),
            pltpu.VMEM((f_blocks, d_blocks, block, block), BF16),
            pltpu.VMEM((block, block), BF16),
            pltpu.SemaphoreType.DMA,
        ],
        compiler_params=params(VMEM_LIMIT + 2 * f_blocks * d_blocks * block * block),
        cost_estimate=cost(2 * slots * block * block * tokens, 2 * slots * block * block),
        name="down_grads",
    )(index, count, near, far, *pieces)


def on_device(
    tokens, cotangent, gate_vals, up_vals, gu_index, gu_count, down_vals, down_index, down_count
):
    block = gate_vals.shape[-1]
    slots = gate_vals.shape[2]
    wide = lax.axis_size("wide")
    narrow = lax.axis_size("narrow")
    chips = wide // 2
    rows = tokens.shape[0]
    d_blocks = tokens.shape[1] // block
    f_blocks = FF // (block * wide)

    def exchange(array):
        return [swap(array, "narrow", narrow, k) for k in range(1, narrow)]

    flips = [chips >> hop for hop in range(1, chips.bit_length())]
    x, y = tokens, cotangent
    x_recv = swap(x, "wide", wide, 2 * flips[0])
    gate_w, up_w = fill(gu_index, gu_count, (gate_vals, up_vals), d_blocks, f_blocks)
    y, _ = lax.optimization_barrier((y, x_recv))
    y_recv = swap(y, "wide", wide, 2 * flips[0])
    for hop, flip in enumerate(flips[1:-1]):
        x = jnp.concatenate([x, x_recv], axis=0)
        if hop == 0:
            x, gate_w, up_w, index = lax.optimization_barrier((x, gate_w, up_w, down_index))
            (down_w,) = fill(index, down_count, (down_vals,), f_blocks, d_blocks)
        x_recv = swap(x, "wide", wide, 2 * flip)
        y = jnp.concatenate([y, y_recv], axis=0)
        y, _ = lax.optimization_barrier((y, x_recv))
        y_recv = swap(y, "wide", wide, 2 * flip)
    x = jnp.concatenate([x, x_recv], axis=0)
    x, down_w = lax.optimization_barrier((x, down_w))

    x_near = [x, swap(x, "wide", wide, 1)]
    x_far = swap(x, "wide", wide, 2 * flips[-1])
    near_own, near_send = gate_up(x_near, gate_w, up_w)
    near_recv = exchange(near_send)
    y = jnp.concatenate([y, y_recv], axis=0)
    x_far, y, _ = lax.optimization_barrier((x_far, y, near_send))
    y_far = swap(y, "wide", wide, 2 * flips[-1])
    y_near = [y, swap(y, "wide", wide, 1)]
    x_far = [x_far, swap(x_far, "wide", wide, 1)]
    far_own, far_send = gate_up(x_far, gate_w, up_w)
    far_recv = exchange(far_send)
    near_hidden, near_coef = activate(near_own, near_recv)
    y_far, _ = lax.optimization_barrier((y_far, far_send))
    y_far = [y_far, swap(y_far, "wide", wide, 1)]
    x_pieces = x_near + x_far
    y_pieces = y_near + y_far
    down_w, near_hidden = lax.optimization_barrier((down_w, near_hidden))
    dh_own, dh_send, turned = d_hidden(y_pieces, x_pieces, down_w)
    dh_recv = exchange(dh_send)
    far_hidden, far_coef = activate(far_own, far_recv)
    down_grad = down_grads(down_index, down_count, y_pieces, near_hidden, far_hidden, slots)
    down_grad, far_coef = lax.optimization_barrier((down_grad, far_coef))
    own, send, d_pair = d_tokens_part(
        near_coef, far_coef, dh_own, dh_recv, gate_w, up_w
    )

    own = own + swap(send, "wide", wide, 1).astype(F32)
    kept = chips // 2 * rows
    far = own[kept:].astype(BF16)
    own = own[:kept]
    parts = 2 if slots % 2 == 0 else 1
    far, d_pair = lax.optimization_barrier((far, d_pair))
    grads = gu_grads(gu_index, gu_count, d_pair, turned, slots, 0, parts, ())
    own = own + swap(far, "wide", wide, 2).astype(F32)
    sends = [own[p * rows : (p + 1) * rows].astype(BF16) for p in range(1, chips // 2)]
    if parts == 2:
        sends, d_pair = lax.optimization_barrier((sends, d_pair))
        grads = gu_grads(gu_index, gu_count, d_pair, turned, slots, 1, parts, grads)
    gate_grad, up_grad = grads
    total = own[:rows]
    for p, part in enumerate(sends, 1):
        total = total + swap(part, "wide", wide, 2 * reverse_bits(p, chips)).astype(F32)
    return (
        total.astype(BF16),
        gate_grad[None, None],
        up_grad[None, None],
        down_grad[None, None],
    )


def solution(mesh):
    in_specs = (
        P("wide", "narrow"),
        P("wide", "narrow"),
        P("narrow", "wide", None, None, None),
        P("narrow", "wide", None, None, None),
        P("narrow", "wide", None),
        P("narrow", "wide"),
        P("wide", "narrow", None, None, None),
        P("wide", "narrow", None),
        P("wide", "narrow"),
    )
    out_specs = (
        P("wide", "narrow"),
        P("narrow", "wide", None, None, None),
        P("narrow", "wide", None, None, None),
        P("wide", "narrow", None, None, None),
    )
    return jax.shard_map(
        on_device, mesh=mesh, in_specs=in_specs, out_specs=out_specs, check_vma=False
    )
```

```python
import functools
import math

import jax
import jax.numpy as jnp
from jax import lax
from jax.experimental import pallas as pl
from jax.experimental.pallas import tpu as pltpu
from jax.sharding import PartitionSpec as P

FF = 16384
F32 = jnp.float32
BF16 = jnp.bfloat16
VMEM_LIMIT = 8 * 1024 * 1024

WHOLE = pl.BlockSpec(memory_space=pltpu.VMEM)
SCALARS = pl.BlockSpec(memory_space=pltpu.SMEM)
IN_HBM = pl.BlockSpec(memory_space=pltpu.HBM)


def params(vmem=VMEM_LIMIT):
    return pltpu.CompilerParams(vmem_limit_bytes=vmem)


def cost(flops, bytes_accessed):
    return pl.CostEstimate(flops=int(flops), bytes_accessed=int(bytes_accessed), transcendentals=0)


def resident(array):
    return pltpu.with_memory_space_constraint(array, pltpu.VMEM)


def in_hbm(array):
    return pltpu.with_memory_space_constraint(array, pltpu.HBM)


def swap(array, axis, size, flip):
    return lax.ppermute(array, axis, [(i, i ^ flip) for i in range(size)])


def split_index(number, size):
    if size & (size - 1):
        return number // size, number % size
    return number >> (size.bit_length() - 1), number & (size - 1)


class Slots:
    def __init__(self, index_from, count, index, sem):
        self.copy = pltpu.make_async_copy(index_from, index, sem)
        self.index, self.live = index, count[0, 0]

    @staticmethod
    def scratch(index):
        return [pltpu.SMEM(index.shape, index.dtype), pltpu.SemaphoreType.DMA]

    def place(self, slot, size):
        return split_index(self.index[0, 0, slot], size)


def fill_body(index, count, source, target, index_here, slots_sem, sem):
    slots = Slots(index, count, index_here, slots_sem)
    slots.copy.start()
    outer, inner = target.shape[:2]
    chunk = min(inner, 8)

    @pl.loop(0, outer)
    def _(high):
        target[high] = jnp.zeros(target.shape[1:], target.dtype)

    slots.copy.wait()

    @pl.loop(0, slots.live)
    def _(s):
        high, low = slots.place(s, inner)
        pltpu.make_async_copy(source.at[0, 0, s], target.at[high, low], sem).start()

    many, few = split_index(slots.live, chunk)

    @pl.loop(0, many)
    def _(_):
        blocks = pl.ds(0, chunk)
        pltpu.make_async_copy(source.at[0, 0, blocks], target.at[0, blocks], sem).wait()

    @pl.loop(0, few)
    def _(_):
        pltpu.make_async_copy(source.at[0, 0, 0], target.at[0, 0], sem).wait()


def fill(index, count, slots, outer, inner):
    block = slots.shape[-1]
    return pl.pallas_call(
        fill_body,
        out_shape=pltpu.VMEM((outer, inner, block, block), BF16),
        in_specs=[IN_HBM, SCALARS, IN_HBM],
        out_specs=WHOLE,
        scratch_shapes=[*Slots.scratch(index), pltpu.SemaphoreType.DMA],
        compiler_params=params(),
        cost_estimate=cost(0, slots.size * 2),
        name="fill",
    )(in_hbm(index), count, in_hbm(slots))


def stack(pieces):
    return jnp.concatenate([piece[...] for piece in pieces], axis=0)


def gate_up_body(first, *refs):
    *pieces, gate_w, up_w, own, send = refs
    d_blocks, _, block, _ = gate_w.shape
    x = stack(pieces)

    @pl.loop(0, own.shape[0])
    def _(c):
        weights = jnp.concatenate(
            [
                gate_w[:, first + c].reshape(d_blocks * block, block),
                up_w[:, first + c].reshape(d_blocks * block, block),
            ],
            axis=1,
        )
        result = jnp.dot(x, weights, preferred_element_type=F32)
        own[c] = result
        send[c] = result.astype(BF16)


def gate_up(pieces, gate_w, up_w, half):
    d_blocks, f_blocks, block, _ = gate_w.shape
    tokens = sum(piece.shape[0] for piece in pieces)
    shape = (f_blocks // 2, tokens, 2 * block)
    return pl.pallas_call(
        functools.partial(gate_up_body, half * f_blocks // 2),
        out_shape=(jax.ShapeDtypeStruct(shape, F32), jax.ShapeDtypeStruct(shape, BF16)),
        in_specs=[WHOLE] * (len(pieces) + 2),
        out_specs=(WHOLE,) * 2,
        compiler_params=params(),
        cost_estimate=cost(2 * tokens * gate_w.size, 2 * gate_w.size),
        name="gate_up",
    )(*pieces, resident(gate_w), resident(up_w))


def d_hidden_body(pieces_count, *refs):
    y_pieces, x_pieces = refs[:pieces_count], refs[pieces_count : 2 * pieces_count]
    down_w, own, send, turned = refs[2 * pieces_count :]
    f_blocks, d_blocks, block, _ = down_w.shape
    y = stack(y_pieces)

    @pl.loop(0, f_blocks // 2)
    def _(pair):
        weights = jnp.concatenate(
            [
                down_w[pl.ds(2 * pair, 2), d].reshape(2 * block, block)
                for d in range(d_blocks)
            ],
            axis=1,
        )
        result = lax.dot_general(
            y, weights, (((1,), (1,)), ((), ())), preferred_element_type=F32
        )
        for half in range(2):
            part = result[:, half * block : (half + 1) * block]
            own[2 * pair + half] = part
            send[2 * pair + half] = part.astype(BF16)

    for d in range(d_blocks):
        columns = slice(d * block, (d + 1) * block)
        turned[d] = jnp.concatenate([piece[:, columns] for piece in x_pieces], axis=0).T


def d_hidden(y_pieces, x_pieces, down_w):
    f_blocks, d_blocks, block, _ = down_w.shape
    tokens = sum(piece.shape[0] for piece in y_pieces)
    shape = (f_blocks, tokens, block)
    return pl.pallas_call(
        functools.partial(d_hidden_body, len(y_pieces)),
        out_shape=(
            jax.ShapeDtypeStruct(shape, F32),
            jax.ShapeDtypeStruct(shape, BF16),
            jax.ShapeDtypeStruct((d_blocks, block, tokens), BF16),
        ),
        in_specs=[WHOLE] * (2 * len(y_pieces) + 1),
        out_specs=(WHOLE,) * 3,
        compiler_params=params(),
        cost_estimate=cost(2 * tokens * down_w.size, 2 * down_w.size),
        name="d_hidden",
    )(*y_pieces, *x_pieces, resident(down_w))


def d_tokens_body(group, *refs):
    *coef, dh_own = refs[:3]
    *dh_recv, gate_w, up_w, own, send, d_pair, turned = refs[3:]
    d_blocks, f_blocks, block, _ = gate_w.shape
    half = own.shape[0]
    for c in range(f_blocks):
        dh = dh_own[c]
        for part in dh_recv:
            dh = dh + part[c].astype(F32)
        side, at = divmod(c, f_blocks // 2)
        both = (jnp.concatenate([dh, dh], axis=1) * coef[side][at]).astype(BF16)
        d_pair[c] = both
        for side in range(2):
            turned[pl.ds((2 * c + side) * block, block), :] = both[
                :, side * block : (side + 1) * block
            ].T
    grads = turned[...]

    for at in range(d_blocks // group):
        weights = jnp.concatenate(
            [
                ref[at * group : (at + 1) * group, c].reshape(group * block, block)
                for c in range(f_blocks)
                for ref in (gate_w, up_w)
            ],
            axis=1,
        )
        result = jnp.dot(weights, grads, preferred_element_type=F32).T
        columns = slice(at * group * block, (at + 1) * group * block)
        own[:, columns] = result[:half]
        send[:, columns] = result[half:].astype(BF16)


def d_tokens_part(coef, dh_own, dh_recv, gate_w, up_w):
    d_blocks, f_blocks, block, _ = gate_w.shape
    tokens = dh_own.shape[1]
    width = d_blocks * block
    group = max(n for n in (1, 2, 4) if d_blocks % n == 0)
    return pl.pallas_call(
        functools.partial(d_tokens_body, group),
        out_shape=(
            jax.ShapeDtypeStruct((tokens // 2, width), F32),
            jax.ShapeDtypeStruct((tokens // 2, width), BF16),
            jax.ShapeDtypeStruct((f_blocks, tokens, 2 * block), BF16),
        ),
        in_specs=[WHOLE] * (5 + len(dh_recv)),
        out_specs=(WHOLE,) * 3,
        scratch_shapes=[pltpu.VMEM((f_blocks * 2 * block, tokens), BF16)],
        compiler_params=params(),
        cost_estimate=cost(4 * tokens * gate_w.size, 4 * gate_w.size),
        name="d_tokens",
    )(*coef, dh_own, *dh_recv, resident(gate_w), resident(up_w))


def step_slots(slots):
    return max(n for n in range(1, 17) if slots % n == 0)


def gu_grad_body(first, given, index, count, d_pair, turned, *refs):
    gate_out, up_out, *scalars = refs[given:]
    slots = Slots(index, count, *scalars)
    f_blocks = d_pair.shape[0]
    block = turned.shape[1]
    step = pl.program_id(0)

    @pl.when(step == 0)
    def _():
        slots.copy.start()
        slots.copy.wait()

    for j in range(gate_out.shape[0]):
        slot = (step + first) * gate_out.shape[0] + j
        d, f = slots.place(slot, f_blocks)
        result = jnp.dot(turned[d], d_pair[f], preferred_element_type=F32)
        result = jnp.where(slot < slots.live, result, 0.0).astype(BF16)
        gate_out[j] = result[:, :block]
        up_out[j] = result[:, block:]


def gu_grads(index, count, d_pair, turned, total, begin, end, before):
    block, tokens = turned.shape[1:]
    chunk = step_slots(math.gcd(begin, end))
    first = begin // chunk
    shape = jax.ShapeDtypeStruct((total, block, block), BF16)
    out = pl.BlockSpec((chunk, block, block), lambda i: (i + first, 0, 0))
    size = (end - begin) * block * block
    return pl.pallas_call(
        functools.partial(gu_grad_body, first, len(before)),
        out_shape=(shape,) * 2,
        grid=((end - begin) // chunk,),
        in_specs=[IN_HBM, SCALARS] + [WHOLE] * 2 + [pl.BlockSpec(memory_space=pl.ANY)] * len(before),
        out_specs=(out,) * 2,
        scratch_shapes=Slots.scratch(index),
        input_output_aliases={4 + at: at for at in range(len(before))},
        compiler_params=params(),
        cost_estimate=cost(4 * size * tokens, 4 * size),
        name="gu_grads",
    )(in_hbm(index), count, d_pair, turned, *before)


def activate_body(*refs):
    own, *recv, hidden, coef = refs
    block = hidden.shape[2]
    for f in range(hidden.shape[0]):
        both = own[f]
        for part in recv:
            both = both + part[f].astype(F32)
        gate, up = both[:, :block], both[:, block:]
        sig = jax.nn.sigmoid(gate)
        silu = gate * sig
        hidden[f] = (silu * up).astype(BF16)
        coef[f, :, :block] = up * sig * (1.0 + gate * (1.0 - sig))
        coef[f, :, block:] = silu


def activate(own, recv):
    f_blocks, tokens, pair = own.shape
    return pl.pallas_call(
        activate_body,
        out_shape=(
            jax.ShapeDtypeStruct((f_blocks, tokens, pair // 2), BF16),
            jax.ShapeDtypeStruct(own.shape, F32),
        ),
        in_specs=[WHOLE] * (1 + len(recv)),
        out_specs=(WHOLE,) * 2,
        compiler_params=params(),
        cost_estimate=cost(20 * own.size, 8 * own.size),
        name="activate",
    )(own, *recv)


def down_grad_body(index, count, near, far, *refs):
    *pieces, out, index_here, slots_sem, turned, dense, zero, sem = refs
    slots = Slots(index, count, index_here, slots_sem)
    slots.copy.start()
    f_blocks, d_blocks, block, _ = dense.shape
    total = out.shape[0]
    halves = 2 if d_blocks % 4 == 0 else 1
    width = d_blocks // halves
    for f in range(f_blocks):
        half = (near, far)[f * 2 // f_blocks]
        turned[pl.ds(f * block, block), :] = half[f % (f_blocks // 2)].T
    zero[...] = jnp.zeros(zero.shape, zero.dtype)
    slots.copy.wait()

    @pl.loop(slots.live, total)
    def _(s):
        pltpu.make_async_copy(zero, out.at[s], sem).start()

    for part in range(halves):

        @pl.loop(0, width // 2)
        def _(pair):
            d = part * width + 2 * pair
            columns = pl.ds(pl.multiple_of(d * block, 2 * block), 2 * block)
            y = jnp.concatenate([piece[:, columns] for piece in pieces], axis=0)
            for f in range(0, f_blocks, 2):
                rows = turned[pl.ds(f * block, 2 * block), :]
                result = jnp.dot(rows, y, preferred_element_type=F32).astype(BF16)
                for side in range(2):
                    at = result[:, side * block : (side + 1) * block]
                    dense[pl.ds(f, 2), d + side] = at.reshape(2, block, block)

        @pl.loop(0, slots.live)
        def _(s):
            f, d = slots.place(s, d_blocks)

            @pl.when((d >= part * width) & (d < (part + 1) * width))
            def _():
                pltpu.make_async_copy(dense.at[f, d], out.at[s], sem).start()

    pltpu.make_async_copy(out, out, sem).wait()


def down_grads(index, count, pieces, near, far, slots):
    f_blocks, tokens, block = near.shape
    f_blocks = 2 * f_blocks
    d_blocks = pieces[0].shape[1] // block
    return pl.pallas_call(
        down_grad_body,
        out_shape=jax.ShapeDtypeStruct((slots, block, block), BF16),
        in_specs=[IN_HBM, SCALARS] + [WHOLE] * (2 + len(pieces)),
        out_specs=IN_HBM,
        scratch_shapes=[
            *Slots.scratch(index),
            pltpu.VMEM((f_blocks * block, tokens), BF16),
            pltpu.VMEM((f_blocks, d_blocks, block, block), BF16),
            pltpu.VMEM((block, block), BF16),
            pltpu.SemaphoreType.DMA,
        ],
        compiler_params=params(VMEM_LIMIT + 2 * f_blocks * d_blocks * block * block),
        cost_estimate=cost(2 * slots * block * block * tokens, 2 * slots * block * block),
        name="down_grads",
    )(in_hbm(index), count, near, far, *pieces)


def on_device(
    tokens, cotangent, gate_vals, up_vals, gu_index, gu_count, down_vals, down_index, down_count
):
    block = gate_vals.shape[-1]
    slots = gate_vals.shape[2]
    wide = lax.axis_size("wide")
    narrow = lax.axis_size("narrow")
    chips = wide // 2
    rows = tokens.shape[0]
    d_blocks = tokens.shape[1] // block
    f_blocks = FF // (block * wide)

    def exchange(array):
        return [swap(array, "narrow", narrow, k) for k in range(1, narrow)]

    flips = [chips >> hop for hop in range(1, chips.bit_length())]
    vals = (gate_vals, up_vals)
    x, y, index = tokens, cotangent, gu_index
    weights = []
    for hop, flip in enumerate(flips):
        if hop > 0:
            x = jnp.concatenate([x, x_recv], axis=0)
            y = jnp.concatenate([y, y_recv], axis=0)
            x, weights, index = lax.optimization_barrier((x, weights, index))
        x_recv = swap(x, "wide", wide, 2 * flip)
        if hop < 2:
            weights.append(fill(index, gu_count, vals[hop], d_blocks, f_blocks))
        y, _ = lax.optimization_barrier((y, x_recv))
        y_recv = swap(y, "wide", wide, 2 * flip)
    x_pieces = [x, x_recv, swap(x, "wide", wide, 1), swap(x_recv, "wide", wide, 1)]

    near_own, near_send = gate_up(x_pieces, *weights, 0)
    near_recv = exchange(near_send)
    late, _ = lax.optimization_barrier((x, near_send))
    far_own, far_send = gate_up([late, *x_pieces[1:]], *weights, 1)
    far_recv = exchange(far_send)
    index, _ = lax.optimization_barrier((down_index, far_send))
    down_w = fill(index, down_count, down_vals, f_blocks, d_blocks)
    y, y_recv, down_w = lax.optimization_barrier((y, y_recv, down_w))
    y_pieces = [y, y_recv, swap(y, "wide", wide, 1), swap(y_recv, "wide", wide, 1)]
    near_hidden, near_coef = activate(near_own, near_recv)
    down_w, near_hidden = lax.optimization_barrier((down_w, near_hidden))
    dh_own, dh_send, turned = d_hidden(y_pieces, x_pieces, down_w)
    dh_recv = exchange(dh_send)
    far_hidden, far_coef = activate(far_own, far_recv)
    down_grad = down_grads(down_index, down_count, y_pieces, near_hidden, far_hidden, slots)
    down_grad, far_coef = lax.optimization_barrier((down_grad, far_coef))
    own, send, d_pair = d_tokens_part((near_coef, far_coef), dh_own, dh_recv, *weights)

    own = own + swap(send, "wide", wide, 1).astype(F32)
    cuts = [0, slots // 2, slots * 3 // 4, slots]
    if slots % 4:
        cuts = [0, slots]
    grads = ()
    for hop, flip in enumerate(reversed(flips)):
        kept = own.shape[0] // 2
        far = own[kept:].astype(BF16)
        own = own[:kept]
        if hop + 1 < len(cuts):
            far, d_pair, grads = lax.optimization_barrier((far, d_pair, grads))
            grads = gu_grads(
                gu_index, gu_count, d_pair, turned, slots, cuts[hop], cuts[hop + 1], grads
            )
        own = own + swap(far, "wide", wide, 2 * flip).astype(F32)
    gate_grad, up_grad = grads
    return (
        own.astype(BF16),
        gate_grad[None, None],
        up_grad[None, None],
        down_grad[None, None],
    )


def solution(mesh):
    in_specs = (
        P("wide", "narrow"),
        P("wide", "narrow"),
        P("narrow", "wide", None, None, None),
        P("narrow", "wide", None, None, None),
        P("narrow", "wide", None),
        P("narrow", "wide"),
        P("wide", "narrow", None, None, None),
        P("wide", "narrow", None),
        P("wide", "narrow"),
    )
    out_specs = (
        P("wide", "narrow"),
        P("narrow", "wide", None, None, None),
        P("narrow", "wide", None, None, None),
        P("wide", "narrow", None, None, None),
    )
    return jax.shard_map(
        on_device, mesh=mesh, in_specs=in_specs, out_specs=out_specs, check_vma=False
    )
```

```python
import functools
import math

import jax
import jax.numpy as jnp
from jax import lax
from jax.experimental import pallas as pl
from jax.experimental.pallas import tpu as pltpu
from jax.sharding import PartitionSpec as P

FF = 16384
F32 = jnp.float32
BF16 = jnp.bfloat16
VMEM_LIMIT = 8 * 1024 * 1024

WHOLE = pl.BlockSpec(memory_space=pltpu.VMEM)
SCALARS = pl.BlockSpec(memory_space=pltpu.SMEM)
IN_HBM = pl.BlockSpec(memory_space=pltpu.HBM)


def params(vmem=VMEM_LIMIT):
    return pltpu.CompilerParams(vmem_limit_bytes=vmem)


def cost(flops, bytes_accessed):
    return pl.CostEstimate(flops=int(flops), bytes_accessed=int(bytes_accessed), transcendentals=0)


def resident(array):
    return pltpu.with_memory_space_constraint(array, pltpu.VMEM)


def in_hbm(array):
    return pltpu.with_memory_space_constraint(array, pltpu.HBM)


def swap(array, axis, size, flip):
    return lax.ppermute(array, axis, [(i, i ^ flip) for i in range(size)])


def split_index(number, size):
    if size & (size - 1):
        return number // size, number % size
    return number >> (size.bit_length() - 1), number & (size - 1)


class Slots:
    def __init__(self, index_from, count, index, sem):
        self.copy = pltpu.make_async_copy(index_from, index, sem)
        self.index, self.live = index, count[0, 0]

    @staticmethod
    def scratch(index):
        return [pltpu.SMEM(index.shape, index.dtype), pltpu.SemaphoreType.DMA]

    def place(self, slot, size):
        return split_index(self.index[0, 0, slot], size)


def fill_body(index, count, source, target, index_here, slots_sem, sem):
    slots = Slots(index, count, index_here, slots_sem)
    slots.copy.start()
    outer, inner = target.shape[:2]
    chunk = min(inner, 8)

    @pl.loop(0, outer)
    def _(high):
        target[high] = jnp.zeros(target.shape[1:], target.dtype)

    slots.copy.wait()

    @pl.loop(0, slots.live)
    def _(s):
        high, low = slots.place(s, inner)
        pltpu.make_async_copy(source.at[0, 0, s], target.at[high, low], sem).start()

    many, few = split_index(slots.live, chunk)

    @pl.loop(0, many)
    def _(_):
        blocks = pl.ds(0, chunk)
        pltpu.make_async_copy(source.at[0, 0, blocks], target.at[0, blocks], sem).wait()

    @pl.loop(0, few)
    def _(_):
        pltpu.make_async_copy(source.at[0, 0, 0], target.at[0, 0], sem).wait()


def fill(index, count, slots, outer, inner):
    block = slots.shape[-1]
    return pl.pallas_call(
        fill_body,
        out_shape=pltpu.VMEM((outer, inner, block, block), BF16),
        in_specs=[IN_HBM, SCALARS, IN_HBM],
        out_specs=WHOLE,
        scratch_shapes=[*Slots.scratch(index), pltpu.SemaphoreType.DMA],
        compiler_params=params(),
        cost_estimate=cost(0, slots.size * 2),
        name="fill",
    )(in_hbm(index), count, in_hbm(slots))


def stack(pieces):
    return jnp.concatenate([piece[...] for piece in pieces], axis=0)


def gate_up_body(first, *refs):
    *pieces, gate_w, up_w, own, send = refs
    d_blocks, _, block, _ = gate_w.shape
    x = stack(pieces)

    @pl.loop(0, own.shape[0])
    def _(c):
        weights = jnp.concatenate(
            [
                gate_w[:, first + c].reshape(d_blocks * block, block),
                up_w[:, first + c].reshape(d_blocks * block, block),
            ],
            axis=1,
        )
        result = jnp.dot(x, weights, preferred_element_type=F32)
        own[c] = result
        send[c] = result.astype(BF16)


def gate_up(pieces, gate_w, up_w, half):
    d_blocks, f_blocks, block, _ = gate_w.shape
    tokens = sum(piece.shape[0] for piece in pieces)
    shape = (f_blocks // 2, tokens, 2 * block)
    return pl.pallas_call(
        functools.partial(gate_up_body, half * f_blocks // 2),
        out_shape=(jax.ShapeDtypeStruct(shape, F32), jax.ShapeDtypeStruct(shape, BF16)),
        in_specs=[WHOLE] * (len(pieces) + 2),
        out_specs=(WHOLE,) * 2,
        compiler_params=params(),
        cost_estimate=cost(2 * tokens * gate_w.size, 2 * gate_w.size),
        name="gate_up",
    )(*pieces, resident(gate_w), resident(up_w))


def d_hidden_body(pieces_count, *refs):
    y_pieces, x_pieces = refs[:pieces_count], refs[pieces_count : 2 * pieces_count]
    down_w, own, send, turned = refs[2 * pieces_count :]
    f_blocks, d_blocks, block, _ = down_w.shape
    y = stack(y_pieces)

    @pl.loop(0, f_blocks // 2)
    def _(pair):
        weights = jnp.concatenate(
            [
                down_w[pl.ds(2 * pair, 2), d].reshape(2 * block, block)
                for d in range(d_blocks)
            ],
            axis=1,
        )
        result = lax.dot_general(
            y, weights, (((1,), (1,)), ((), ())), preferred_element_type=F32
        )
        for half in range(2):
            part = result[:, half * block : (half + 1) * block]
            own[2 * pair + half] = part
            send[2 * pair + half] = part.astype(BF16)

    for d in range(d_blocks):
        columns = slice(d * block, (d + 1) * block)
        turned[d] = jnp.concatenate([piece[:, columns] for piece in x_pieces], axis=0).T


def d_hidden(y_pieces, x_pieces, down_w):
    f_blocks, d_blocks, block, _ = down_w.shape
    tokens = sum(piece.shape[0] for piece in y_pieces)
    shape = (f_blocks, tokens, block)
    return pl.pallas_call(
        functools.partial(d_hidden_body, len(y_pieces)),
        out_shape=(
            jax.ShapeDtypeStruct(shape, F32),
            jax.ShapeDtypeStruct(shape, BF16),
            jax.ShapeDtypeStruct((d_blocks, block, tokens), BF16),
        ),
        in_specs=[WHOLE] * (2 * len(y_pieces) + 1),
        out_specs=(WHOLE,) * 3,
        compiler_params=params(),
        cost_estimate=cost(2 * tokens * down_w.size, 2 * down_w.size),
        name="d_hidden",
    )(*y_pieces, *x_pieces, resident(down_w))


def d_tokens_body(group, *refs):
    *coef, dh_own = refs[:3]
    *dh_recv, gate_w, up_w, own, send, d_pair, turned = refs[3:]
    d_blocks, f_blocks, block, _ = gate_w.shape
    half = own.shape[0]
    for c in range(f_blocks):
        dh = dh_own[c]
        for part in dh_recv:
            dh = dh + part[c].astype(F32)
        side, at = divmod(c, f_blocks // 2)
        both = (jnp.concatenate([dh, dh], axis=1) * coef[side][at]).astype(BF16)
        d_pair[c] = both
        for side in range(2):
            turned[pl.ds((2 * c + side) * block, block), :] = both[
                :, side * block : (side + 1) * block
            ].T
    grads = turned[...]

    for at in range(d_blocks // group):
        weights = jnp.concatenate(
            [
                ref[at * group : (at + 1) * group, c].reshape(group * block, block)
                for c in range(f_blocks)
                for ref in (gate_w, up_w)
            ],
            axis=1,
        )
        result = jnp.dot(weights, grads, preferred_element_type=F32).T
        columns = slice(at * group * block, (at + 1) * group * block)
        own[:, columns] = result[:half]
        send[:, columns] = result[half:].astype(BF16)


def d_tokens_part(coef, dh_own, dh_recv, gate_w, up_w):
    d_blocks, f_blocks, block, _ = gate_w.shape
    tokens = dh_own.shape[1]
    width = d_blocks * block
    group = max(n for n in (1, 2, 4) if d_blocks % n == 0)
    return pl.pallas_call(
        functools.partial(d_tokens_body, group),
        out_shape=(
            jax.ShapeDtypeStruct((tokens // 2, width), F32),
            jax.ShapeDtypeStruct((tokens // 2, width), BF16),
            jax.ShapeDtypeStruct((f_blocks, tokens, 2 * block), BF16),
        ),
        in_specs=[WHOLE] * (5 + len(dh_recv)),
        out_specs=(WHOLE,) * 3,
        scratch_shapes=[pltpu.VMEM((f_blocks * 2 * block, tokens), BF16)],
        compiler_params=params(),
        cost_estimate=cost(4 * tokens * gate_w.size, 4 * gate_w.size),
        name="d_tokens",
    )(*coef, dh_own, *dh_recv, resident(gate_w), resident(up_w))


def step_slots(slots):
    return max(n for n in range(1, 17) if slots % n == 0)


def gu_grad_body(first, given, index, count, d_pair, turned, *refs):
    gate_out, up_out, *scalars = refs[given:]
    slots = Slots(index, count, *scalars)
    f_blocks = d_pair.shape[0]
    block = turned.shape[1]
    step = pl.program_id(0)

    @pl.when(step == 0)
    def _():
        slots.copy.start()
        slots.copy.wait()

    for j in range(gate_out.shape[0]):
        slot = (step + first) * gate_out.shape[0] + j
        d, f = slots.place(slot, f_blocks)
        result = jnp.dot(turned[d], d_pair[f], preferred_element_type=F32)
        result = jnp.where(slot < slots.live, result, 0.0).astype(BF16)
        gate_out[j] = result[:, :block]
        up_out[j] = result[:, block:]


def gu_grads(index, count, d_pair, turned, total, begin, end, before):
    block, tokens = turned.shape[1:]
    chunk = step_slots(math.gcd(begin, end))
    first = begin // chunk
    shape = jax.ShapeDtypeStruct((total, block, block), BF16)
    out = pl.BlockSpec((chunk, block, block), lambda i: (i + first, 0, 0))
    size = (end - begin) * block * block
    return pl.pallas_call(
        functools.partial(gu_grad_body, first, len(before)),
        out_shape=(shape,) * 2,
        grid=((end - begin) // chunk,),
        in_specs=[IN_HBM, SCALARS] + [WHOLE] * 2 + [pl.BlockSpec(memory_space=pl.ANY)] * len(before),
        out_specs=(out,) * 2,
        scratch_shapes=Slots.scratch(index),
        input_output_aliases={4 + at: at for at in range(len(before))},
        compiler_params=params(),
        cost_estimate=cost(4 * size * tokens, 4 * size),
        name="gu_grads",
    )(in_hbm(index), count, d_pair, turned, *before)


def activate_body(*refs):
    own, *recv, hidden, coef = refs
    block = hidden.shape[2]
    for f in range(hidden.shape[0]):
        both = own[f]
        for part in recv:
            both = both + part[f].astype(F32)
        gate, up = both[:, :block], both[:, block:]
        sig = jax.nn.sigmoid(gate)
        silu = gate * sig
        hidden[f] = (silu * up).astype(BF16)
        coef[f, :, :block] = up * sig * (1.0 + gate * (1.0 - sig))
        coef[f, :, block:] = silu


def activate(own, recv):
    f_blocks, tokens, pair = own.shape
    return pl.pallas_call(
        activate_body,
        out_shape=(
            jax.ShapeDtypeStruct((f_blocks, tokens, pair // 2), BF16),
            jax.ShapeDtypeStruct(own.shape, F32),
        ),
        in_specs=[WHOLE] * (1 + len(recv)),
        out_specs=(WHOLE,) * 2,
        compiler_params=params(),
        cost_estimate=cost(20 * own.size, 8 * own.size),
        name="activate",
    )(own, *recv)


def down_grad_body(index, count, near, far, *refs):
    *pieces, out, index_here, slots_sem, turned, dense, sem = refs
    slots = Slots(index, count, index_here, slots_sem)
    slots.copy.start()
    block = dense.shape[1]
    f_blocks = turned.shape[0] // block
    d_blocks = (dense.shape[0] - 1) // f_blocks
    zeros = f_blocks * d_blocks
    dense[zeros] = jnp.zeros(dense.shape[1:], dense.dtype)
    for f in range(f_blocks):
        half = (near, far)[f * 2 // f_blocks]
        turned[f * block : (f + 1) * block, :] = half[f % (f_blocks // 2)].T
    for d in range(0, d_blocks, 2):
        y = jnp.concatenate([piece[:, d * block : (d + 2) * block] for piece in pieces], axis=0)
        for f in range(0, f_blocks, 2):
            rows = turned[f * block : (f + 2) * block, :]
            result = jnp.dot(rows, y, preferred_element_type=F32).astype(BF16)
            for row in range(2):
                for side in range(2):
                    dense[(f + row) * d_blocks + d + side] = result[
                        row * block : (row + 1) * block, side * block : (side + 1) * block
                    ]
    slots.copy.wait()
    total = out.shape[0]

    @pl.loop(0, total, unroll=max(n for n in (1, 2, 4, 8) if total % n == 0))
    def _(s):
        place = jnp.where(s < slots.live, slots.index[0, 0, s], zeros)
        pltpu.make_async_copy(dense.at[place], out.at[s], sem).start()

    pltpu.make_async_copy(out, out, sem).wait()


def down_grads(index, count, pieces, near, far, slots):
    f_blocks, tokens, block = near.shape
    f_blocks = 2 * f_blocks
    d_blocks = pieces[0].shape[1] // block
    blocks = f_blocks * d_blocks + 1
    return pl.pallas_call(
        down_grad_body,
        out_shape=jax.ShapeDtypeStruct((slots, block, block), BF16),
        in_specs=[IN_HBM, SCALARS] + [WHOLE] * (2 + len(pieces)),
        out_specs=IN_HBM,
        scratch_shapes=[
            *Slots.scratch(index),
            pltpu.VMEM((f_blocks * block, tokens), BF16),
            pltpu.VMEM((blocks, block, block), BF16),
            pltpu.SemaphoreType.DMA,
        ],
        compiler_params=params(VMEM_LIMIT + 2 * blocks * block * block),
        cost_estimate=cost(2 * slots * block * block * tokens, 2 * slots * block * block),
        name="down_grads",
    )(in_hbm(index), count, near, far, *pieces)


def on_device(
    tokens, cotangent, gate_vals, up_vals, gu_index, gu_count, down_vals, down_index, down_count
):
    block = gate_vals.shape[-1]
    slots = gate_vals.shape[2]
    wide = lax.axis_size("wide")
    narrow = lax.axis_size("narrow")
    chips = wide // 2
    rows = tokens.shape[0]
    d_blocks = tokens.shape[1] // block
    f_blocks = FF // (block * wide)

    def exchange(array):
        return [swap(array, "narrow", narrow, k) for k in range(1, narrow)]

    flips = [chips >> hop for hop in range(1, chips.bit_length())]
    vals = (gate_vals, up_vals)
    x, index = tokens, gu_index
    weights = []
    for hop, flip in enumerate(flips):
        if hop > 0:
            x = jnp.concatenate([x, x_recv], axis=0)
            x, weights, index = lax.optimization_barrier((x, weights, index))
        x_recv = swap(x, "wide", wide, 2 * flip)
        if hop < 2:
            weights.append(fill(index, gu_count, vals[hop], d_blocks, f_blocks))
    y, index, _ = lax.optimization_barrier((cotangent, down_index, x))
    down_w = fill(index, down_count, down_vals, f_blocks, d_blocks)
    for flip in flips[:-1]:
        y = jnp.concatenate([y, swap(y, "wide", wide, 2 * flip)], axis=0)
        y, down_w = lax.optimization_barrier((y, down_w))
    x_pieces = [x, x_recv, swap(x, "wide", wide, 1), swap(x_recv, "wide", wide, 1)]
    y, _ = lax.optimization_barrier((y, x_recv))
    y_recv = swap(y, "wide", wide, 2 * flips[-1])

    near_own, near_send = gate_up(x_pieces, *weights, 0)
    near_recv = exchange(near_send)
    late, _ = lax.optimization_barrier((x, near_send))
    far_own, far_send = gate_up([late, *x_pieces[1:]], *weights, 1)
    far_recv = exchange(far_send)
    y, y_recv, _ = lax.optimization_barrier((y, y_recv, far_send))
    y_pieces = [y, y_recv, swap(y, "wide", wide, 1), swap(y_recv, "wide", wide, 1)]
    near_hidden, near_coef = activate(near_own, near_recv)
    down_w, near_hidden = lax.optimization_barrier((down_w, near_hidden))
    dh_own, dh_send, turned = d_hidden(y_pieces, x_pieces, down_w)
    dh_recv = exchange(dh_send)
    far_hidden, far_coef = activate(far_own, far_recv)
    down_grad = down_grads(down_index, down_count, y_pieces, near_hidden, far_hidden, slots)
    down_grad, far_coef = lax.optimization_barrier((down_grad, far_coef))
    own, send, d_pair = d_tokens_part((near_coef, far_coef), dh_own, dh_recv, *weights)

    own = own + swap(send, "wide", wide, 1).astype(F32)
    kept = own.shape[0] // 2
    far = own[kept:].astype(BF16)
    own = own[:kept]
    cut = slots * 2 // 3 if slots % 3 == 0 else slots
    far, d_pair = lax.optimization_barrier((far, d_pair))
    grads = gu_grads(gu_index, gu_count, d_pair, turned, slots, 0, cut, ())
    own = own + swap(far, "wide", wide, 2 * flips[-1]).astype(F32)
    sends = [own[p * rows : (p + 1) * rows].astype(BF16) for p in range(1, chips // 2)]
    if cut < slots:
        sends, d_pair, grads = lax.optimization_barrier((sends, d_pair, grads))
        grads = gu_grads(gu_index, gu_count, d_pair, turned, slots, cut, slots, grads)
    own = own[:rows]
    for p, part in enumerate(sends, 1):
        flip = sum(flips[bit] for bit in range(len(flips)) if p >> bit & 1)
        own = own + swap(part, "wide", wide, 2 * flip).astype(F32)
    gate_grad, up_grad = grads
    return (
        own.astype(BF16),
        gate_grad[None, None],
        up_grad[None, None],
        down_grad[None, None],
    )


def solution(mesh):
    in_specs = (
        P("wide", "narrow"),
        P("wide", "narrow"),
        P("narrow", "wide", None, None, None),
        P("narrow", "wide", None, None, None),
        P("narrow", "wide", None),
        P("narrow", "wide"),
        P("wide", "narrow", None, None, None),
        P("wide", "narrow", None),
        P("wide", "narrow"),
    )
    out_specs = (
        P("wide", "narrow"),
        P("narrow", "wide", None, None, None),
        P("narrow", "wide", None, None, None),
        P("wide", "narrow", None, None, None),
    )
    return jax.shard_map(
        on_device, mesh=mesh, in_specs=in_specs, out_specs=out_specs, check_vma=False
    )
```

```python
import functools
import math

import jax
import jax.numpy as jnp
from jax import lax
from jax.experimental import pallas as pl
from jax.experimental.pallas import tpu as pltpu
from jax.sharding import PartitionSpec as P

FF = 16384
F32 = jnp.float32
BF16 = jnp.bfloat16
VMEM_LIMIT = 8 * 1024 * 1024

WHOLE = pl.BlockSpec(memory_space=pltpu.VMEM)
SCALARS = pl.BlockSpec(memory_space=pltpu.SMEM)
IN_HBM = pl.BlockSpec(memory_space=pltpu.HBM)


def params(vmem=VMEM_LIMIT):
    return pltpu.CompilerParams(vmem_limit_bytes=vmem)


def cost(flops, bytes_accessed):
    return pl.CostEstimate(flops=int(flops), bytes_accessed=int(bytes_accessed), transcendentals=0)


def resident(array):
    return pltpu.with_memory_space_constraint(array, pltpu.VMEM)


def in_hbm(array):
    return pltpu.with_memory_space_constraint(array, pltpu.HBM)


def swap(array, axis, size, flip):
    return lax.ppermute(array, axis, [(i, i ^ flip) for i in range(size)])


def split_index(number, size):
    if size & (size - 1):
        return number // size, number % size
    return number >> (size.bit_length() - 1), number & (size - 1)


class Slots:
    def __init__(self, index_from, count, index, sem):
        self.copy = pltpu.make_async_copy(index_from, index, sem)
        self.index, self.live = index, count[0, 0]

    @staticmethod
    def scratch(index):
        return [pltpu.SMEM(index.shape, index.dtype), pltpu.SemaphoreType.DMA]

    def place(self, slot, size):
        return split_index(self.index[0, 0, slot], size)


def fill_body(index, count, source, *refs):
    target, index_here, slots_sem, sem = refs[-4:]
    slots = Slots(index, count, index_here, slots_sem)
    slots.copy.start()
    outer, inner = target.shape[:2]
    chunk = min(inner, 8)

    @pl.loop(0, outer)
    def _(high):
        target[high] = jnp.zeros(target.shape[1:], target.dtype)

    slots.copy.wait()

    @pl.loop(0, slots.live)
    def _(s):
        high, low = slots.place(s, inner)
        pltpu.make_async_copy(source.at[0, 0, s], target.at[high, low], sem).start()

    many, few = split_index(slots.live, chunk)

    @pl.loop(0, many)
    def _(_):
        blocks = pl.ds(0, chunk)
        pltpu.make_async_copy(source.at[0, 0, blocks], target.at[0, blocks], sem).wait()

    @pl.loop(0, few)
    def _(_):
        pltpu.make_async_copy(source.at[0, 0, 0], target.at[0, 0], sem).wait()


def fill(index, count, slots, outer, inner, early=()):
    block = slots.shape[-1]
    return pl.pallas_call(
        fill_body,
        out_shape=pltpu.VMEM((outer, inner, block, block), BF16),
        in_specs=[IN_HBM, SCALARS, IN_HBM] + [SCALARS] * len(early),
        out_specs=WHOLE,
        scratch_shapes=[*Slots.scratch(index), pltpu.SemaphoreType.DMA],
        compiler_params=params(),
        cost_estimate=cost(0, slots.size * 2),
        name="fill",
    )(in_hbm(index), count, in_hbm(slots), *early)


def stack(pieces):
    return jnp.concatenate([piece[...] for piece in pieces], axis=0)


def gate_up_body(first, *refs):
    *pieces, gate_w, up_w, own, send = refs
    d_blocks, _, block, _ = gate_w.shape
    x = stack(pieces)

    @pl.loop(0, own.shape[0])
    def _(c):
        weights = jnp.concatenate(
            [
                gate_w[:, first + c].reshape(d_blocks * block, block),
                up_w[:, first + c].reshape(d_blocks * block, block),
            ],
            axis=1,
        )
        result = jnp.dot(x, weights, preferred_element_type=F32)
        own[c] = result
        send[c] = result.astype(BF16)


def gate_up(pieces, gate_w, up_w, half):
    d_blocks, f_blocks, block, _ = gate_w.shape
    tokens = sum(piece.shape[0] for piece in pieces)
    shape = (f_blocks // 2, tokens, 2 * block)
    return pl.pallas_call(
        functools.partial(gate_up_body, half * f_blocks // 2),
        out_shape=(jax.ShapeDtypeStruct(shape, F32), jax.ShapeDtypeStruct(shape, BF16)),
        in_specs=[WHOLE] * (len(pieces) + 2),
        out_specs=(WHOLE,) * 2,
        compiler_params=params(),
        cost_estimate=cost(2 * tokens * gate_w.size, 2 * gate_w.size),
        name="gate_up",
    )(*pieces, resident(gate_w), resident(up_w))


def d_hidden_body(pieces_count, *refs):
    y_pieces, x_pieces = refs[:pieces_count], refs[pieces_count : 2 * pieces_count]
    down_w, own, send, turned = refs[2 * pieces_count :]
    f_blocks, d_blocks, block, _ = down_w.shape
    y = stack(y_pieces)

    @pl.loop(0, f_blocks // 2)
    def _(pair):
        weights = jnp.concatenate(
            [
                down_w[pl.ds(2 * pair, 2), d].reshape(2 * block, block)
                for d in range(d_blocks)
            ],
            axis=1,
        )
        result = lax.dot_general(
            y, weights, (((1,), (1,)), ((), ())), preferred_element_type=F32
        )
        for half in range(2):
            part = result[:, half * block : (half + 1) * block]
            own[2 * pair + half] = part
            send[2 * pair + half] = part.astype(BF16)

    for d in range(d_blocks):
        columns = slice(d * block, (d + 1) * block)
        turned[d] = jnp.concatenate([piece[:, columns] for piece in x_pieces], axis=0).T


def d_hidden(y_pieces, x_pieces, down_w):
    f_blocks, d_blocks, block, _ = down_w.shape
    tokens = sum(piece.shape[0] for piece in y_pieces)
    shape = (f_blocks, tokens, block)
    return pl.pallas_call(
        functools.partial(d_hidden_body, len(y_pieces)),
        out_shape=(
            jax.ShapeDtypeStruct(shape, F32),
            jax.ShapeDtypeStruct(shape, BF16),
            jax.ShapeDtypeStruct((d_blocks, block, tokens), BF16),
        ),
        in_specs=[WHOLE] * (2 * len(y_pieces) + 1),
        out_specs=(WHOLE,) * 3,
        compiler_params=params(),
        cost_estimate=cost(2 * tokens * down_w.size, 2 * down_w.size),
        name="d_hidden",
    )(*y_pieces, *x_pieces, resident(down_w))


def d_tokens_body(group, *refs):
    *coef, dh_own = refs[:3]
    *dh_recv, gate_w, up_w, own, send, d_pair, turned = refs[3:]
    d_blocks, f_blocks, block, _ = gate_w.shape
    half = own.shape[0]
    for c in range(f_blocks):
        dh = dh_own[c]
        for part in dh_recv:
            dh = dh + part[c].astype(F32)
        side, at = divmod(c, f_blocks // 2)
        both = (jnp.concatenate([dh, dh], axis=1) * coef[side][at]).astype(BF16)
        d_pair[c] = both
        for side in range(2):
            turned[pl.ds((2 * c + side) * block, block), :] = both[
                :, side * block : (side + 1) * block
            ].T
    grads = turned[...]

    for at in range(d_blocks // group):
        weights = jnp.concatenate(
            [
                ref[at * group : (at + 1) * group, c].reshape(group * block, block)
                for c in range(f_blocks)
                for ref in (gate_w, up_w)
            ],
            axis=1,
        )
        result = jnp.dot(weights, grads, preferred_element_type=F32).T
        columns = slice(at * group * block, (at + 1) * group * block)
        own[:, columns] = result[:half]
        send[:, columns] = result[half:].astype(BF16)


def d_tokens_part(coef, dh_own, dh_recv, gate_w, up_w):
    d_blocks, f_blocks, block, _ = gate_w.shape
    tokens = dh_own.shape[1]
    width = d_blocks * block
    group = max(n for n in (1, 2, 4) if d_blocks % n == 0)
    return pl.pallas_call(
        functools.partial(d_tokens_body, group),
        out_shape=(
            jax.ShapeDtypeStruct((tokens // 2, width), F32),
            jax.ShapeDtypeStruct((tokens // 2, width), BF16),
            jax.ShapeDtypeStruct((f_blocks, tokens, 2 * block), BF16),
        ),
        in_specs=[WHOLE] * (5 + len(dh_recv)),
        out_specs=(WHOLE,) * 3,
        scratch_shapes=[pltpu.VMEM((f_blocks * 2 * block, tokens), BF16)],
        compiler_params=params(),
        cost_estimate=cost(4 * tokens * gate_w.size, 4 * gate_w.size),
        name="d_tokens",
    )(*coef, dh_own, *dh_recv, resident(gate_w), resident(up_w))


def step_slots(slots):
    return max(n for n in range(1, 17) if slots % n == 0)


def gu_grad_body(first, given, index, count, d_pair, turned, *refs):
    gate_out, up_out, *scalars = refs[given:]
    slots = Slots(index, count, *scalars)
    f_blocks = d_pair.shape[0]
    block = turned.shape[1]
    step = pl.program_id(0)

    @pl.when(step == 0)
    def _():
        slots.copy.start()
        slots.copy.wait()

    for j in range(gate_out.shape[0]):
        slot = (step + first) * gate_out.shape[0] + j
        d, f = slots.place(slot, f_blocks)
        result = jnp.dot(turned[d], d_pair[f], preferred_element_type=F32)
        result = jnp.where(slot < slots.live, result, 0.0).astype(BF16)
        gate_out[j] = result[:, :block]
        up_out[j] = result[:, block:]


def gu_grads(index, count, d_pair, turned, total, begin, end, before):
    block, tokens = turned.shape[1:]
    chunk = step_slots(math.gcd(begin, end))
    first = begin // chunk
    shape = jax.ShapeDtypeStruct((total, block, block), BF16)
    out = pl.BlockSpec((chunk, block, block), lambda i: (i + first, 0, 0))
    size = (end - begin) * block * block
    return pl.pallas_call(
        functools.partial(gu_grad_body, first, len(before)),
        out_shape=(shape,) * 2,
        grid=((end - begin) // chunk,),
        in_specs=[IN_HBM, SCALARS] + [WHOLE] * 2 + [pl.BlockSpec(memory_space=pl.ANY)] * len(before),
        out_specs=(out,) * 2,
        scratch_shapes=Slots.scratch(index),
        input_output_aliases={4 + at: at for at in range(len(before))},
        compiler_params=params(),
        cost_estimate=cost(4 * size * tokens, 4 * size),
        name="gu_grads",
    )(in_hbm(index), count, d_pair, turned, *before)


def activate_body(*refs):
    own, *recv, hidden, coef = refs
    block = hidden.shape[2]
    for f in range(hidden.shape[0]):
        both = own[f]
        for part in recv:
            both = both + part[f].astype(F32)
        gate, up = both[:, :block], both[:, block:]
        sig = jax.nn.sigmoid(gate)
        silu = gate * sig
        hidden[f] = (silu * up).astype(BF16)
        coef[f, :, :block] = up * sig * (1.0 + gate * (1.0 - sig))
        coef[f, :, block:] = silu


def activate(own, recv):
    f_blocks, tokens, pair = own.shape
    return pl.pallas_call(
        activate_body,
        out_shape=(
            jax.ShapeDtypeStruct((f_blocks, tokens, pair // 2), BF16),
            jax.ShapeDtypeStruct(own.shape, F32),
        ),
        in_specs=[WHOLE] * (1 + len(recv)),
        out_specs=(WHOLE,) * 2,
        compiler_params=params(),
        cost_estimate=cost(20 * own.size, 8 * own.size),
        name="activate",
    )(own, *recv)


def down_grad_body(index, count, near, far, *refs):
    *pieces, out, index_here, slots_sem, turned, dense, sem = refs
    slots = Slots(index, count, index_here, slots_sem)
    slots.copy.start()
    block = dense.shape[1]
    f_blocks = turned.shape[0] // block
    d_blocks = (dense.shape[0] - 1) // f_blocks
    zeros = f_blocks * d_blocks
    dense[zeros] = jnp.zeros(dense.shape[1:], dense.dtype)
    for f in range(f_blocks):
        half = (near, far)[f * 2 // f_blocks]
        turned[f * block : (f + 1) * block, :] = half[f % (f_blocks // 2)].T
    for d in range(0, d_blocks, 2):
        y = jnp.concatenate([piece[:, d * block : (d + 2) * block] for piece in pieces], axis=0)
        for f in range(0, f_blocks, 2):
            rows = turned[f * block : (f + 2) * block, :]
            result = jnp.dot(rows, y, preferred_element_type=F32).astype(BF16)
            for row in range(2):
                for side in range(2):
                    dense[(f + row) * d_blocks + d + side] = result[
                        row * block : (row + 1) * block, side * block : (side + 1) * block
                    ]
    slots.copy.wait()
    total = out.shape[0]

    @pl.loop(0, total, unroll=max(n for n in (1, 2, 4, 8) if total % n == 0))
    def _(s):
        place = jnp.where(s < slots.live, slots.index[0, 0, s], zeros)
        pltpu.make_async_copy(dense.at[place], out.at[s], sem).start()

    pltpu.make_async_copy(out, out, sem).wait()


def down_grads(index, count, pieces, near, far, slots):
    f_blocks, tokens, block = near.shape
    f_blocks = 2 * f_blocks
    d_blocks = pieces[0].shape[1] // block
    blocks = f_blocks * d_blocks + 1
    return pl.pallas_call(
        down_grad_body,
        out_shape=jax.ShapeDtypeStruct((slots, block, block), BF16),
        in_specs=[IN_HBM, SCALARS] + [WHOLE] * (2 + len(pieces)),
        out_specs=IN_HBM,
        scratch_shapes=[
            *Slots.scratch(index),
            pltpu.VMEM((f_blocks * block, tokens), BF16),
            pltpu.VMEM((blocks, block, block), BF16),
            pltpu.SemaphoreType.DMA,
        ],
        compiler_params=params(VMEM_LIMIT + 2 * blocks * block * block),
        cost_estimate=cost(2 * slots * block * block * tokens, 2 * slots * block * block),
        name="down_grads",
    )(in_hbm(index), count, near, far, *pieces)


def on_device(
    tokens, cotangent, gate_vals, up_vals, gu_index, gu_count, down_vals, down_index, down_count
):
    block = gate_vals.shape[-1]
    slots = gate_vals.shape[2]
    wide = lax.axis_size("wide")
    narrow = lax.axis_size("narrow")
    chips = wide // 2
    rows = tokens.shape[0]
    d_blocks = tokens.shape[1] // block
    f_blocks = FF // (block * wide)

    def exchange(array):
        return [swap(array, "narrow", narrow, k) for k in range(1, narrow)]

    flips = [chips >> hop for hop in range(1, chips.bit_length())]
    vals = (gate_vals, up_vals)
    x, index = tokens, gu_index
    weights = []
    for hop, flip in enumerate(flips):
        if hop > 0:
            x = jnp.concatenate([x, x_recv], axis=0)
            x, weights, index = lax.optimization_barrier((x, weights, index))
        x_recv = swap(x, "wide", wide, 2 * flip)
        if hop < 2:
            early = (down_count,) if hop == 1 else ()
            weights.append(fill(index, gu_count, vals[hop], d_blocks, f_blocks, early))
        if hop == 1:
            y, _ = lax.optimization_barrier((cotangent, weights[1]))
    index, _ = lax.optimization_barrier((down_index, x))
    down_w = fill(index, down_count, down_vals, f_blocks, d_blocks)
    for flip in flips[:-1]:
        y = jnp.concatenate([y, swap(y, "wide", wide, 2 * flip)], axis=0)
    x, down_w = lax.optimization_barrier((x, down_w))
    x_pieces = [x, x_recv, swap(x, "wide", wide, 1), swap(x_recv, "wide", wide, 1)]
    y, _ = lax.optimization_barrier((y, x_recv))
    y_recv = swap(y, "wide", wide, 2 * flips[-1])

    near_own, near_send = gate_up(x_pieces, *weights, 0)
    near_recv = exchange(near_send)
    late, _ = lax.optimization_barrier((x, near_send))
    far_own, far_send = gate_up([late, *x_pieces[1:]], *weights, 1)
    far_recv = exchange(far_send)
    y, y_recv, _ = lax.optimization_barrier((y, y_recv, far_send))
    y_pieces = [y, y_recv, swap(y, "wide", wide, 1), swap(y_recv, "wide", wide, 1)]
    near_hidden, near_coef = activate(near_own, near_recv)
    down_w, near_hidden = lax.optimization_barrier((down_w, near_hidden))
    dh_own, dh_send, turned = d_hidden(y_pieces, x_pieces, down_w)
    dh_recv = exchange(dh_send)
    far_hidden, far_coef = activate(far_own, far_recv)
    down_grad = down_grads(down_index, down_count, y_pieces, near_hidden, far_hidden, slots)
    down_grad, far_coef = lax.optimization_barrier((down_grad, far_coef))
    own, send, d_pair = d_tokens_part((near_coef, far_coef), dh_own, dh_recv, *weights)

    own = own + swap(send, "wide", wide, 1).astype(F32)
    kept = own.shape[0] // 2
    far = own[kept:].astype(BF16)
    own = own[:kept]
    cut = slots * 2 // 3 if slots % 3 == 0 else slots
    far, d_pair = lax.optimization_barrier((far, d_pair))
    grads = gu_grads(gu_index, gu_count, d_pair, turned, slots, 0, cut, ())
    own = own + swap(far, "wide", wide, 2 * flips[-1]).astype(F32)
    sends = [own[p * rows : (p + 1) * rows].astype(BF16) for p in range(1, chips // 2)]
    if cut < slots:
        sends, d_pair, grads = lax.optimization_barrier((sends, d_pair, grads))
        grads = gu_grads(gu_index, gu_count, d_pair, turned, slots, cut, slots, grads)
    own = own[:rows]
    for p, part in enumerate(sends, 1):
        flip = sum(flips[bit] for bit in range(len(flips)) if p >> bit & 1)
        own = own + swap(part, "wide", wide, 2 * flip).astype(F32)
    gate_grad, up_grad = grads
    return (
        own.astype(BF16),
        gate_grad[None, None],
        up_grad[None, None],
        down_grad[None, None],
    )


def solution(mesh):
    in_specs = (
        P("wide", "narrow"),
        P("wide", "narrow"),
        P("narrow", "wide", None, None, None),
        P("narrow", "wide", None, None, None),
        P("narrow", "wide", None),
        P("narrow", "wide"),
        P("wide", "narrow", None, None, None),
        P("wide", "narrow", None),
        P("wide", "narrow"),
    )
    out_specs = (
        P("wide", "narrow"),
        P("narrow", "wide", None, None, None),
        P("narrow", "wide", None, None, None),
        P("wide", "narrow", None, None, None),
    )
    return jax.shard_map(
        on_device, mesh=mesh, in_specs=in_specs, out_specs=out_specs, check_vma=False
    )
```

```python
import functools
import math

import jax
import jax.numpy as jnp
from jax import lax
from jax.experimental import pallas as pl
from jax.experimental.pallas import tpu as pltpu
from jax.sharding import PartitionSpec as P

FF = 16384
F32 = jnp.float32
BF16 = jnp.bfloat16
VMEM_LIMIT = 8 * 1024 * 1024

WHOLE = pl.BlockSpec(memory_space=pltpu.VMEM)
SCALARS = pl.BlockSpec(memory_space=pltpu.SMEM)
IN_HBM = pl.BlockSpec(memory_space=pltpu.HBM)


def params(vmem=VMEM_LIMIT):
    return pltpu.CompilerParams(vmem_limit_bytes=vmem)


def cost(flops, bytes_accessed):
    return pl.CostEstimate(flops=int(flops), bytes_accessed=int(bytes_accessed), transcendentals=0)


def resident(array):
    return pltpu.with_memory_space_constraint(array, pltpu.VMEM)


def in_hbm(array):
    return pltpu.with_memory_space_constraint(array, pltpu.HBM)


def swap(array, axis, size, flip):
    return lax.ppermute(array, axis, [(i, i ^ flip) for i in range(size)])


def split_index(number, size):
    if size & (size - 1):
        return number // size, number % size
    return number >> (size.bit_length() - 1), number & (size - 1)


class Slots:
    def __init__(self, index_from, count, index, sem):
        self.copy = pltpu.make_async_copy(index_from, index, sem)
        self.index, self.live = index, count[0, 0]

    @staticmethod
    def scratch(index):
        return [pltpu.SMEM(index.shape, index.dtype), pltpu.SemaphoreType.DMA]

    def place(self, slot, size):
        return split_index(self.index[0, 0, slot], size)


def fill_body(index, count, source, *refs):
    target, index_here, slots_sem, sem = refs[-4:]
    slots = Slots(index, count, index_here, slots_sem)
    slots.copy.start()
    outer, inner = target.shape[:2]
    chunk = min(inner, 8)

    @pl.loop(0, outer)
    def _(high):
        target[high] = jnp.zeros(target.shape[1:], target.dtype)

    slots.copy.wait()

    @pl.loop(0, slots.live)
    def _(s):
        high, low = slots.place(s, inner)
        pltpu.make_async_copy(source.at[0, 0, s], target.at[high, low], sem).start()

    many, few = split_index(slots.live, chunk)

    @pl.loop(0, many)
    def _(_):
        blocks = pl.ds(0, chunk)
        pltpu.make_async_copy(source.at[0, 0, blocks], target.at[0, blocks], sem).wait()

    @pl.loop(0, few)
    def _(_):
        pltpu.make_async_copy(source.at[0, 0, 0], target.at[0, 0], sem).wait()


def fill(index, count, slots, outer, inner, early=()):
    block = slots.shape[-1]
    return pl.pallas_call(
        fill_body,
        out_shape=pltpu.VMEM((outer, inner, block, block), BF16),
        in_specs=[IN_HBM, SCALARS, IN_HBM] + [SCALARS] * len(early),
        out_specs=WHOLE,
        scratch_shapes=[*Slots.scratch(index), pltpu.SemaphoreType.DMA],
        compiler_params=params(),
        cost_estimate=cost(0, slots.size * 2),
        name="fill",
    )(in_hbm(index), count, in_hbm(slots), *early)


def stack(pieces):
    return jnp.concatenate([piece[...] for piece in pieces], axis=0)


def gate_up_body(first, *refs):
    *pieces, gate_w, up_w, own, send = refs
    d_blocks, _, block, _ = gate_w.shape
    x = stack(pieces)
    for c in range(own.shape[0]):
        weights = jnp.concatenate(
            [
                gate_w[:, first + c].reshape(d_blocks * block, block),
                up_w[:, first + c].reshape(d_blocks * block, block),
            ],
            axis=1,
        )
        result = jnp.dot(x, weights, preferred_element_type=F32)
        own[c] = result
        send[c] = result.astype(BF16)


def gate_up(pieces, gate_w, up_w, half):
    d_blocks, f_blocks, block, _ = gate_w.shape
    tokens = sum(piece.shape[0] for piece in pieces)
    shape = (f_blocks // 2, tokens, 2 * block)
    return pl.pallas_call(
        functools.partial(gate_up_body, half * f_blocks // 2),
        out_shape=(jax.ShapeDtypeStruct(shape, F32), jax.ShapeDtypeStruct(shape, BF16)),
        in_specs=[WHOLE] * (len(pieces) + 2),
        out_specs=(WHOLE,) * 2,
        compiler_params=params(),
        cost_estimate=cost(2 * tokens * gate_w.size, 2 * gate_w.size),
        name="gate_up",
    )(*pieces, resident(gate_w), resident(up_w))


def d_hidden_body(group, *refs):
    *pieces, down_w, own, send, turned = refs
    f_blocks, d_blocks, block, _ = down_w.shape
    for d in range(d_blocks):
        at = slice(d * block, (d + 1) * block)
        turned[at, :] = jnp.concatenate([piece[:, at] for piece in pieces], axis=0).T
    y = turned[...]
    for f in range(0, f_blocks, group):
        weights = jnp.concatenate(
            [
                down_w[f : f + group, d].reshape(group * block, block)
                for d in range(d_blocks)
            ],
            axis=1,
        )
        result = jnp.dot(weights, y, preferred_element_type=F32).T
        for side in range(group):
            part = result[:, side * block : (side + 1) * block]
            own[f + side] = part
            send[f + side] = part.astype(BF16)


def d_hidden(pieces, down_w):
    f_blocks, d_blocks, block, _ = down_w.shape
    tokens = sum(piece.shape[0] for piece in pieces)
    shape = (f_blocks, tokens, block)
    group = max(n for n in (1, 2, 4) if f_blocks % n == 0)
    return pl.pallas_call(
        functools.partial(d_hidden_body, group),
        out_shape=(jax.ShapeDtypeStruct(shape, F32), jax.ShapeDtypeStruct(shape, BF16)),
        in_specs=[WHOLE] * (len(pieces) + 1),
        out_specs=(WHOLE,) * 2,
        scratch_shapes=[pltpu.VMEM((d_blocks * block, tokens), BF16)],
        compiler_params=params(),
        cost_estimate=cost(2 * tokens * down_w.size, 2 * down_w.size),
        name="d_hidden",
    )(*pieces, resident(down_w))


def turn_body(*refs):
    *pieces, turned = refs
    block = turned.shape[1]
    for d in range(turned.shape[0]):
        columns = slice(d * block, (d + 1) * block)
        turned[d] = jnp.concatenate([piece[:, columns] for piece in pieces], axis=0).T


def turn(pieces, block):
    tokens = sum(piece.shape[0] for piece in pieces)
    width = pieces[0].shape[1]
    return pl.pallas_call(
        turn_body,
        out_shape=jax.ShapeDtypeStruct((width // block, block, tokens), BF16),
        in_specs=[WHOLE] * len(pieces),
        out_specs=WHOLE,
        compiler_params=params(),
        cost_estimate=cost(0, 4 * tokens * width),
        name="turn",
    )(*pieces)


def d_tokens_body(group, *refs):
    *coef, dh_own = refs[:3]
    *dh_recv, gate_w, up_w, own, send, d_pair, turned = refs[3:]
    d_blocks, f_blocks, block, _ = gate_w.shape
    half = own.shape[0]
    for c in range(f_blocks):
        dh = dh_own[c]
        for part in dh_recv:
            dh = dh + part[c].astype(F32)
        side, at = divmod(c, f_blocks // 2)
        both = (jnp.concatenate([dh, dh], axis=1) * coef[side][at]).astype(BF16)
        d_pair[c] = both
        for side in range(2):
            turned[pl.ds((2 * c + side) * block, block), :] = both[
                :, side * block : (side + 1) * block
            ].T
    grads = turned[...]

    for at in range(d_blocks // group):
        weights = jnp.concatenate(
            [
                ref[at * group : (at + 1) * group, c].reshape(group * block, block)
                for c in range(f_blocks)
                for ref in (gate_w, up_w)
            ],
            axis=1,
        )
        result = jnp.dot(weights, grads, preferred_element_type=F32).T
        columns = slice(at * group * block, (at + 1) * group * block)
        own[:, columns] = result[:half]
        send[:, columns] = result[half:].astype(BF16)


def d_tokens_part(coef, dh_own, dh_recv, gate_w, up_w):
    d_blocks, f_blocks, block, _ = gate_w.shape
    tokens = dh_own.shape[1]
    width = d_blocks * block
    group = max(n for n in (1, 2, 4) if d_blocks % n == 0)
    return pl.pallas_call(
        functools.partial(d_tokens_body, group),
        out_shape=(
            jax.ShapeDtypeStruct((tokens // 2, width), F32),
            jax.ShapeDtypeStruct((tokens // 2, width), BF16),
            jax.ShapeDtypeStruct((f_blocks, tokens, 2 * block), BF16),
        ),
        in_specs=[WHOLE] * (5 + len(dh_recv)),
        out_specs=(WHOLE,) * 3,
        scratch_shapes=[pltpu.VMEM((f_blocks * 2 * block, tokens), BF16)],
        compiler_params=params(),
        cost_estimate=cost(4 * tokens * gate_w.size, 4 * gate_w.size),
        name="d_tokens",
    )(*coef, dh_own, *dh_recv, resident(gate_w), resident(up_w))


def step_slots(slots):
    return max(n for n in range(1, 17) if slots % n == 0)


def gu_grad_body(first, given, index, count, d_pair, turned, *refs):
    gate_out, up_out, *scalars = refs[given:]
    slots = Slots(index, count, *scalars)
    f_blocks = d_pair.shape[0]
    block = turned.shape[1]
    step = pl.program_id(0)

    @pl.when(step == 0)
    def _():
        slots.copy.start()
        slots.copy.wait()

    for j in range(gate_out.shape[0]):
        slot = (step + first) * gate_out.shape[0] + j
        d, f = slots.place(slot, f_blocks)
        result = jnp.dot(turned[d], d_pair[f], preferred_element_type=F32)
        result = jnp.where(slot < slots.live, result, 0.0).astype(BF16)
        gate_out[j] = result[:, :block]
        up_out[j] = result[:, block:]


def gu_grads(index, count, d_pair, turned, total, begin, end, before):
    block, tokens = turned.shape[1:]
    chunk = step_slots(math.gcd(begin, end))
    first = begin // chunk
    shape = jax.ShapeDtypeStruct((total, block, block), BF16)
    out = pl.BlockSpec((chunk, block, block), lambda i: (i + first, 0, 0))
    size = (end - begin) * block * block
    return pl.pallas_call(
        functools.partial(gu_grad_body, first, len(before)),
        out_shape=(shape,) * 2,
        grid=((end - begin) // chunk,),
        in_specs=[IN_HBM, SCALARS] + [WHOLE] * 2 + [pl.BlockSpec(memory_space=pl.ANY)] * len(before),
        out_specs=(out,) * 2,
        scratch_shapes=Slots.scratch(index),
        input_output_aliases={4 + at: at for at in range(len(before))},
        compiler_params=params(),
        cost_estimate=cost(4 * size * tokens, 4 * size),
        name="gu_grads",
    )(in_hbm(index), count, d_pair, turned, *before)


def activate_body(*refs):
    own, *recv, hidden, coef = refs
    block = hidden.shape[2]
    for f in range(hidden.shape[0]):
        both = own[f]
        for part in recv:
            both = both + part[f].astype(F32)
        gate, up = both[:, :block], both[:, block:]
        sig = jax.nn.sigmoid(gate)
        silu = gate * sig
        hidden[f] = (silu * up).astype(BF16)
        coef[f, :, :block] = up * sig * (1.0 + gate * (1.0 - sig))
        coef[f, :, block:] = silu


def activate(own, recv):
    f_blocks, tokens, pair = own.shape
    return pl.pallas_call(
        activate_body,
        out_shape=(
            jax.ShapeDtypeStruct((f_blocks, tokens, pair // 2), BF16),
            jax.ShapeDtypeStruct(own.shape, F32),
        ),
        in_specs=[WHOLE] * (1 + len(recv)),
        out_specs=(WHOLE,) * 2,
        compiler_params=params(),
        cost_estimate=cost(20 * own.size, 8 * own.size),
        name="activate",
    )(own, *recv)


def down_grad_body(index, count, near, far, *refs):
    *pieces, out, index_here, slots_sem, turned, dense, sem = refs
    slots = Slots(index, count, index_here, slots_sem)
    slots.copy.start()
    block = dense.shape[1]
    f_blocks = turned.shape[0] // block
    d_blocks = (dense.shape[0] - 1) // f_blocks
    zeros = f_blocks * d_blocks
    dense[zeros] = jnp.zeros(dense.shape[1:], dense.dtype)
    for f in range(f_blocks):
        half = (near, far)[f * 2 // f_blocks]
        turned[f * block : (f + 1) * block, :] = half[f % (f_blocks // 2)].T
    for d in range(0, d_blocks, 2):
        y = jnp.concatenate([piece[:, d * block : (d + 2) * block] for piece in pieces], axis=0)
        for f in range(0, f_blocks, 2):
            rows = turned[f * block : (f + 2) * block, :]
            result = jnp.dot(rows, y, preferred_element_type=F32).astype(BF16)
            for row in range(2):
                for side in range(2):
                    dense[(f + row) * d_blocks + d + side] = result[
                        row * block : (row + 1) * block, side * block : (side + 1) * block
                    ]
    slots.copy.wait()
    total = out.shape[0]

    @pl.loop(0, total, unroll=max(n for n in (1, 2, 4, 8) if total % n == 0))
    def _(s):
        place = jnp.where(s < slots.live, slots.index[0, 0, s], zeros)
        pltpu.make_async_copy(dense.at[place], out.at[s], sem).start()

    pltpu.make_async_copy(out, out, sem).wait()


def down_grads(index, count, pieces, near, far, slots):
    f_blocks, tokens, block = near.shape
    f_blocks = 2 * f_blocks
    d_blocks = pieces[0].shape[1] // block
    blocks = f_blocks * d_blocks + 1
    return pl.pallas_call(
        down_grad_body,
        out_shape=jax.ShapeDtypeStruct((slots, block, block), BF16),
        in_specs=[IN_HBM, SCALARS] + [WHOLE] * (2 + len(pieces)),
        out_specs=IN_HBM,
        scratch_shapes=[
            *Slots.scratch(index),
            pltpu.VMEM((f_blocks * block, tokens), BF16),
            pltpu.VMEM((blocks, block, block), BF16),
            pltpu.SemaphoreType.DMA,
        ],
        compiler_params=params(VMEM_LIMIT + 2 * blocks * block * block),
        cost_estimate=cost(2 * slots * block * block * tokens, 2 * slots * block * block),
        name="down_grads",
    )(in_hbm(index), count, near, far, *pieces)


def on_device(
    tokens, cotangent, gate_vals, up_vals, gu_index, gu_count, down_vals, down_index, down_count
):
    block = gate_vals.shape[-1]
    slots = gate_vals.shape[2]
    wide = lax.axis_size("wide")
    narrow = lax.axis_size("narrow")
    chips = wide // 2
    rows = tokens.shape[0]
    d_blocks = tokens.shape[1] // block
    f_blocks = FF // (block * wide)

    def exchange(array):
        return [swap(array, "narrow", narrow, k) for k in range(1, narrow)]

    flips = [chips >> hop for hop in range(1, chips.bit_length())]
    vals = (gate_vals, up_vals)
    x, y, index = tokens, cotangent, gu_index
    weights = []
    for hop, flip in enumerate(flips):
        if hop > 0:
            x = jnp.concatenate([x, x_recv], axis=0)
            y = jnp.concatenate([y, y_recv], axis=0)
            x, weights, index = lax.optimization_barrier((x, weights, index))
        x_recv = swap(x, "wide", wide, 2 * flip)
        if hop < 2:
            early = (down_count,) if hop == 1 else ()
            weights.append(fill(index, gu_count, vals[hop], d_blocks, f_blocks, early))
        if hop < len(flips) - 1:
            y, _ = lax.optimization_barrier((y, x_recv))
            y_recv = swap(y, "wide", wide, 2 * flip)
    index, _ = lax.optimization_barrier((down_index, x))
    down_w = fill(index, down_count, down_vals, f_blocks, d_blocks)
    x, down_w = lax.optimization_barrier((x, down_w))
    x_pieces = [x, x_recv, swap(x, "wide", wide, 1), swap(x_recv, "wide", wide, 1)]

    near_own, near_send = gate_up(x_pieces, *weights, 0)
    near_recv = exchange(near_send)
    late, y, _ = lax.optimization_barrier((x_pieces, y, near_send))
    y_recv = swap(y, "wide", wide, 2 * flips[-1])
    far_own, far_send = gate_up(late, *weights, 1)
    far_recv = exchange(far_send)
    late, _ = lax.optimization_barrier((x_pieces, far_send))
    turned = turn(late, block)
    near_hidden, near_coef = activate(near_own, near_recv)
    y = jnp.concatenate([y, y_recv], axis=0)
    y, turned, near_hidden = lax.optimization_barrier((y, turned, near_hidden))
    y_pieces = [y, swap(y, "wide", wide, 1)]
    dh_own, dh_send = d_hidden(y_pieces, down_w)
    dh_recv = exchange(dh_send)
    far_hidden, far_coef = activate(far_own, far_recv)
    down_grad = down_grads(down_index, down_count, y_pieces, near_hidden, far_hidden, slots)
    down_grad, far_coef = lax.optimization_barrier((down_grad, far_coef))
    own, send, d_pair = d_tokens_part((near_coef, far_coef), dh_own, dh_recv, *weights)

    own = own + swap(send, "wide", wide, 1).astype(F32)
    kept = own.shape[0] // 2
    far = own[kept:].astype(BF16)
    own = own[:kept]
    cut = slots * 2 // 3 if slots % 3 == 0 else slots
    far, d_pair = lax.optimization_barrier((far, d_pair))
    grads = gu_grads(gu_index, gu_count, d_pair, turned, slots, 0, cut, ())
    own = own + swap(far, "wide", wide, 2 * flips[-1]).astype(F32)
    sends = [own[p * rows : (p + 1) * rows].astype(BF16) for p in range(1, chips // 2)]
    if cut < slots:
        sends, d_pair, grads = lax.optimization_barrier((sends, d_pair, grads))
        grads = gu_grads(gu_index, gu_count, d_pair, turned, slots, cut, slots, grads)
    own = own[:rows]
    for p, part in enumerate(sends, 1):
        flip = sum(flips[bit] for bit in range(len(flips)) if p >> bit & 1)
        own = own + swap(part, "wide", wide, 2 * flip).astype(F32)
    gate_grad, up_grad = grads
    return (
        own.astype(BF16),
        gate_grad[None, None],
        up_grad[None, None],
        down_grad[None, None],
    )


def solution(mesh):
    in_specs = (
        P("wide", "narrow"),
        P("wide", "narrow"),
        P("narrow", "wide", None, None, None),
        P("narrow", "wide", None, None, None),
        P("narrow", "wide", None),
        P("narrow", "wide"),
        P("wide", "narrow", None, None, None),
        P("wide", "narrow", None),
        P("wide", "narrow"),
    )
    out_specs = (
        P("wide", "narrow"),
        P("narrow", "wide", None, None, None),
        P("narrow", "wide", None, None, None),
        P("wide", "narrow", None, None, None),
    )
    return jax.shard_map(
        on_device, mesh=mesh, in_specs=in_specs, out_specs=out_specs, check_vma=False
    )
```

```python
import functools
import math

import jax
import jax.numpy as jnp
from jax import lax
from jax.experimental import pallas as pl
from jax.experimental.pallas import tpu as pltpu
from jax.sharding import PartitionSpec as P

FF = 16384
F32 = jnp.float32
BF16 = jnp.bfloat16
VMEM_LIMIT = 8 * 1024 * 1024

WHOLE = pl.BlockSpec(memory_space=pltpu.VMEM)
SCALARS = pl.BlockSpec(memory_space=pltpu.SMEM)
IN_HBM = pl.BlockSpec(memory_space=pltpu.HBM)


def params(vmem=VMEM_LIMIT):
    return pltpu.CompilerParams(vmem_limit_bytes=vmem)


def cost(flops, bytes_accessed):
    return pl.CostEstimate(flops=int(flops), bytes_accessed=int(bytes_accessed), transcendentals=0)


def resident(array):
    return pltpu.with_memory_space_constraint(array, pltpu.VMEM)


def in_hbm(array):
    return pltpu.with_memory_space_constraint(array, pltpu.HBM)


def swap(array, axis, size, flip):
    return lax.ppermute(array, axis, [(i, i ^ flip) for i in range(size)])


def split_index(number, size):
    if size & (size - 1):
        return number // size, number % size
    return number >> (size.bit_length() - 1), number & (size - 1)


class Slots:
    def __init__(self, index_from, count, index, sem):
        self.copy = pltpu.make_async_copy(index_from, index, sem)
        self.index, self.live = index, count[0, 0]

    @staticmethod
    def scratch(index):
        return [pltpu.SMEM(index.shape, index.dtype), pltpu.SemaphoreType.DMA]

    def place(self, slot, size):
        return split_index(self.index[0, 0, slot], size)


def fill_body(index, count, source, *refs):
    target, index_here, slots_sem, sem = refs[-4:]
    slots = Slots(index, count, index_here, slots_sem)
    slots.copy.start()
    outer, inner = target.shape[:2]
    chunk = min(inner, 8)

    @pl.loop(0, outer)
    def _(high):
        target[high] = jnp.zeros(target.shape[1:], target.dtype)

    slots.copy.wait()

    @pl.loop(0, slots.live)
    def _(s):
        high, low = slots.place(s, inner)
        pltpu.make_async_copy(source.at[0, 0, s], target.at[high, low], sem).start()

    many, few = split_index(slots.live, chunk)

    @pl.loop(0, many)
    def _(_):
        blocks = pl.ds(0, chunk)
        pltpu.make_async_copy(source.at[0, 0, blocks], target.at[0, blocks], sem).wait()

    @pl.loop(0, few)
    def _(_):
        pltpu.make_async_copy(source.at[0, 0, 0], target.at[0, 0], sem).wait()


def fill(index, count, slots, outer, inner, early=()):
    block = slots.shape[-1]
    return pl.pallas_call(
        fill_body,
        out_shape=pltpu.VMEM((outer, inner, block, block), BF16),
        in_specs=[IN_HBM, SCALARS, IN_HBM] + [SCALARS] * len(early),
        out_specs=WHOLE,
        scratch_shapes=[*Slots.scratch(index), pltpu.SemaphoreType.DMA],
        compiler_params=params(),
        cost_estimate=cost(0, slots.size * 2),
        name="fill",
    )(in_hbm(index), count, in_hbm(slots), *early)


def stack(pieces):
    return jnp.concatenate([piece[...] for piece in pieces], axis=0)


def gate_up_body(first, *refs):
    *pieces, gate_w, up_w, own, send = refs
    d_blocks, _, block, _ = gate_w.shape
    x = stack(pieces)
    for c in range(own.shape[0]):
        weights = jnp.concatenate(
            [
                gate_w[:, first + c].reshape(d_blocks * block, block),
                up_w[:, first + c].reshape(d_blocks * block, block),
            ],
            axis=1,
        )
        result = jnp.dot(x, weights, preferred_element_type=F32)
        own[c] = result
        send[c] = result.astype(BF16)


def gate_up(pieces, gate_w, up_w, half):
    d_blocks, f_blocks, block, _ = gate_w.shape
    tokens = sum(piece.shape[0] for piece in pieces)
    shape = (f_blocks // 2, tokens, 2 * block)
    return pl.pallas_call(
        functools.partial(gate_up_body, half * f_blocks // 2),
        out_shape=(jax.ShapeDtypeStruct(shape, F32), jax.ShapeDtypeStruct(shape, BF16)),
        in_specs=[WHOLE] * (len(pieces) + 2),
        out_specs=(WHOLE,) * 2,
        compiler_params=params(),
        cost_estimate=cost(2 * tokens * gate_w.size, 2 * gate_w.size),
        name="gate_up",
    )(*pieces, resident(gate_w), resident(up_w))


def d_hidden_body(group, pieces_count, *refs):
    y_pieces, x_pieces = refs[:pieces_count], refs[pieces_count : 2 * pieces_count]
    down_w, own, send, x_turned, y_turned = refs[2 * pieces_count :]
    f_blocks, d_blocks, block, _ = down_w.shape
    for d in range(d_blocks):
        at = slice(d * block, (d + 1) * block)
        y_turned[at, :] = jnp.concatenate([piece[:, at] for piece in y_pieces], axis=0).T
    y = y_turned[...]
    for f in range(0, f_blocks, group):
        weights = jnp.concatenate(
            [
                down_w[f : f + group, d].reshape(group * block, block)
                for d in range(d_blocks)
            ],
            axis=1,
        )
        result = jnp.dot(weights, y, preferred_element_type=F32).T
        for side in range(group):
            part = result[:, side * block : (side + 1) * block]
            own[f + side] = part
            send[f + side] = part.astype(BF16)
    for d in range(d_blocks):
        at = slice(d * block, (d + 1) * block)
        x_turned[d] = jnp.concatenate([piece[:, at] for piece in x_pieces], axis=0).T


def d_hidden(y_pieces, x_pieces, down_w):
    f_blocks, d_blocks, block, _ = down_w.shape
    tokens = sum(piece.shape[0] for piece in y_pieces)
    shape = (f_blocks, tokens, block)
    group = max(n for n in (1, 2, 4) if f_blocks % n == 0)
    return pl.pallas_call(
        functools.partial(d_hidden_body, group, len(y_pieces)),
        out_shape=(
            jax.ShapeDtypeStruct(shape, F32),
            jax.ShapeDtypeStruct(shape, BF16),
            jax.ShapeDtypeStruct((d_blocks, block, tokens), BF16),
        ),
        in_specs=[WHOLE] * (2 * len(y_pieces) + 1),
        out_specs=(WHOLE,) * 3,
        scratch_shapes=[pltpu.VMEM((d_blocks * block, tokens), BF16)],
        compiler_params=params(),
        cost_estimate=cost(2 * tokens * down_w.size, 2 * down_w.size),
        name="d_hidden",
    )(*y_pieces, *x_pieces, resident(down_w))


def d_tokens_body(group, *refs):
    *coef, dh_own = refs[:3]
    *dh_recv, gate_w, up_w, own, send, d_pair, turned = refs[3:]
    d_blocks, f_blocks, block, _ = gate_w.shape
    half = own.shape[0]
    for c in range(f_blocks):
        dh = dh_own[c]
        for part in dh_recv:
            dh = dh + part[c].astype(F32)
        side, at = divmod(c, f_blocks // 2)
        both = (jnp.concatenate([dh, dh], axis=1) * coef[side][at]).astype(BF16)
        d_pair[c] = both
        for side in range(2):
            turned[pl.ds((2 * c + side) * block, block), :] = both[
                :, side * block : (side + 1) * block
            ].T
    grads = turned[...]

    for at in range(d_blocks // group):
        weights = jnp.concatenate(
            [
                ref[at * group : (at + 1) * group, c].reshape(group * block, block)
                for c in range(f_blocks)
                for ref in (gate_w, up_w)
            ],
            axis=1,
        )
        result = jnp.dot(weights, grads, preferred_element_type=F32).T
        columns = slice(at * group * block, (at + 1) * group * block)
        own[:, columns] = result[:half]
        send[:, columns] = result[half:].astype(BF16)


def d_tokens_part(coef, dh_own, dh_recv, gate_w, up_w):
    d_blocks, f_blocks, block, _ = gate_w.shape
    tokens = dh_own.shape[1]
    width = d_blocks * block
    group = max(n for n in (1, 2, 4) if d_blocks % n == 0)
    return pl.pallas_call(
        functools.partial(d_tokens_body, group),
        out_shape=(
            jax.ShapeDtypeStruct((tokens // 2, width), F32),
            jax.ShapeDtypeStruct((tokens // 2, width), BF16),
            jax.ShapeDtypeStruct((f_blocks, tokens, 2 * block), BF16),
        ),
        in_specs=[WHOLE] * (5 + len(dh_recv)),
        out_specs=(WHOLE,) * 3,
        scratch_shapes=[pltpu.VMEM((f_blocks * 2 * block, tokens), BF16)],
        compiler_params=params(),
        cost_estimate=cost(4 * tokens * gate_w.size, 4 * gate_w.size),
        name="d_tokens",
    )(*coef, dh_own, *dh_recv, resident(gate_w), resident(up_w))


def step_slots(slots):
    return max(n for n in range(1, 17) if slots % n == 0)


def gu_grad_body(first, given, index, count, d_pair, turned, *refs):
    gate_out, up_out, *scalars = refs[given:]
    slots = Slots(index, count, *scalars)
    f_blocks = d_pair.shape[0]
    block = turned.shape[1]
    step = pl.program_id(0)

    @pl.when(step == 0)
    def _():
        slots.copy.start()
        slots.copy.wait()

    for j in range(gate_out.shape[0]):
        slot = (step + first) * gate_out.shape[0] + j
        d, f = slots.place(slot, f_blocks)
        result = jnp.dot(turned[d], d_pair[f], preferred_element_type=F32)
        result = jnp.where(slot < slots.live, result, 0.0).astype(BF16)
        gate_out[j] = result[:, :block]
        up_out[j] = result[:, block:]


def gu_grads(index, count, d_pair, turned, total, begin, end, before):
    block, tokens = turned.shape[1:]
    chunk = step_slots(math.gcd(begin, end))
    first = begin // chunk
    shape = jax.ShapeDtypeStruct((total, block, block), BF16)
    out = pl.BlockSpec((chunk, block, block), lambda i: (i + first, 0, 0))
    size = (end - begin) * block * block
    return pl.pallas_call(
        functools.partial(gu_grad_body, first, len(before)),
        out_shape=(shape,) * 2,
        grid=((end - begin) // chunk,),
        in_specs=[IN_HBM, SCALARS] + [WHOLE] * 2 + [pl.BlockSpec(memory_space=pl.ANY)] * len(before),
        out_specs=(out,) * 2,
        scratch_shapes=Slots.scratch(index),
        input_output_aliases={4 + at: at for at in range(len(before))},
        compiler_params=params(),
        cost_estimate=cost(4 * size * tokens, 4 * size),
        name="gu_grads",
    )(in_hbm(index), count, d_pair, turned, *before)


def activate_body(*refs):
    own, *recv, hidden, coef = refs
    block = hidden.shape[2]
    for f in range(hidden.shape[0]):
        both = own[f]
        for part in recv:
            both = both + part[f].astype(F32)
        gate, up = both[:, :block], both[:, block:]
        sig = jax.nn.sigmoid(gate)
        silu = gate * sig
        hidden[f] = (silu * up).astype(BF16)
        coef[f, :, :block] = up * sig * (1.0 + gate * (1.0 - sig))
        coef[f, :, block:] = silu


def activate(own, recv):
    f_blocks, tokens, pair = own.shape
    return pl.pallas_call(
        activate_body,
        out_shape=(
            jax.ShapeDtypeStruct((f_blocks, tokens, pair // 2), BF16),
            jax.ShapeDtypeStruct(own.shape, F32),
        ),
        in_specs=[WHOLE] * (1 + len(recv)),
        out_specs=(WHOLE,) * 2,
        compiler_params=params(),
        cost_estimate=cost(20 * own.size, 8 * own.size),
        name="activate",
    )(own, *recv)


def down_grad_body(index, count, near, far, *refs):
    *pieces, out, index_here, slots_sem, turned, dense, sem = refs
    slots = Slots(index, count, index_here, slots_sem)
    slots.copy.start()
    block = dense.shape[1]
    f_blocks = turned.shape[0] // block
    d_blocks = (dense.shape[0] - 1) // f_blocks
    zeros = f_blocks * d_blocks
    dense[zeros] = jnp.zeros(dense.shape[1:], dense.dtype)
    for f in range(f_blocks):
        half = (near, far)[f * 2 // f_blocks]
        turned[f * block : (f + 1) * block, :] = half[f % (f_blocks // 2)].T
    for d in range(0, d_blocks, 2):
        y = jnp.concatenate([piece[:, d * block : (d + 2) * block] for piece in pieces], axis=0)
        for f in range(0, f_blocks, 2):
            rows = turned[f * block : (f + 2) * block, :]
            result = jnp.dot(rows, y, preferred_element_type=F32).astype(BF16)
            for row in range(2):
                for side in range(2):
                    dense[(f + row) * d_blocks + d + side] = result[
                        row * block : (row + 1) * block, side * block : (side + 1) * block
                    ]
    slots.copy.wait()
    total = out.shape[0]

    @pl.loop(0, total, unroll=max(n for n in (1, 2, 4, 8) if total % n == 0))
    def _(s):
        place = jnp.where(s < slots.live, slots.index[0, 0, s], zeros)
        pltpu.make_async_copy(dense.at[place], out.at[s], sem).start()

    pltpu.make_async_copy(out, out, sem).wait()


def down_grads(index, count, pieces, near, far, slots):
    f_blocks, tokens, block = near.shape
    f_blocks = 2 * f_blocks
    d_blocks = pieces[0].shape[1] // block
    blocks = f_blocks * d_blocks + 1
    return pl.pallas_call(
        down_grad_body,
        out_shape=jax.ShapeDtypeStruct((slots, block, block), BF16),
        in_specs=[IN_HBM, SCALARS] + [WHOLE] * (2 + len(pieces)),
        out_specs=IN_HBM,
        scratch_shapes=[
            *Slots.scratch(index),
            pltpu.VMEM((f_blocks * block, tokens), BF16),
            pltpu.VMEM((blocks, block, block), BF16),
            pltpu.SemaphoreType.DMA,
        ],
        compiler_params=params(VMEM_LIMIT + 2 * blocks * block * block),
        cost_estimate=cost(2 * slots * block * block * tokens, 2 * slots * block * block),
        name="down_grads",
    )(in_hbm(index), count, near, far, *pieces)


def on_device(
    tokens, cotangent, gate_vals, up_vals, gu_index, gu_count, down_vals, down_index, down_count
):
    block = gate_vals.shape[-1]
    slots = gate_vals.shape[2]
    wide = lax.axis_size("wide")
    narrow = lax.axis_size("narrow")
    chips = wide // 2
    rows = tokens.shape[0]
    d_blocks = tokens.shape[1] // block
    f_blocks = FF // (block * wide)

    def exchange(array):
        return [swap(array, "narrow", narrow, k) for k in range(1, narrow)]

    flips = [chips >> hop for hop in range(1, chips.bit_length())]
    vals = (gate_vals, up_vals)
    x, index = tokens, gu_index
    weights = []
    for hop, flip in enumerate(flips):
        if hop > 0:
            x = jnp.concatenate([x, x_recv], axis=0)
            x, weights, index = lax.optimization_barrier((x, weights, index))
        x_recv = swap(x, "wide", wide, 2 * flip)
        if hop < 2:
            early = (down_count,) if hop == 0 else ()
            weights.append(fill(index, gu_count, vals[hop], d_blocks, f_blocks, early))
    y, index, _ = lax.optimization_barrier((cotangent, down_index, x))
    down_w = fill(index, down_count, down_vals, f_blocks, d_blocks)
    for flip in flips[:-1]:
        y = jnp.concatenate([y, swap(y, "wide", wide, 2 * flip)], axis=0)
        y, down_w = lax.optimization_barrier((y, down_w))
    x_pieces = [x, x_recv, swap(x, "wide", wide, 1), swap(x_recv, "wide", wide, 1)]
    y, _ = lax.optimization_barrier((y, x_recv))
    y_recv = swap(y, "wide", wide, 2 * flips[-1])

    near_own, near_send = gate_up(x_pieces, *weights, 0)
    near_recv = exchange(near_send)
    late, _ = lax.optimization_barrier((x, near_send))
    far_own, far_send = gate_up([late, *x_pieces[1:]], *weights, 1)
    far_recv = exchange(far_send)
    y, y_recv, _ = lax.optimization_barrier((y, y_recv, far_send))
    y_pieces = [y, y_recv, swap(y, "wide", wide, 1), swap(y_recv, "wide", wide, 1)]
    near_hidden, near_coef = activate(near_own, near_recv)
    down_w, near_hidden = lax.optimization_barrier((down_w, near_hidden))
    dh_own, dh_send, turned = d_hidden(y_pieces, x_pieces, down_w)
    dh_recv = exchange(dh_send)
    far_hidden, far_coef = activate(far_own, far_recv)
    down_grad = down_grads(down_index, down_count, y_pieces, near_hidden, far_hidden, slots)
    down_grad, far_coef = lax.optimization_barrier((down_grad, far_coef))
    own, send, d_pair = d_tokens_part((near_coef, far_coef), dh_own, dh_recv, *weights)

    own = own + swap(send, "wide", wide, 1).astype(F32)
    kept = own.shape[0] // 2
    far = own[kept:].astype(BF16)
    own = own[:kept]
    cut = slots * 2 // 3 if slots % 3 == 0 else slots
    far, d_pair = lax.optimization_barrier((far, d_pair))
    grads = gu_grads(gu_index, gu_count, d_pair, turned, slots, 0, cut, ())
    own = own + swap(far, "wide", wide, 2 * flips[-1]).astype(F32)
    sends = [own[p * rows : (p + 1) * rows].astype(BF16) for p in range(1, chips // 2)]
    if cut < slots:
        sends, d_pair, grads = lax.optimization_barrier((sends, d_pair, grads))
        grads = gu_grads(gu_index, gu_count, d_pair, turned, slots, cut, slots, grads)
    own = own[:rows]
    for p, part in enumerate(sends, 1):
        flip = sum(flips[bit] for bit in range(len(flips)) if p >> bit & 1)
        own = own + swap(part, "wide", wide, 2 * flip).astype(F32)
    gate_grad, up_grad = grads
    return (
        own.astype(BF16),
        gate_grad[None, None],
        up_grad[None, None],
        down_grad[None, None],
    )


def solution(mesh):
    in_specs = (
        P("wide", "narrow"),
        P("wide", "narrow"),
        P("narrow", "wide", None, None, None),
        P("narrow", "wide", None, None, None),
        P("narrow", "wide", None),
        P("narrow", "wide"),
        P("wide", "narrow", None, None, None),
        P("wide", "narrow", None),
        P("wide", "narrow"),
    )
    out_specs = (
        P("wide", "narrow"),
        P("narrow", "wide", None, None, None),
        P("narrow", "wide", None, None, None),
        P("wide", "narrow", None, None, None),
    )
    return jax.shard_map(
        on_device, mesh=mesh, in_specs=in_specs, out_specs=out_specs, check_vma=False
    )
```

```python
import functools
import math

import jax
import jax.numpy as jnp
from jax import lax
from jax.experimental import pallas as pl
from jax.experimental.pallas import tpu as pltpu
from jax.sharding import PartitionSpec as P

FF = 16384
F32 = jnp.float32
BF16 = jnp.bfloat16
VMEM_LIMIT = 8 * 1024 * 1024

WHOLE = pl.BlockSpec(memory_space=pltpu.VMEM)
SCALARS = pl.BlockSpec(memory_space=pltpu.SMEM)
IN_HBM = pl.BlockSpec(memory_space=pltpu.HBM)


def params(vmem=VMEM_LIMIT):
    return pltpu.CompilerParams(vmem_limit_bytes=vmem)


def cost(flops, bytes_accessed):
    return pl.CostEstimate(flops=int(flops), bytes_accessed=int(bytes_accessed), transcendentals=0)


def resident(array):
    return pltpu.with_memory_space_constraint(array, pltpu.VMEM)


def in_hbm(array):
    return pltpu.with_memory_space_constraint(array, pltpu.HBM)


def swap(array, axis, size, flip):
    return lax.ppermute(array, axis, [(i, i ^ flip) for i in range(size)])


def split_index(number, size):
    if size & (size - 1):
        return number // size, number % size
    return number >> (size.bit_length() - 1), number & (size - 1)


class Slots:
    def __init__(self, index_from, count, index, sem):
        self.copy = pltpu.make_async_copy(index_from, index, sem)
        self.index, self.live = index, count[0, 0]

    @staticmethod
    def scratch(index):
        return [pltpu.SMEM(index.shape, index.dtype), pltpu.SemaphoreType.DMA]

    def place(self, slot, size):
        return split_index(self.index[0, 0, slot], size)


def fill_body(index, count, source, *refs):
    target, index_here, slots_sem, sem = refs[-4:]
    slots = Slots(index, count, index_here, slots_sem)
    slots.copy.start()
    outer, inner = target.shape[:2]
    chunk = min(inner, 8)

    @pl.loop(0, outer)
    def _(high):
        target[high] = jnp.zeros(target.shape[1:], target.dtype)

    slots.copy.wait()

    @pl.loop(0, slots.live)
    def _(s):
        high, low = slots.place(s, inner)
        pltpu.make_async_copy(source.at[0, 0, s], target.at[high, low], sem).start()

    many, few = split_index(slots.live, chunk)

    @pl.loop(0, many)
    def _(_):
        blocks = pl.ds(0, chunk)
        pltpu.make_async_copy(source.at[0, 0, blocks], target.at[0, blocks], sem).wait()

    @pl.loop(0, few)
    def _(_):
        pltpu.make_async_copy(source.at[0, 0, 0], target.at[0, 0], sem).wait()


def fill(index, count, slots, outer, inner, early=()):
    block = slots.shape[-1]
    return pl.pallas_call(
        fill_body,
        out_shape=pltpu.VMEM((outer, inner, block, block), BF16),
        in_specs=[IN_HBM, SCALARS, IN_HBM] + [SCALARS] * len(early),
        out_specs=WHOLE,
        scratch_shapes=[*Slots.scratch(index), pltpu.SemaphoreType.DMA],
        compiler_params=params(),
        cost_estimate=cost(0, slots.size * 2),
        name="fill",
    )(in_hbm(index), count, in_hbm(slots), *early)


def stack(pieces):
    return jnp.concatenate([piece[...] for piece in pieces], axis=0)


def gate_up_body(first, *refs):
    *pieces, gate_w, up_w, own, send = refs
    d_blocks, _, block, _ = gate_w.shape
    x = stack(pieces)
    for c in range(own.shape[0]):
        weights = jnp.concatenate(
            [
                gate_w[:, first + c].reshape(d_blocks * block, block),
                up_w[:, first + c].reshape(d_blocks * block, block),
            ],
            axis=1,
        )
        result = jnp.dot(x, weights, preferred_element_type=F32)
        own[c] = result
        send[c] = result.astype(BF16)


def gate_up(pieces, gate_w, up_w, half):
    d_blocks, f_blocks, block, _ = gate_w.shape
    tokens = sum(piece.shape[0] for piece in pieces)
    shape = (f_blocks // 2, tokens, 2 * block)
    return pl.pallas_call(
        functools.partial(gate_up_body, half * f_blocks // 2),
        out_shape=(jax.ShapeDtypeStruct(shape, F32), jax.ShapeDtypeStruct(shape, BF16)),
        in_specs=[WHOLE] * (len(pieces) + 2),
        out_specs=(WHOLE,) * 2,
        compiler_params=params(),
        cost_estimate=cost(2 * tokens * gate_w.size, 2 * gate_w.size),
        name="gate_up",
    )(*pieces, resident(gate_w), resident(up_w))


def d_hidden_body(group, pieces_count, *refs):
    y_pieces, x_pieces = refs[:pieces_count], refs[pieces_count : 2 * pieces_count]
    down_w, own, send, x_turned, y_turned = refs[2 * pieces_count :]
    f_blocks, d_blocks, block, _ = down_w.shape
    for d in range(d_blocks):
        at = slice(d * block, (d + 1) * block)
        y_turned[at, :] = jnp.concatenate([piece[:, at] for piece in y_pieces], axis=0).T
    y = y_turned[...]
    for f in range(0, f_blocks, group):
        weights = jnp.concatenate(
            [
                down_w[f : f + group, d].reshape(group * block, block)
                for d in range(d_blocks)
            ],
            axis=1,
        )
        result = jnp.dot(weights, y, preferred_element_type=F32).T
        for side in range(group):
            part = result[:, side * block : (side + 1) * block]
            own[f + side] = part
            send[f + side] = part.astype(BF16)
    for d in range(d_blocks):
        at = slice(d * block, (d + 1) * block)
        x_turned[d] = jnp.concatenate([piece[:, at] for piece in x_pieces], axis=0).T


def d_hidden(y_pieces, x_pieces, down_w):
    f_blocks, d_blocks, block, _ = down_w.shape
    tokens = sum(piece.shape[0] for piece in y_pieces)
    shape = (f_blocks, tokens, block)
    group = max(n for n in (1, 2, 4) if f_blocks % n == 0)
    return pl.pallas_call(
        functools.partial(d_hidden_body, group, len(y_pieces)),
        out_shape=(
            jax.ShapeDtypeStruct(shape, F32),
            jax.ShapeDtypeStruct(shape, BF16),
            jax.ShapeDtypeStruct((d_blocks, block, tokens), BF16),
        ),
        in_specs=[WHOLE] * (2 * len(y_pieces) + 1),
        out_specs=(WHOLE,) * 3,
        scratch_shapes=[pltpu.VMEM((d_blocks * block, tokens), BF16)],
        compiler_params=params(),
        cost_estimate=cost(2 * tokens * down_w.size, 2 * down_w.size),
        name="d_hidden",
    )(*y_pieces, *x_pieces, resident(down_w))


def d_tokens_columns(group, begin, grads, gate_w, up_w, own, send):
    f_blocks, block = gate_w.shape[1:3]
    half = own.shape[0]
    for at in range(0, own.shape[1] // block, group):
        rows = slice(begin + at, begin + at + group)
        weights = jnp.concatenate(
            [
                ref[rows, c].reshape(group * block, block)
                for c in range(f_blocks)
                for ref in (gate_w, up_w)
            ],
            axis=1,
        )
        result = jnp.dot(weights, grads, preferred_element_type=F32).T
        columns = slice(at * block, (at + group) * block)
        own[:, columns] = result[:half]
        send[:, columns] = result[half:].astype(BF16)


def d_tokens_first_body(group, *refs):
    *coef, dh_own = refs[:3]
    *dh_recv, gate_w, up_w, own, send, d_pair, turned = refs[3:]
    f_blocks, block = gate_w.shape[1:3]
    for c in range(f_blocks):
        dh = dh_own[c]
        for part in dh_recv:
            dh = dh + part[c].astype(F32)
        side, at = divmod(c, f_blocks // 2)
        both = (jnp.concatenate([dh, dh], axis=1) * coef[side][at]).astype(BF16)
        d_pair[c] = both
        for side in range(2):
            turned[pl.ds((2 * c + side) * block, block), :] = both[
                :, side * block : (side + 1) * block
            ].T
    d_tokens_columns(group, 0, turned[...], gate_w, up_w, own, send)


def d_tokens_second_body(group, turned, gate_w, up_w, own, send):
    d_blocks = gate_w.shape[0]
    d_tokens_columns(group, d_blocks // 2, turned[...], gate_w, up_w, own, send)


def d_tokens_parts(coef, dh_own, dh_recv, gate_w, up_w):
    d_blocks, f_blocks, block, _ = gate_w.shape
    tokens = dh_own.shape[1]
    half = (tokens // 2, d_blocks // 2 * block)
    group = max(n for n in (1, 2, 4) if d_blocks // 2 % n == 0)
    halves = (jax.ShapeDtypeStruct(half, F32), jax.ShapeDtypeStruct(half, BF16))
    common = dict(
        compiler_params=params(),
        cost_estimate=cost(2 * tokens * gate_w.size, 2 * gate_w.size),
    )
    weights = resident(gate_w), resident(up_w)
    own, send, d_pair, turned = pl.pallas_call(
        functools.partial(d_tokens_first_body, group),
        out_shape=(
            *halves,
            jax.ShapeDtypeStruct((f_blocks, tokens, 2 * block), BF16),
            jax.ShapeDtypeStruct((f_blocks * 2 * block, tokens), BF16),
        ),
        in_specs=[WHOLE] * (5 + len(dh_recv)),
        out_specs=(WHOLE,) * 4,
        name="d_tokens_first",
        **common,
    )(*coef, dh_own, *dh_recv, *weights)
    second = pl.pallas_call(
        functools.partial(d_tokens_second_body, group),
        out_shape=halves,
        in_specs=[WHOLE] * 3,
        out_specs=(WHOLE,) * 2,
        name="d_tokens_second",
        **common,
    )(turned, *weights)
    return ((own, send), second), d_pair


def step_slots(slots):
    return max(n for n in range(1, 17) if slots % n == 0)


def gu_grad_body(first, given, index, count, d_pair, turned, *refs):
    gate_out, up_out, *scalars = refs[given:]
    slots = Slots(index, count, *scalars)
    f_blocks = d_pair.shape[0]
    block = turned.shape[1]
    step = pl.program_id(0)

    @pl.when(step == 0)
    def _():
        slots.copy.start()
        slots.copy.wait()

    for j in range(gate_out.shape[0]):
        slot = (step + first) * gate_out.shape[0] + j
        d, f = slots.place(slot, f_blocks)
        result = jnp.dot(turned[d], d_pair[f], preferred_element_type=F32)
        result = jnp.where(slot < slots.live, result, 0.0).astype(BF16)
        gate_out[j] = result[:, :block]
        up_out[j] = result[:, block:]


def gu_grads(index, count, d_pair, turned, total, begin, end, before):
    block, tokens = turned.shape[1:]
    chunk = step_slots(math.gcd(begin, end))
    first = begin // chunk
    shape = jax.ShapeDtypeStruct((total, block, block), BF16)
    out = pl.BlockSpec((chunk, block, block), lambda i: (i + first, 0, 0))
    size = (end - begin) * block * block
    return pl.pallas_call(
        functools.partial(gu_grad_body, first, len(before)),
        out_shape=(shape,) * 2,
        grid=((end - begin) // chunk,),
        in_specs=[IN_HBM, SCALARS] + [WHOLE] * 2 + [pl.BlockSpec(memory_space=pl.ANY)] * len(before),
        out_specs=(out,) * 2,
        scratch_shapes=Slots.scratch(index),
        input_output_aliases={4 + at: at for at in range(len(before))},
        compiler_params=params(),
        cost_estimate=cost(4 * size * tokens, 4 * size),
        name="gu_grads",
    )(in_hbm(index), count, d_pair, turned, *before)


def activate_body(*refs):
    own, *recv, hidden, coef = refs
    block = hidden.shape[2]
    for f in range(hidden.shape[0]):
        both = own[f]
        for part in recv:
            both = both + part[f].astype(F32)
        gate, up = both[:, :block], both[:, block:]
        sig = jax.nn.sigmoid(gate)
        silu = gate * sig
        hidden[f] = (silu * up).astype(BF16)
        coef[f, :, :block] = up * sig * (1.0 + gate * (1.0 - sig))
        coef[f, :, block:] = silu


def activate(own, recv):
    f_blocks, tokens, pair = own.shape
    return pl.pallas_call(
        activate_body,
        out_shape=(
            jax.ShapeDtypeStruct((f_blocks, tokens, pair // 2), BF16),
            jax.ShapeDtypeStruct(own.shape, F32),
        ),
        in_specs=[WHOLE] * (1 + len(recv)),
        out_specs=(WHOLE,) * 2,
        compiler_params=params(),
        cost_estimate=cost(20 * own.size, 8 * own.size),
        name="activate",
    )(own, *recv)


def down_grad_body(index, count, near, far, *refs):
    *pieces, out, index_here, slots_sem, turned, dense, sem = refs
    slots = Slots(index, count, index_here, slots_sem)
    slots.copy.start()
    block = dense.shape[1]
    f_blocks = turned.shape[0] // block
    d_blocks = (dense.shape[0] - 1) // f_blocks
    zeros = f_blocks * d_blocks
    dense[zeros] = jnp.zeros(dense.shape[1:], dense.dtype)
    for f in range(f_blocks):
        half = (near, far)[f * 2 // f_blocks]
        turned[f * block : (f + 1) * block, :] = half[f % (f_blocks // 2)].T
    for d in range(0, d_blocks, 2):
        y = jnp.concatenate([piece[:, d * block : (d + 2) * block] for piece in pieces], axis=0)
        for f in range(0, f_blocks, 2):
            rows = turned[f * block : (f + 2) * block, :]
            result = jnp.dot(rows, y, preferred_element_type=F32).astype(BF16)
            for row in range(2):
                for side in range(2):
                    dense[(f + row) * d_blocks + d + side] = result[
                        row * block : (row + 1) * block, side * block : (side + 1) * block
                    ]
    slots.copy.wait()
    total = out.shape[0]

    @pl.loop(0, total, unroll=max(n for n in (1, 2, 4, 8) if total % n == 0))
    def _(s):
        place = jnp.where(s < slots.live, slots.index[0, 0, s], zeros)
        pltpu.make_async_copy(dense.at[place], out.at[s], sem).start()

    pltpu.make_async_copy(out, out, sem).wait()


def down_grads(index, count, pieces, near, far, slots):
    f_blocks, tokens, block = near.shape
    f_blocks = 2 * f_blocks
    d_blocks = pieces[0].shape[1] // block
    blocks = f_blocks * d_blocks + 1
    return pl.pallas_call(
        down_grad_body,
        out_shape=jax.ShapeDtypeStruct((slots, block, block), BF16),
        in_specs=[IN_HBM, SCALARS] + [WHOLE] * (2 + len(pieces)),
        out_specs=IN_HBM,
        scratch_shapes=[
            *Slots.scratch(index),
            pltpu.VMEM((f_blocks * block, tokens), BF16),
            pltpu.VMEM((blocks, block, block), BF16),
            pltpu.SemaphoreType.DMA,
        ],
        compiler_params=params(VMEM_LIMIT + 2 * blocks * block * block),
        cost_estimate=cost(2 * slots * block * block * tokens, 2 * slots * block * block),
        name="down_grads",
    )(in_hbm(index), count, near, far, *pieces)


def on_device(
    tokens, cotangent, gate_vals, up_vals, gu_index, gu_count, down_vals, down_index, down_count
):
    block = gate_vals.shape[-1]
    slots = gate_vals.shape[2]
    wide = lax.axis_size("wide")
    narrow = lax.axis_size("narrow")
    chips = wide // 2
    rows = tokens.shape[0]
    d_blocks = tokens.shape[1] // block
    f_blocks = FF // (block * wide)

    def exchange(array):
        return [swap(array, "narrow", narrow, k) for k in range(1, narrow)]

    flips = [chips >> hop for hop in range(1, chips.bit_length())]
    vals = (gate_vals, up_vals)
    x, index = tokens, gu_index
    weights = []
    for hop, flip in enumerate(flips):
        if hop > 0:
            x = jnp.concatenate([x, x_recv], axis=0)
            x, weights, index = lax.optimization_barrier((x, weights, index))
        x_recv = swap(x, "wide", wide, 2 * flip)
        if hop < 2:
            early = (down_count,) if hop == 0 else ()
            weights.append(fill(index, gu_count, vals[hop], d_blocks, f_blocks, early))
    y, index, _ = lax.optimization_barrier((cotangent, down_index, x))
    down_w = fill(index, down_count, down_vals, f_blocks, d_blocks)
    for flip in flips[:-1]:
        y = jnp.concatenate([y, swap(y, "wide", wide, 2 * flip)], axis=0)
        y, down_w = lax.optimization_barrier((y, down_w))
    x_pieces = [x, x_recv, swap(x, "wide", wide, 1), swap(x_recv, "wide", wide, 1)]
    y, _ = lax.optimization_barrier((y, x_recv))
    y_recv = swap(y, "wide", wide, 2 * flips[-1])

    near_own, near_send = gate_up(x_pieces, *weights, 0)
    near_recv = exchange(near_send)
    late, _ = lax.optimization_barrier((x, near_send))
    far_own, far_send = gate_up([late, *x_pieces[1:]], *weights, 1)
    far_recv = exchange(far_send)
    y, y_recv, _ = lax.optimization_barrier((y, y_recv, far_send))
    y_pieces = [y, y_recv, swap(y, "wide", wide, 1), swap(y_recv, "wide", wide, 1)]
    near_hidden, near_coef = activate(near_own, near_recv)
    down_w, near_hidden = lax.optimization_barrier((down_w, near_hidden))
    dh_own, dh_send, turned = d_hidden(y_pieces, x_pieces, down_w)
    dh_recv = exchange(dh_send)
    far_hidden, far_coef = activate(far_own, far_recv)
    down_grad = down_grads(down_index, down_count, y_pieces, near_hidden, far_hidden, slots)
    down_grad, far_coef = lax.optimization_barrier((down_grad, far_coef))
    halves, d_pair = d_tokens_parts((near_coef, far_coef), dh_own, dh_recv, *weights)

    halves = [own + swap(send, "wide", wide, 1).astype(F32) for own, send in halves]
    kept = chips // 2 * rows
    far = [own[kept:].astype(BF16) for own in halves]
    cut = slots // 2 if slots % 2 == 0 else slots
    far[1], d_pair = lax.optimization_barrier((far[1], d_pair))
    grads = gu_grads(gu_index, gu_count, d_pair, turned, slots, 0, cut, ())
    halves = [
        own[:kept] + swap(part, "wide", wide, 2 * flips[-1]).astype(F32)
        for own, part in zip(halves, far)
    ]
    own = jnp.concatenate(halves, axis=1)
    sends = [own[p * rows : (p + 1) * rows].astype(BF16) for p in range(1, chips // 2)]
    if cut < slots:
        sends, d_pair, grads = lax.optimization_barrier((sends, d_pair, grads))
        grads = gu_grads(gu_index, gu_count, d_pair, turned, slots, cut, slots, grads)
    own = own[:rows]
    for p, part in enumerate(sends, 1):
        flip = sum(flips[bit] for bit in range(len(flips)) if p >> bit & 1)
        own = own + swap(part, "wide", wide, 2 * flip).astype(F32)
    gate_grad, up_grad = grads
    return (
        own.astype(BF16),
        gate_grad[None, None],
        up_grad[None, None],
        down_grad[None, None],
    )


def solution(mesh):
    in_specs = (
        P("wide", "narrow"),
        P("wide", "narrow"),
        P("narrow", "wide", None, None, None),
        P("narrow", "wide", None, None, None),
        P("narrow", "wide", None),
        P("narrow", "wide"),
        P("wide", "narrow", None, None, None),
        P("wide", "narrow", None),
        P("wide", "narrow"),
    )
    out_specs = (
        P("wide", "narrow"),
        P("narrow", "wide", None, None, None),
        P("narrow", "wide", None, None, None),
        P("wide", "narrow", None, None, None),
    )
    return jax.shard_map(
        on_device, mesh=mesh, in_specs=in_specs, out_specs=out_specs, check_vma=False
    )
```

```python
import functools
import math

import jax
import jax.numpy as jnp
from jax import lax
from jax.experimental import pallas as pl
from jax.experimental.pallas import tpu as pltpu
from jax.sharding import PartitionSpec as P

FF = 16384
F32 = jnp.float32
BF16 = jnp.bfloat16
VMEM_LIMIT = 8 * 1024 * 1024

WHOLE = pl.BlockSpec(memory_space=pltpu.VMEM)
SCALARS = pl.BlockSpec(memory_space=pltpu.SMEM)
IN_HBM = pl.BlockSpec(memory_space=pltpu.HBM)


def params(vmem=VMEM_LIMIT):
    return pltpu.CompilerParams(vmem_limit_bytes=vmem)


def cost(flops, bytes_accessed):
    return pl.CostEstimate(flops=int(flops), bytes_accessed=int(bytes_accessed), transcendentals=0)


def resident(array):
    return pltpu.with_memory_space_constraint(array, pltpu.VMEM)


def in_hbm(array):
    return pltpu.with_memory_space_constraint(array, pltpu.HBM)


def swap(array, axis, size, flip):
    return lax.ppermute(array, axis, [(i, i ^ flip) for i in range(size)])


def split_index(number, size):
    if size & (size - 1):
        return number // size, number % size
    return number >> (size.bit_length() - 1), number & (size - 1)


class Slots:
    def __init__(self, index_from, count, index, sem):
        self.copy = pltpu.make_async_copy(index_from, index, sem)
        self.index, self.live = index, count[0, 0]

    @staticmethod
    def scratch(index):
        return [pltpu.SMEM(index.shape, index.dtype), pltpu.SemaphoreType.DMA]

    def place(self, slot, size):
        return split_index(self.index[0, 0, slot], size)


def fill_body(index, count, source, *refs):
    target, index_here, slots_sem, sem = refs[-4:]
    slots = Slots(index, count, index_here, slots_sem)
    slots.copy.start()
    outer, inner = target.shape[:2]
    chunk = min(inner, 8)

    @pl.loop(0, outer)
    def _(high):
        target[high] = jnp.zeros(target.shape[1:], target.dtype)

    slots.copy.wait()

    @pl.loop(0, slots.live)
    def _(s):
        high, low = slots.place(s, inner)
        pltpu.make_async_copy(source.at[0, 0, s], target.at[high, low], sem).start()

    many, few = split_index(slots.live, chunk)

    @pl.loop(0, many)
    def _(_):
        blocks = pl.ds(0, chunk)
        pltpu.make_async_copy(source.at[0, 0, blocks], target.at[0, blocks], sem).wait()

    @pl.loop(0, few)
    def _(_):
        pltpu.make_async_copy(source.at[0, 0, 0], target.at[0, 0], sem).wait()


def fill(index, count, slots, outer, inner, early=()):
    block = slots.shape[-1]
    return pl.pallas_call(
        fill_body,
        out_shape=pltpu.VMEM((outer, inner, block, block), BF16),
        in_specs=[IN_HBM, SCALARS, IN_HBM] + [SCALARS] * len(early),
        out_specs=WHOLE,
        scratch_shapes=[*Slots.scratch(index), pltpu.SemaphoreType.DMA],
        compiler_params=params(),
        cost_estimate=cost(0, slots.size * 2),
        name="fill",
    )(in_hbm(index), count, in_hbm(slots), *early)


def stack(pieces):
    return jnp.concatenate([piece[...] for piece in pieces], axis=0)


def gate_up_body(first, *refs):
    *pieces, gate_w, up_w, own, send = refs
    d_blocks, _, block, _ = gate_w.shape
    x = stack(pieces)
    for c in range(own.shape[0]):
        weights = jnp.concatenate(
            [
                gate_w[:, first + c].reshape(d_blocks * block, block),
                up_w[:, first + c].reshape(d_blocks * block, block),
            ],
            axis=1,
        )
        result = jnp.dot(x, weights, preferred_element_type=F32)
        own[c] = result
        send[c] = result.astype(BF16)


def gate_up(pieces, gate_w, up_w, half):
    d_blocks, f_blocks, block, _ = gate_w.shape
    tokens = sum(piece.shape[0] for piece in pieces)
    shape = (f_blocks // 2, tokens, 2 * block)
    return pl.pallas_call(
        functools.partial(gate_up_body, half * f_blocks // 2),
        out_shape=(jax.ShapeDtypeStruct(shape, F32), jax.ShapeDtypeStruct(shape, BF16)),
        in_specs=[WHOLE] * (len(pieces) + 2),
        out_specs=(WHOLE,) * 2,
        compiler_params=params(),
        cost_estimate=cost(2 * tokens * gate_w.size, 2 * gate_w.size),
        name="gate_up",
    )(*pieces, resident(gate_w), resident(up_w))


def d_hidden_body(group, pieces_count, *refs):
    y_pieces, x_pieces = refs[:pieces_count], refs[pieces_count : 2 * pieces_count]
    down_w, own, send, x_turned, y_turned = refs[2 * pieces_count :]
    f_blocks, d_blocks, block, _ = down_w.shape
    for d in range(d_blocks):
        at = slice(d * block, (d + 1) * block)
        y_turned[at, :] = jnp.concatenate([piece[:, at] for piece in y_pieces], axis=0).T
    y = y_turned[...]
    for f in range(0, f_blocks, group):
        weights = jnp.concatenate(
            [
                down_w[f : f + group, d].reshape(group * block, block)
                for d in range(d_blocks)
            ],
            axis=1,
        )
        result = jnp.dot(weights, y, preferred_element_type=F32).T
        for side in range(group):
            part = result[:, side * block : (side + 1) * block]
            own[f + side] = part
            send[f + side] = part.astype(BF16)
    for d in range(d_blocks):
        at = slice(d * block, (d + 1) * block)
        x_turned[d] = jnp.concatenate([piece[:, at] for piece in x_pieces], axis=0).T


def d_hidden(y_pieces, x_pieces, down_w):
    f_blocks, d_blocks, block, _ = down_w.shape
    tokens = sum(piece.shape[0] for piece in y_pieces)
    shape = (f_blocks, tokens, block)
    group = max(n for n in (1, 2, 4) if f_blocks % n == 0)
    return pl.pallas_call(
        functools.partial(d_hidden_body, group, len(y_pieces)),
        out_shape=(
            jax.ShapeDtypeStruct(shape, F32),
            jax.ShapeDtypeStruct(shape, BF16),
            jax.ShapeDtypeStruct((d_blocks, block, tokens), BF16),
        ),
        in_specs=[WHOLE] * (2 * len(y_pieces) + 1),
        out_specs=(WHOLE,) * 3,
        scratch_shapes=[pltpu.VMEM((d_blocks * block, tokens), BF16)],
        compiler_params=params(),
        cost_estimate=cost(2 * tokens * down_w.size, 2 * down_w.size),
        name="d_hidden",
    )(*y_pieces, *x_pieces, resident(down_w))


def d_tokens_columns(group, begin, grads, gate_w, up_w, own, send):
    f_blocks, block = gate_w.shape[1:3]
    half = own.shape[0]
    for at in range(0, own.shape[1] // block, group):
        rows = slice(begin + at, begin + at + group)
        weights = jnp.concatenate(
            [
                ref[rows, c].reshape(group * block, block)
                for c in range(f_blocks)
                for ref in (gate_w, up_w)
            ],
            axis=1,
        )
        result = jnp.dot(weights, grads, preferred_element_type=F32).T
        columns = slice(at * block, (at + group) * block)
        own[:, columns] = result[:half]
        send[:, columns] = result[half:].astype(BF16)


def d_tokens_first_body(group, *refs):
    *coef, dh_own = refs[:3]
    *dh_recv, gate_w, up_w, own, send, d_pair, turned = refs[3:]
    f_blocks, block = gate_w.shape[1:3]
    for c in range(f_blocks):
        dh = dh_own[c]
        for part in dh_recv:
            dh = dh + part[c].astype(F32)
        side, at = divmod(c, f_blocks // 2)
        both = (jnp.concatenate([dh, dh], axis=1) * coef[side][at]).astype(BF16)
        d_pair[c] = both
        for side in range(2):
            turned[pl.ds((2 * c + side) * block, block), :] = both[
                :, side * block : (side + 1) * block
            ].T
    d_tokens_columns(group, 0, turned[...], gate_w, up_w, own, send)


def d_tokens_second_body(group, turned, gate_w, up_w, own, send):
    d_blocks = gate_w.shape[0]
    d_tokens_columns(group, d_blocks // 2, turned[...], gate_w, up_w, own, send)


def d_tokens_parts(coef, dh_own, dh_recv, gate_w, up_w):
    d_blocks, f_blocks, block, _ = gate_w.shape
    tokens = dh_own.shape[1]
    half = (tokens // 2, d_blocks // 2 * block)
    group = max(n for n in (1, 2, 4) if d_blocks // 2 % n == 0)
    halves = (jax.ShapeDtypeStruct(half, F32), jax.ShapeDtypeStruct(half, BF16))
    common = dict(
        compiler_params=params(),
        cost_estimate=cost(2 * tokens * gate_w.size, 2 * gate_w.size),
    )
    weights = resident(gate_w), resident(up_w)
    own, send, d_pair, turned = pl.pallas_call(
        functools.partial(d_tokens_first_body, group),
        out_shape=(
            *halves,
            jax.ShapeDtypeStruct((f_blocks, tokens, 2 * block), BF16),
            jax.ShapeDtypeStruct((f_blocks * 2 * block, tokens), BF16),
        ),
        in_specs=[WHOLE] * (5 + len(dh_recv)),
        out_specs=(WHOLE,) * 4,
        name="d_tokens_first",
        **common,
    )(*coef, dh_own, *dh_recv, *weights)
    second = pl.pallas_call(
        functools.partial(d_tokens_second_body, group),
        out_shape=halves,
        in_specs=[WHOLE] * 3,
        out_specs=(WHOLE,) * 2,
        name="d_tokens_second",
        **common,
    )(turned, *weights)
    return ((own, send), second), d_pair


def step_slots(slots):
    return max(n for n in range(1, 33) if slots % n == 0)


def gu_grad_body(first, given, index, count, d_pair, turned, *refs):
    gate_out, up_out, *scalars = refs[given:]
    slots = Slots(index, count, *scalars)
    f_blocks = d_pair.shape[0]
    block = turned.shape[1]
    step = pl.program_id(0)

    @pl.when(step == 0)
    def _():
        slots.copy.start()
        slots.copy.wait()

    chunk = gate_out.shape[0]
    begin = (step + first) * chunk

    def work(masked):
        for j in range(chunk):
            d, f = slots.place(begin + j, f_blocks)
            result = jnp.dot(turned[d], d_pair[f], preferred_element_type=F32)
            if masked:
                result = jnp.where(begin + j < slots.live, result, 0.0)
            result = result.astype(BF16)
            gate_out[j] = result[:, :block]
            up_out[j] = result[:, block:]

    @pl.when(begin + chunk <= slots.live)
    def _():
        work(False)

    @pl.when(begin + chunk > slots.live)
    def _():
        work(True)


def gu_grads(index, count, d_pair, turned, total, begin, end, before):
    block, tokens = turned.shape[1:]
    chunk = step_slots(math.gcd(begin, end))
    first = begin // chunk
    shape = jax.ShapeDtypeStruct((total, block, block), BF16)
    out = pl.BlockSpec((chunk, block, block), lambda i: (i + first, 0, 0))
    size = (end - begin) * block * block
    return pl.pallas_call(
        functools.partial(gu_grad_body, first, len(before)),
        out_shape=(shape,) * 2,
        grid=((end - begin) // chunk,),
        in_specs=[IN_HBM, SCALARS] + [WHOLE] * 2 + [pl.BlockSpec(memory_space=pl.ANY)] * len(before),
        out_specs=(out,) * 2,
        scratch_shapes=Slots.scratch(index),
        input_output_aliases={4 + at: at for at in range(len(before))},
        compiler_params=params(),
        cost_estimate=cost(4 * size * tokens, 4 * size),
        name="gu_grads",
    )(in_hbm(index), count, d_pair, turned, *before)


def activate_body(*refs):
    own, *recv, hidden, coef = refs
    block = hidden.shape[2]
    for f in range(hidden.shape[0]):
        both = own[f]
        for part in recv:
            both = both + part[f].astype(F32)
        gate, up = both[:, :block], both[:, block:]
        sig = jax.nn.sigmoid(gate)
        silu = gate * sig
        hidden[f] = (silu * up).astype(BF16)
        coef[f, :, :block] = up * sig * (1.0 + gate * (1.0 - sig))
        coef[f, :, block:] = silu


def activate(own, recv):
    f_blocks, tokens, pair = own.shape
    return pl.pallas_call(
        activate_body,
        out_shape=(
            jax.ShapeDtypeStruct((f_blocks, tokens, pair // 2), BF16),
            jax.ShapeDtypeStruct(own.shape, F32),
        ),
        in_specs=[WHOLE] * (1 + len(recv)),
        out_specs=(WHOLE,) * 2,
        compiler_params=params(),
        cost_estimate=cost(20 * own.size, 8 * own.size),
        name="activate",
    )(own, *recv)


def down_blocks(first, hidden, pieces, dense, turned):
    f_blocks, tokens, block = hidden.shape
    d_blocks = pieces[0].shape[1] // block
    group = 2 if f_blocks % 2 == 0 else 1
    for f in range(f_blocks):
        turned[f * block : (f + 1) * block, :] = hidden[f].T
    for d in range(0, d_blocks, 2):
        y = jnp.concatenate([piece[:, d * block : (d + 2) * block] for piece in pieces], axis=0)
        for f in range(0, f_blocks, group):
            rows = turned[f * block : (f + group) * block, :]
            result = jnp.dot(rows, y, preferred_element_type=F32).astype(BF16)
            for row in range(group):
                for side in range(2):
                    dense[(first + f + row) * d_blocks + d + side] = result[
                        row * block : (row + 1) * block, side * block : (side + 1) * block
                    ]


def down_first_body(hidden, *refs):
    *pieces, dense, turned = refs
    dense[dense.shape[0] - 1] = jnp.zeros(dense.shape[1:], dense.dtype)
    down_blocks(0, hidden, pieces, dense, turned)


def down_second_body(first, index, count, hidden, _, *refs):
    *pieces, out, dense, index_here, slots_sem, turned, sem = refs
    slots = Slots(index, count, index_here, slots_sem)
    slots.copy.start()
    down_blocks(first, hidden, pieces, dense, turned)
    slots.copy.wait()
    zeros = dense.shape[0] - 1
    total = out.shape[0]

    @pl.loop(0, total, unroll=max(n for n in (1, 2, 4, 8) if total % n == 0))
    def _(s):
        place = jnp.where(s < slots.live, slots.index[0, 0, s], zeros)
        pltpu.make_async_copy(dense.at[place], out.at[s], sem).start()

    pltpu.make_async_copy(out, out, sem).wait()


def down_first(pieces, hidden, f_blocks):
    _, tokens, block = hidden.shape
    blocks = f_blocks * (pieces[0].shape[1] // block) + 1
    return pl.pallas_call(
        down_first_body,
        out_shape=pltpu.VMEM((blocks, block, block), BF16),
        in_specs=[WHOLE] * (1 + len(pieces)),
        out_specs=WHOLE,
        scratch_shapes=[pltpu.VMEM((hidden.shape[0] * block, tokens), BF16)],
        compiler_params=params(),
        cost_estimate=cost(blocks * block * block * tokens, 2 * blocks * block * block),
        name="down_first",
    )(hidden, *pieces)


def down_second(index, count, pieces, hidden, dense, slots):
    far_blocks, tokens, block = hidden.shape
    d_blocks = pieces[0].shape[1] // block
    first = (dense.shape[0] - 1) // d_blocks - far_blocks
    out, _ = pl.pallas_call(
        functools.partial(down_second_body, first),
        out_shape=(
            jax.ShapeDtypeStruct((slots, block, block), BF16),
            pltpu.VMEM(dense.shape, BF16),
        ),
        in_specs=[IN_HBM, SCALARS] + [WHOLE] * (2 + len(pieces)),
        out_specs=(IN_HBM, WHOLE),
        scratch_shapes=[
            *Slots.scratch(index),
            pltpu.VMEM((far_blocks * block, tokens), BF16),
            pltpu.SemaphoreType.DMA,
        ],
        input_output_aliases={3: 1},
        compiler_params=params(),
        cost_estimate=cost(slots * block * block * tokens, 2 * slots * block * block),
        name="down_second",
    )(in_hbm(index), count, hidden, resident(dense), *pieces)
    return out


def on_device(
    tokens, cotangent, gate_vals, up_vals, gu_index, gu_count, down_vals, down_index, down_count
):
    block = gate_vals.shape[-1]
    slots = gate_vals.shape[2]
    wide = lax.axis_size("wide")
    narrow = lax.axis_size("narrow")
    chips = wide // 2
    rows = tokens.shape[0]
    d_blocks = tokens.shape[1] // block
    f_blocks = FF // (block * wide)

    def exchange(array):
        return [swap(array, "narrow", narrow, k) for k in range(1, narrow)]

    flips = [chips >> hop for hop in range(1, chips.bit_length())]
    vals = (gate_vals, up_vals)
    x, index = tokens, gu_index
    weights = []
    for hop, flip in enumerate(flips):
        if hop > 0:
            x = jnp.concatenate([x, x_recv], axis=0)
            x, weights, index = lax.optimization_barrier((x, weights, index))
        x_recv = swap(x, "wide", wide, 2 * flip)
        if hop < 2:
            early = (down_count,) if hop == 0 else ()
            weights.append(fill(index, gu_count, vals[hop], d_blocks, f_blocks, early))
    y, index, _ = lax.optimization_barrier((cotangent, down_index, x))
    down_w = fill(index, down_count, down_vals, f_blocks, d_blocks)
    for flip in flips[:-1]:
        y = jnp.concatenate([y, swap(y, "wide", wide, 2 * flip)], axis=0)
        y, down_w = lax.optimization_barrier((y, down_w))
    x_pieces = [x, x_recv, swap(x, "wide", wide, 1), swap(x_recv, "wide", wide, 1)]
    y, _ = lax.optimization_barrier((y, x_recv))
    y_recv = swap(y, "wide", wide, 2 * flips[-1])

    near_own, near_send = gate_up(x_pieces, *weights, 0)
    near_recv = exchange(near_send)
    late, _ = lax.optimization_barrier((x, near_send))
    far_own, far_send = gate_up([late, *x_pieces[1:]], *weights, 1)
    far_recv = exchange(far_send)
    y, y_recv, _ = lax.optimization_barrier((y, y_recv, far_send))
    y_pieces = [y, y_recv, swap(y, "wide", wide, 1), swap(y_recv, "wide", wide, 1)]
    near_hidden, near_coef = activate(near_own, near_recv)
    down_w, near_hidden = lax.optimization_barrier((down_w, near_hidden))
    dh_own, dh_send, turned = d_hidden(y_pieces, x_pieces, down_w)
    y_pieces, dh_send = lax.optimization_barrier((y_pieces, dh_send))
    dh_recv = exchange(dh_send)
    dense = down_first(y_pieces, near_hidden, f_blocks)
    far_own, dense = lax.optimization_barrier((far_own, dense))
    far_hidden, far_coef = activate(far_own, far_recv)
    down_grad = down_second(down_index, down_count, y_pieces, far_hidden, dense, slots)
    down_grad, far_coef = lax.optimization_barrier((down_grad, far_coef))
    halves, d_pair = d_tokens_parts((near_coef, far_coef), dh_own, dh_recv, *weights)

    halves = [own + swap(send, "wide", wide, 1).astype(F32) for own, send in halves]
    kept = chips // 2 * rows
    far = [own[kept:].astype(BF16) for own in halves]
    cut = slots // 2 if slots % 2 == 0 else slots
    far[1], d_pair = lax.optimization_barrier((far[1], d_pair))
    grads = gu_grads(gu_index, gu_count, d_pair, turned, slots, 0, cut, ())
    halves = [
        own[:kept] + swap(part, "wide", wide, 2 * flips[-1]).astype(F32)
        for own, part in zip(halves, far)
    ]
    own = jnp.concatenate(halves, axis=1)
    sends = [own[p * rows : (p + 1) * rows].astype(BF16) for p in range(1, chips // 2)]
    if cut < slots:
        sends, d_pair, grads = lax.optimization_barrier((sends, d_pair, grads))
        grads = gu_grads(gu_index, gu_count, d_pair, turned, slots, cut, slots, grads)
    own = own[:rows]
    for p, part in enumerate(sends, 1):
        flip = sum(flips[bit] for bit in range(len(flips)) if p >> bit & 1)
        own = own + swap(part, "wide", wide, 2 * flip).astype(F32)
    gate_grad, up_grad = grads
    return (
        own.astype(BF16),
        gate_grad[None, None],
        up_grad[None, None],
        down_grad[None, None],
    )


def solution(mesh):
    in_specs = (
        P("wide", "narrow"),
        P("wide", "narrow"),
        P("narrow", "wide", None, None, None),
        P("narrow", "wide", None, None, None),
        P("narrow", "wide", None),
        P("narrow", "wide"),
        P("wide", "narrow", None, None, None),
        P("wide", "narrow", None),
        P("wide", "narrow"),
    )
    out_specs = (
        P("wide", "narrow"),
        P("narrow", "wide", None, None, None),
        P("narrow", "wide", None, None, None),
        P("wide", "narrow", None, None, None),
    )
    return jax.shard_map(
        on_device, mesh=mesh, in_specs=in_specs, out_specs=out_specs, check_vma=False
    )
```

```python
import functools
import math

import jax
import jax.numpy as jnp
from jax import lax
from jax.experimental import pallas as pl
from jax.experimental.pallas import tpu as pltpu
from jax.sharding import PartitionSpec as P

FF = 16384
F32 = jnp.float32
BF16 = jnp.bfloat16
VMEM_LIMIT = 8 * 1024 * 1024

WHOLE = pl.BlockSpec(memory_space=pltpu.VMEM)
SCALARS = pl.BlockSpec(memory_space=pltpu.SMEM)
IN_HBM = pl.BlockSpec(memory_space=pltpu.HBM)


def params(vmem=VMEM_LIMIT):
    return pltpu.CompilerParams(vmem_limit_bytes=vmem)


def cost(flops, bytes_accessed):
    return pl.CostEstimate(flops=int(flops), bytes_accessed=int(bytes_accessed), transcendentals=0)


def resident(array):
    return pltpu.with_memory_space_constraint(array, pltpu.VMEM)


def in_hbm(array):
    return pltpu.with_memory_space_constraint(array, pltpu.HBM)


def swap(array, axis, size, flip):
    return lax.ppermute(array, axis, [(i, i ^ flip) for i in range(size)])


def split_index(number, size):
    if size & (size - 1):
        return number // size, number % size
    return number >> (size.bit_length() - 1), number & (size - 1)


class Slots:
    def __init__(self, index_from, count, index, sem):
        self.copy = pltpu.make_async_copy(index_from, index, sem)
        self.index, self.live = index, count[0, 0]

    @staticmethod
    def scratch(index):
        return [pltpu.SMEM(index.shape, index.dtype), pltpu.SemaphoreType.DMA]

    def place(self, slot, size):
        return split_index(self.index[0, 0, slot], size)


def fill_body(index, count, source, *refs):
    target, index_here, slots_sem, sem = refs[-4:]
    slots = Slots(index, count, index_here, slots_sem)
    slots.copy.start()
    outer, inner = target.shape[:2]
    chunk = min(inner, 8)

    @pl.loop(0, outer)
    def _(high):
        target[high] = jnp.zeros(target.shape[1:], target.dtype)

    slots.copy.wait()

    @pl.loop(0, slots.live)
    def _(s):
        high, low = slots.place(s, inner)
        pltpu.make_async_copy(source.at[0, 0, s], target.at[high, low], sem).start()

    many, few = split_index(slots.live, chunk)

    @pl.loop(0, many)
    def _(_):
        blocks = pl.ds(0, chunk)
        pltpu.make_async_copy(source.at[0, 0, blocks], target.at[0, blocks], sem).wait()

    @pl.loop(0, few)
    def _(_):
        pltpu.make_async_copy(source.at[0, 0, 0], target.at[0, 0], sem).wait()


def fill(index, count, slots, outer, inner, early=()):
    block = slots.shape[-1]
    return pl.pallas_call(
        fill_body,
        out_shape=pltpu.VMEM((outer, inner, block, block), BF16),
        in_specs=[IN_HBM, SCALARS, IN_HBM] + [SCALARS] * len(early),
        out_specs=WHOLE,
        scratch_shapes=[*Slots.scratch(index), pltpu.SemaphoreType.DMA],
        compiler_params=params(),
        cost_estimate=cost(0, slots.size * 2),
        name="fill",
    )(in_hbm(index), count, in_hbm(slots), *early)


def stack(pieces):
    return jnp.concatenate([piece[...] for piece in pieces], axis=0)


def gate_up_body(first, *refs):
    *pieces, gate_w, up_w, own, send = refs
    d_blocks, _, block, _ = gate_w.shape
    x = stack(pieces)
    for c in range(own.shape[0]):
        weights = jnp.concatenate(
            [
                gate_w[:, first + c].reshape(d_blocks * block, block),
                up_w[:, first + c].reshape(d_blocks * block, block),
            ],
            axis=1,
        )
        result = jnp.dot(x, weights, preferred_element_type=F32)
        own[c] = result
        send[c] = result.astype(BF16)


def gate_up(pieces, gate_w, up_w, half):
    d_blocks, f_blocks, block, _ = gate_w.shape
    tokens = sum(piece.shape[0] for piece in pieces)
    shape = (f_blocks // 2, tokens, 2 * block)
    return pl.pallas_call(
        functools.partial(gate_up_body, half * f_blocks // 2),
        out_shape=(jax.ShapeDtypeStruct(shape, F32), jax.ShapeDtypeStruct(shape, BF16)),
        in_specs=[WHOLE] * (len(pieces) + 2),
        out_specs=(WHOLE,) * 2,
        compiler_params=params(),
        cost_estimate=cost(2 * tokens * gate_w.size, 2 * gate_w.size),
        name="gate_up",
    )(*pieces, resident(gate_w), resident(up_w))


def d_hidden_body(group, pieces_count, *refs):
    y_pieces, x_pieces = refs[:pieces_count], refs[pieces_count : 2 * pieces_count]
    down_w, own, send, x_turned, y_turned = refs[2 * pieces_count :]
    f_blocks, d_blocks, block, _ = down_w.shape
    for d in range(d_blocks):
        at = slice(d * block, (d + 1) * block)
        y_turned[at, :] = jnp.concatenate([piece[:, at] for piece in y_pieces], axis=0).T
    y = y_turned[...]
    for f in range(0, f_blocks, group):
        weights = jnp.concatenate(
            [
                down_w[f : f + group, d].reshape(group * block, block)
                for d in range(d_blocks)
            ],
            axis=1,
        )
        result = jnp.dot(weights, y, preferred_element_type=F32).T
        for side in range(group):
            part = result[:, side * block : (side + 1) * block]
            own[f + side] = part
            send[f + side] = part.astype(BF16)
    for d in range(d_blocks):
        at = slice(d * block, (d + 1) * block)
        x_turned[d] = jnp.concatenate([piece[:, at] for piece in x_pieces], axis=0).T


def d_hidden(y_pieces, x_pieces, down_w):
    f_blocks, d_blocks, block, _ = down_w.shape
    tokens = sum(piece.shape[0] for piece in y_pieces)
    shape = (f_blocks, tokens, block)
    group = max(n for n in (1, 2, 4) if f_blocks % n == 0)
    return pl.pallas_call(
        functools.partial(d_hidden_body, group, len(y_pieces)),
        out_shape=(
            jax.ShapeDtypeStruct(shape, F32),
            jax.ShapeDtypeStruct(shape, BF16),
            jax.ShapeDtypeStruct((d_blocks, block, tokens), BF16),
        ),
        in_specs=[WHOLE] * (2 * len(y_pieces) + 1),
        out_specs=(WHOLE,) * 3,
        scratch_shapes=[pltpu.VMEM((d_blocks * block, tokens), BF16)],
        compiler_params=params(),
        cost_estimate=cost(2 * tokens * down_w.size, 2 * down_w.size),
        name="d_hidden",
    )(*y_pieces, *x_pieces, resident(down_w))


def d_tokens_columns(group, begin, grads, gate_w, up_w, own, send):
    f_blocks, block = gate_w.shape[1:3]
    half = own.shape[0]
    for at in range(0, own.shape[1] // block, group):
        rows = slice(begin + at, begin + at + group)
        weights = jnp.concatenate(
            [
                ref[rows, c].reshape(group * block, block)
                for c in range(f_blocks)
                for ref in (gate_w, up_w)
            ],
            axis=1,
        )
        result = jnp.dot(weights, grads, preferred_element_type=F32).T
        columns = slice(at * block, (at + group) * block)
        own[:, columns] = result[:half]
        send[:, columns] = result[half:].astype(BF16)


def d_tokens_first_body(group, *refs):
    *coef, dh_own = refs[:3]
    *dh_recv, gate_w, up_w, own, send, d_pair, turned = refs[3:]
    f_blocks, block = gate_w.shape[1:3]
    for c in range(f_blocks):
        dh = dh_own[c]
        for part in dh_recv:
            dh = dh + part[c].astype(F32)
        side, at = divmod(c, f_blocks // 2)
        both = (jnp.concatenate([dh, dh], axis=1) * coef[side][at]).astype(BF16)
        d_pair[c] = both
        for side in range(2):
            turned[pl.ds((2 * c + side) * block, block), :] = both[
                :, side * block : (side + 1) * block
            ].T
    d_tokens_columns(group, 0, turned[...], gate_w, up_w, own, send)


def d_tokens_second_body(group, turned, gate_w, up_w, own, send):
    d_blocks = gate_w.shape[0]
    d_tokens_columns(group, d_blocks // 2, turned[...], gate_w, up_w, own, send)


def d_tokens_parts(coef, dh_own, dh_recv, gate_w, up_w):
    d_blocks, f_blocks, block, _ = gate_w.shape
    tokens = dh_own.shape[1]
    half = (tokens // 2, d_blocks // 2 * block)
    group = max(n for n in (1, 2, 4) if d_blocks // 2 % n == 0)
    halves = (jax.ShapeDtypeStruct(half, F32), jax.ShapeDtypeStruct(half, BF16))
    common = dict(
        compiler_params=params(),
        cost_estimate=cost(2 * tokens * gate_w.size, 2 * gate_w.size),
    )
    weights = resident(gate_w), resident(up_w)
    own, send, d_pair, turned = pl.pallas_call(
        functools.partial(d_tokens_first_body, group),
        out_shape=(
            *halves,
            jax.ShapeDtypeStruct((f_blocks, tokens, 2 * block), BF16),
            jax.ShapeDtypeStruct((f_blocks * 2 * block, tokens), BF16),
        ),
        in_specs=[WHOLE] * (5 + len(dh_recv)),
        out_specs=(WHOLE,) * 4,
        name="d_tokens_first",
        **common,
    )(*coef, dh_own, *dh_recv, *weights)
    second = pl.pallas_call(
        functools.partial(d_tokens_second_body, group),
        out_shape=halves,
        in_specs=[WHOLE] * 3,
        out_specs=(WHOLE,) * 2,
        name="d_tokens_second",
        **common,
    )(turned, *weights)
    return ((own, send), second), d_pair


def step_slots(slots):
    return max(n for n in range(1, 33) if slots % n == 0)


def gu_grad_body(first, given, index, count, d_pair, turned, *refs):
    gate_out, up_out, *scalars = refs[given:]
    slots = Slots(index, count, *scalars)
    f_blocks = d_pair.shape[0]
    block = turned.shape[1]
    step = pl.program_id(0)

    @pl.when(step == 0)
    def _():
        slots.copy.start()
        slots.copy.wait()

    chunk = gate_out.shape[0]
    begin = (step + first) * chunk

    def work(masked):
        for j in range(chunk):
            d, f = slots.place(begin + j, f_blocks)
            result = jnp.dot(turned[d], d_pair[f], preferred_element_type=F32)
            if masked:
                result = jnp.where(begin + j < slots.live, result, 0.0)
            result = result.astype(BF16)
            gate_out[j] = result[:, :block]
            up_out[j] = result[:, block:]

    @pl.when(begin + chunk <= slots.live)
    def _():
        work(False)

    @pl.when(begin + chunk > slots.live)
    def _():
        work(True)


def gu_grads(index, count, d_pair, turned, total, begin, end, before):
    block, tokens = turned.shape[1:]
    chunk = step_slots(math.gcd(begin, end))
    first = begin // chunk
    shape = jax.ShapeDtypeStruct((total, block, block), BF16)
    out = pl.BlockSpec((chunk, block, block), lambda i: (i + first, 0, 0))
    size = (end - begin) * block * block
    return pl.pallas_call(
        functools.partial(gu_grad_body, first, len(before)),
        out_shape=(shape,) * 2,
        grid=((end - begin) // chunk,),
        in_specs=[IN_HBM, SCALARS] + [WHOLE] * 2 + [pl.BlockSpec(memory_space=pl.ANY)] * len(before),
        out_specs=(out,) * 2,
        scratch_shapes=Slots.scratch(index),
        input_output_aliases={4 + at: at for at in range(len(before))},
        compiler_params=params(),
        cost_estimate=cost(4 * size * tokens, 4 * size),
        name="gu_grads",
    )(in_hbm(index), count, d_pair, turned, *before)


def activate_body(*refs):
    own, *recv, hidden, coef = refs
    block = hidden.shape[2]
    for f in range(hidden.shape[0]):
        both = own[f]
        for part in recv:
            both = both + part[f].astype(F32)
        gate, up = both[:, :block], both[:, block:]
        sig = jax.nn.sigmoid(gate)
        silu = gate * sig
        hidden[f] = (silu * up).astype(BF16)
        coef[f, :, :block] = up * sig * (1.0 + gate * (1.0 - sig))
        coef[f, :, block:] = silu


def activate(own, recv):
    f_blocks, tokens, pair = own.shape
    return pl.pallas_call(
        activate_body,
        out_shape=(
            jax.ShapeDtypeStruct((f_blocks, tokens, pair // 2), BF16),
            jax.ShapeDtypeStruct(own.shape, F32),
        ),
        in_specs=[WHOLE] * (1 + len(recv)),
        out_specs=(WHOLE,) * 2,
        compiler_params=params(),
        cost_estimate=cost(20 * own.size, 8 * own.size),
        name="activate",
    )(own, *recv)


def down_blocks(first, hidden, pieces, dense, turned):
    f_blocks, tokens, block = hidden.shape
    d_blocks = pieces[0].shape[1] // block
    group = 2 if f_blocks % 2 == 0 else 1
    for f in range(f_blocks):
        turned[f * block : (f + 1) * block, :] = hidden[f].T
    for d in range(0, d_blocks, 2):
        y = jnp.concatenate([piece[:, d * block : (d + 2) * block] for piece in pieces], axis=0)
        for f in range(0, f_blocks, group):
            rows = turned[f * block : (f + group) * block, :]
            result = jnp.dot(rows, y, preferred_element_type=F32).astype(BF16)
            for row in range(group):
                for side in range(2):
                    dense[(first + f + row) * d_blocks + d + side] = result[
                        row * block : (row + 1) * block, side * block : (side + 1) * block
                    ]


def down_first_body(hidden, *refs):
    *pieces, dense, turned = refs
    dense[dense.shape[0] - 1] = jnp.zeros(dense.shape[1:], dense.dtype)
    down_blocks(0, hidden, pieces, dense, turned)


def down_second_body(first, index, count, hidden, _, *refs):
    *pieces, out, dense, index_here, slots_sem, turned, sem = refs
    slots = Slots(index, count, index_here, slots_sem)
    slots.copy.start()
    down_blocks(first, hidden, pieces, dense, turned)
    slots.copy.wait()
    zeros = dense.shape[0] - 1
    total = out.shape[0]

    @pl.loop(0, total, unroll=max(n for n in (1, 2, 4, 8) if total % n == 0))
    def _(s):
        place = jnp.where(s < slots.live, slots.index[0, 0, s], zeros)
        pltpu.make_async_copy(dense.at[place], out.at[s], sem).start()

    pltpu.make_async_copy(out, out, sem).wait()


def down_first(pieces, hidden, f_blocks):
    _, tokens, block = hidden.shape
    blocks = f_blocks * (pieces[0].shape[1] // block) + 1
    return pl.pallas_call(
        down_first_body,
        out_shape=pltpu.VMEM((blocks, block, block), BF16),
        in_specs=[WHOLE] * (1 + len(pieces)),
        out_specs=WHOLE,
        scratch_shapes=[pltpu.VMEM((hidden.shape[0] * block, tokens), BF16)],
        compiler_params=params(),
        cost_estimate=cost(blocks * block * block * tokens, 2 * blocks * block * block),
        name="down_first",
    )(hidden, *pieces)


def down_second(index, count, pieces, hidden, dense, slots):
    far_blocks, tokens, block = hidden.shape
    d_blocks = pieces[0].shape[1] // block
    first = (dense.shape[0] - 1) // d_blocks - far_blocks
    out, _ = pl.pallas_call(
        functools.partial(down_second_body, first),
        out_shape=(
            jax.ShapeDtypeStruct((slots, block, block), BF16),
            pltpu.VMEM(dense.shape, BF16),
        ),
        in_specs=[IN_HBM, SCALARS] + [WHOLE] * (2 + len(pieces)),
        out_specs=(IN_HBM, WHOLE),
        scratch_shapes=[
            *Slots.scratch(index),
            pltpu.VMEM((far_blocks * block, tokens), BF16),
            pltpu.SemaphoreType.DMA,
        ],
        input_output_aliases={3: 1},
        compiler_params=params(),
        cost_estimate=cost(slots * block * block * tokens, 2 * slots * block * block),
        name="down_second",
    )(in_hbm(index), count, hidden, resident(dense), *pieces)
    return out


def on_device(
    tokens, cotangent, gate_vals, up_vals, gu_index, gu_count, down_vals, down_index, down_count
):
    block = gate_vals.shape[-1]
    slots = gate_vals.shape[2]
    wide = lax.axis_size("wide")
    narrow = lax.axis_size("narrow")
    chips = wide // 2
    rows = tokens.shape[0]
    d_blocks = tokens.shape[1] // block
    f_blocks = FF // (block * wide)

    def exchange(array):
        return [swap(array, "narrow", narrow, k) for k in range(1, narrow)]

    flips = [chips >> hop for hop in range(1, chips.bit_length())]
    vals = (gate_vals, up_vals)
    x, index = tokens, gu_index
    weights = []
    for hop, flip in enumerate(flips):
        if hop > 0:
            x = jnp.concatenate([x, x_recv], axis=0)
            x, weights, index = lax.optimization_barrier((x, weights, index))
        x_recv = swap(x, "wide", wide, 2 * flip)
        if hop < 2:
            early = (down_count,) if hop == 0 else ()
            weights.append(fill(index, gu_count, vals[hop], d_blocks, f_blocks, early))
    y, index, _ = lax.optimization_barrier((cotangent, down_index, x))
    down_w = fill(index, down_count, down_vals, f_blocks, d_blocks)
    for flip in flips[:-1]:
        y = jnp.concatenate([y, swap(y, "wide", wide, 2 * flip)], axis=0)
    x, down_w = lax.optimization_barrier((x, down_w))
    x_pieces = [x, x_recv, swap(x, "wide", wide, 1), swap(x_recv, "wide", wide, 1)]
    y, _ = lax.optimization_barrier((y, x_recv))
    y_recv = swap(y, "wide", wide, 2 * flips[-1])

    near_own, near_send = gate_up(x_pieces, *weights, 0)
    near_recv = exchange(near_send)
    late, _ = lax.optimization_barrier((x, near_send))
    far_own, far_send = gate_up([late, *x_pieces[1:]], *weights, 1)
    far_recv = exchange(far_send)
    y, y_recv, _ = lax.optimization_barrier((y, y_recv, far_send))
    y_pieces = [y, y_recv, swap(y, "wide", wide, 1), swap(y_recv, "wide", wide, 1)]
    near_hidden, near_coef = activate(near_own, near_recv)
    down_w, near_hidden = lax.optimization_barrier((down_w, near_hidden))
    dh_own, dh_send, turned = d_hidden(y_pieces, x_pieces, down_w)
    y_pieces, dh_send = lax.optimization_barrier((y_pieces, dh_send))
    dh_recv = exchange(dh_send)
    dense = down_first(y_pieces, near_hidden, f_blocks)
    far_own, dense = lax.optimization_barrier((far_own, dense))
    far_hidden, far_coef = activate(far_own, far_recv)
    down_grad = down_second(down_index, down_count, y_pieces, far_hidden, dense, slots)
    down_grad, far_coef = lax.optimization_barrier((down_grad, far_coef))
    halves, d_pair = d_tokens_parts((near_coef, far_coef), dh_own, dh_recv, *weights)

    halves = [own + swap(send, "wide", wide, 1).astype(F32) for own, send in halves]
    kept = chips // 2 * rows
    far = [own[kept:].astype(BF16) for own in halves]
    cut = slots * 2 // 3 if slots % 3 == 0 else slots
    far[1], d_pair = lax.optimization_barrier((far[1], d_pair))
    grads = gu_grads(gu_index, gu_count, d_pair, turned, slots, 0, cut, ())
    halves = [
        own[:kept] + swap(part, "wide", wide, 2 * flips[-1]).astype(F32)
        for own, part in zip(halves, far)
    ]
    own = jnp.concatenate(halves, axis=1)
    sends = [own[p * rows : (p + 1) * rows].astype(BF16) for p in range(1, chips // 2)]
    if cut < slots:
        sends, d_pair, grads = lax.optimization_barrier((sends, d_pair, grads))
        grads = gu_grads(gu_index, gu_count, d_pair, turned, slots, cut, slots, grads)
    own = own[:rows]
    for p, part in enumerate(sends, 1):
        flip = sum(flips[bit] for bit in range(len(flips)) if p >> bit & 1)
        own = own + swap(part, "wide", wide, 2 * flip).astype(F32)
    gate_grad, up_grad = grads
    return (
        own.astype(BF16),
        gate_grad[None, None],
        up_grad[None, None],
        down_grad[None, None],
    )


def solution(mesh):
    in_specs = (
        P("wide", "narrow"),
        P("wide", "narrow"),
        P("narrow", "wide", None, None, None),
        P("narrow", "wide", None, None, None),
        P("narrow", "wide", None),
        P("narrow", "wide"),
        P("wide", "narrow", None, None, None),
        P("wide", "narrow", None),
        P("wide", "narrow"),
    )
    out_specs = (
        P("wide", "narrow"),
        P("narrow", "wide", None, None, None),
        P("narrow", "wide", None, None, None),
        P("wide", "narrow", None, None, None),
    )
    return jax.shard_map(
        on_device, mesh=mesh, in_specs=in_specs, out_specs=out_specs, check_vma=False
    )
```

```python
import functools
import math

import jax
import jax.numpy as jnp
from jax import lax
from jax.experimental import pallas as pl
from jax.experimental.pallas import tpu as pltpu
from jax.sharding import PartitionSpec as P

FF = 16384
F32 = jnp.float32
BF16 = jnp.bfloat16
VMEM_LIMIT = 8 * 1024 * 1024

WHOLE = pl.BlockSpec(memory_space=pltpu.VMEM)
SCALARS = pl.BlockSpec(memory_space=pltpu.SMEM)
IN_HBM = pl.BlockSpec(memory_space=pltpu.HBM)


def params(vmem=VMEM_LIMIT):
    return pltpu.CompilerParams(vmem_limit_bytes=vmem)


def cost(flops, bytes_accessed):
    return pl.CostEstimate(flops=int(flops), bytes_accessed=int(bytes_accessed), transcendentals=0)


def resident(array):
    return pltpu.with_memory_space_constraint(array, pltpu.VMEM)


def in_hbm(array):
    return pltpu.with_memory_space_constraint(array, pltpu.HBM)


def swap(array, axis, size, flip):
    return lax.ppermute(array, axis, [(i, i ^ flip) for i in range(size)])


def split_index(number, size):
    if size & (size - 1):
        return number // size, number % size
    return number >> (size.bit_length() - 1), number & (size - 1)


class Slots:
    def __init__(self, index_from, count, index, sem):
        self.copy = pltpu.make_async_copy(index_from, index, sem)
        self.index, self.live = index, count[0, 0]

    @staticmethod
    def scratch(index):
        return [pltpu.SMEM(index.shape, index.dtype), pltpu.SemaphoreType.DMA]

    def place(self, slot, size):
        return split_index(self.index[0, 0, slot], size)


def fill_body(index, count, source, *refs):
    target, index_here, slots_sem, sem = refs[-4:]
    slots = Slots(index, count, index_here, slots_sem)
    slots.copy.start()
    outer, inner = target.shape[:2]
    chunk = min(inner, 8)

    @pl.loop(0, outer)
    def _(high):
        target[high] = jnp.zeros(target.shape[1:], target.dtype)

    slots.copy.wait()

    @pl.loop(0, slots.live)
    def _(s):
        high, low = slots.place(s, inner)
        pltpu.make_async_copy(source.at[0, 0, s], target.at[high, low], sem).start()

    many, few = split_index(slots.live, chunk)

    @pl.loop(0, many)
    def _(_):
        blocks = pl.ds(0, chunk)
        pltpu.make_async_copy(source.at[0, 0, blocks], target.at[0, blocks], sem).wait()

    @pl.loop(0, few)
    def _(_):
        pltpu.make_async_copy(source.at[0, 0, 0], target.at[0, 0], sem).wait()


def fill(index, count, slots, outer, inner, early=()):
    block = slots.shape[-1]
    return pl.pallas_call(
        fill_body,
        out_shape=pltpu.VMEM((outer, inner, block, block), BF16),
        in_specs=[IN_HBM, SCALARS, IN_HBM] + [SCALARS] * len(early),
        out_specs=WHOLE,
        scratch_shapes=[*Slots.scratch(index), pltpu.SemaphoreType.DMA],
        compiler_params=params(),
        cost_estimate=cost(0, slots.size * 2),
        name="fill",
    )(in_hbm(index), count, in_hbm(slots), *early)


def stack(pieces):
    return jnp.concatenate([piece[...] for piece in pieces], axis=0)


def gate_up_body(first, *refs):
    *pieces, gate_w, up_w, own, send = refs
    d_blocks, _, block, _ = gate_w.shape
    x = stack(pieces)
    for c in range(own.shape[0]):
        weights = jnp.concatenate(
            [
                gate_w[:, first + c].reshape(d_blocks * block, block),
                up_w[:, first + c].reshape(d_blocks * block, block),
            ],
            axis=1,
        )
        result = jnp.dot(x, weights, preferred_element_type=F32)
        own[c] = result
        send[c] = result.astype(BF16)


def gate_up(pieces, gate_w, up_w, half):
    d_blocks, f_blocks, block, _ = gate_w.shape
    tokens = sum(piece.shape[0] for piece in pieces)
    shape = (f_blocks // 2, tokens, 2 * block)
    return pl.pallas_call(
        functools.partial(gate_up_body, half * f_blocks // 2),
        out_shape=(jax.ShapeDtypeStruct(shape, F32), jax.ShapeDtypeStruct(shape, BF16)),
        in_specs=[WHOLE] * (len(pieces) + 2),
        out_specs=(WHOLE,) * 2,
        compiler_params=params(),
        cost_estimate=cost(2 * tokens * gate_w.size, 2 * gate_w.size),
        name="gate_up",
    )(*pieces, resident(gate_w), resident(up_w))


def d_hidden_body(group, pieces_count, *refs):
    y_pieces, x_pieces = refs[:pieces_count], refs[pieces_count : 2 * pieces_count]
    down_w, own, send, x_turned, y_turned = refs[2 * pieces_count :]
    f_blocks, d_blocks, block, _ = down_w.shape
    for d in range(d_blocks):
        at = slice(d * block, (d + 1) * block)
        y_turned[at, :] = jnp.concatenate([piece[:, at] for piece in y_pieces], axis=0).T
    y = y_turned[...]
    for f in range(0, f_blocks, group):
        weights = jnp.concatenate(
            [
                down_w[f : f + group, d].reshape(group * block, block)
                for d in range(d_blocks)
            ],
            axis=1,
        )
        result = jnp.dot(weights, y, preferred_element_type=F32).T
        for side in range(group):
            part = result[:, side * block : (side + 1) * block]
            own[f + side] = part
            send[f + side] = part.astype(BF16)
    for d in range(d_blocks):
        at = slice(d * block, (d + 1) * block)
        x_turned[d] = jnp.concatenate([piece[:, at] for piece in x_pieces], axis=0).T


def d_hidden(y_pieces, x_pieces, down_w):
    f_blocks, d_blocks, block, _ = down_w.shape
    tokens = sum(piece.shape[0] for piece in y_pieces)
    shape = (f_blocks, tokens, block)
    group = max(n for n in (1, 2, 4) if f_blocks % n == 0)
    return pl.pallas_call(
        functools.partial(d_hidden_body, group, len(y_pieces)),
        out_shape=(
            jax.ShapeDtypeStruct(shape, F32),
            jax.ShapeDtypeStruct(shape, BF16),
            jax.ShapeDtypeStruct((d_blocks, block, tokens), BF16),
        ),
        in_specs=[WHOLE] * (2 * len(y_pieces) + 1),
        out_specs=(WHOLE,) * 3,
        scratch_shapes=[pltpu.VMEM((d_blocks * block, tokens), BF16)],
        compiler_params=params(),
        cost_estimate=cost(2 * tokens * down_w.size, 2 * down_w.size),
        name="d_hidden",
    )(*y_pieces, *x_pieces, resident(down_w))


def d_tokens_columns(group, begin, grads, gate_w, up_w, own, send):
    f_blocks, block = gate_w.shape[1:3]
    half = own.shape[0]
    for at in range(0, own.shape[1] // block, group):
        rows = slice(begin + at, begin + at + group)
        weights = jnp.concatenate(
            [
                ref[rows, c].reshape(group * block, block)
                for c in range(f_blocks)
                for ref in (gate_w, up_w)
            ],
            axis=1,
        )
        result = jnp.dot(weights, grads, preferred_element_type=F32).T
        columns = slice(at * block, (at + group) * block)
        own[:, columns] = result[:half]
        send[:, columns] = result[half:].astype(BF16)


def d_tokens_first_body(group, *refs):
    *coef, dh_own = refs[:3]
    *dh_recv, gate_w, up_w, own, send, d_pair, turned = refs[3:]
    f_blocks, block = gate_w.shape[1:3]
    for c in range(f_blocks):
        dh = dh_own[c]
        for part in dh_recv:
            dh = dh + part[c].astype(F32)
        side, at = divmod(c, f_blocks // 2)
        both = (jnp.concatenate([dh, dh], axis=1) * coef[side][at]).astype(BF16)
        d_pair[c] = both
        for side in range(2):
            turned[pl.ds((2 * c + side) * block, block), :] = both[
                :, side * block : (side + 1) * block
            ].T
    d_tokens_columns(group, 0, turned[...], gate_w, up_w, own, send)


def d_tokens_second_body(group, turned, gate_w, up_w, own, send):
    d_blocks = gate_w.shape[0]
    d_tokens_columns(group, d_blocks // 2, turned[...], gate_w, up_w, own, send)


def d_tokens_parts(coef, dh_own, dh_recv, gate_w, up_w):
    d_blocks, f_blocks, block, _ = gate_w.shape
    tokens = dh_own.shape[1]
    half = (tokens // 2, d_blocks // 2 * block)
    group = max(n for n in (1, 2, 4) if d_blocks // 2 % n == 0)
    halves = (jax.ShapeDtypeStruct(half, F32), jax.ShapeDtypeStruct(half, BF16))
    common = dict(
        compiler_params=params(),
        cost_estimate=cost(2 * tokens * gate_w.size, 2 * gate_w.size),
    )
    weights = resident(gate_w), resident(up_w)
    own, send, d_pair, turned = pl.pallas_call(
        functools.partial(d_tokens_first_body, group),
        out_shape=(
            *halves,
            jax.ShapeDtypeStruct((f_blocks, tokens, 2 * block), BF16),
            jax.ShapeDtypeStruct((f_blocks * 2 * block, tokens), BF16),
        ),
        in_specs=[WHOLE] * (5 + len(dh_recv)),
        out_specs=(WHOLE,) * 4,
        name="d_tokens_first",
        **common,
    )(*coef, dh_own, *dh_recv, *weights)
    second = pl.pallas_call(
        functools.partial(d_tokens_second_body, group),
        out_shape=halves,
        in_specs=[WHOLE] * 3,
        out_specs=(WHOLE,) * 2,
        name="d_tokens_second",
        **common,
    )(turned, *weights)
    return ((own, send), second), d_pair


def step_slots(slots):
    return max(n for n in range(1, 33) if slots % n == 0)


def gu_grad_body(first, given, index, count, d_pair, turned, *refs):
    gate_out, up_out, *scalars = refs[given:]
    slots = Slots(index, count, *scalars)
    f_blocks = d_pair.shape[0]
    block = turned.shape[1]
    step = pl.program_id(0)

    @pl.when(step == 0)
    def _():
        slots.copy.start()
        slots.copy.wait()

    chunk = gate_out.shape[0]
    begin = (step + first) * chunk

    def work(masked):
        for j in range(chunk):
            d, f = slots.place(begin + j, f_blocks)
            result = jnp.dot(turned[d], d_pair[f], preferred_element_type=F32)
            if masked:
                result = jnp.where(begin + j < slots.live, result, 0.0)
            result = result.astype(BF16)
            gate_out[j] = result[:, :block]
            up_out[j] = result[:, block:]

    @pl.when(begin + chunk <= slots.live)
    def _():
        work(False)

    @pl.when(begin + chunk > slots.live)
    def _():
        work(True)


def gu_grads(index, count, d_pair, turned, total, begin, end, before):
    block, tokens = turned.shape[1:]
    chunk = step_slots(math.gcd(begin, end))
    first = begin // chunk
    shape = jax.ShapeDtypeStruct((total, block, block), BF16)
    out = pl.BlockSpec((chunk, block, block), lambda i: (i + first, 0, 0))
    size = (end - begin) * block * block
    return pl.pallas_call(
        functools.partial(gu_grad_body, first, len(before)),
        out_shape=(shape,) * 2,
        grid=((end - begin) // chunk,),
        in_specs=[IN_HBM, SCALARS] + [WHOLE] * 2 + [pl.BlockSpec(memory_space=pl.ANY)] * len(before),
        out_specs=(out,) * 2,
        scratch_shapes=Slots.scratch(index),
        input_output_aliases={4 + at: at for at in range(len(before))},
        compiler_params=params(),
        cost_estimate=cost(4 * size * tokens, 4 * size),
        name="gu_grads",
    )(in_hbm(index), count, d_pair, turned, *before)


def activate_body(*refs):
    own, *recv, hidden, coef = refs
    block = hidden.shape[2]
    for f in range(hidden.shape[0]):
        both = own[f]
        for part in recv:
            both = both + part[f].astype(F32)
        gate, up = both[:, :block], both[:, block:]
        sig = jax.nn.sigmoid(gate)
        silu = gate * sig
        hidden[f] = (silu * up).astype(BF16)
        coef[f, :, :block] = up * sig * (1.0 + gate * (1.0 - sig))
        coef[f, :, block:] = silu


def activate(own, recv):
    f_blocks, tokens, pair = own.shape
    return pl.pallas_call(
        activate_body,
        out_shape=(
            jax.ShapeDtypeStruct((f_blocks, tokens, pair // 2), BF16),
            jax.ShapeDtypeStruct(own.shape, F32),
        ),
        in_specs=[WHOLE] * (1 + len(recv)),
        out_specs=(WHOLE,) * 2,
        compiler_params=params(),
        cost_estimate=cost(20 * own.size, 8 * own.size),
        name="activate",
    )(own, *recv)


def down_blocks(first, hidden, pieces, dense, turned):
    f_blocks, tokens, block = hidden.shape
    d_blocks = pieces[0].shape[1] // block
    group = 2 if f_blocks % 2 == 0 else 1
    for f in range(f_blocks):
        turned[f * block : (f + 1) * block, :] = hidden[f].T
    for d in range(0, d_blocks, 2):
        y = jnp.concatenate([piece[:, d * block : (d + 2) * block] for piece in pieces], axis=0)
        for f in range(0, f_blocks, group):
            rows = turned[f * block : (f + group) * block, :]
            result = jnp.dot(rows, y, preferred_element_type=F32).astype(BF16)
            for row in range(group):
                for side in range(2):
                    dense[(first + f + row) * d_blocks + d + side] = result[
                        row * block : (row + 1) * block, side * block : (side + 1) * block
                    ]


def down_first_body(hidden, *refs):
    *pieces, dense, turned = refs
    dense[dense.shape[0] - 1] = jnp.zeros(dense.shape[1:], dense.dtype)
    down_blocks(0, hidden, pieces, dense, turned)


def down_second_body(first, index, count, hidden, _, *refs):
    *pieces, out, dense, index_here, slots_sem, turned, sem = refs
    slots = Slots(index, count, index_here, slots_sem)
    slots.copy.start()
    down_blocks(first, hidden, pieces, dense, turned)
    slots.copy.wait()
    zeros = dense.shape[0] - 1
    total = out.shape[0]

    @pl.loop(0, total, unroll=max(n for n in (1, 2, 4, 8) if total % n == 0))
    def _(s):
        place = jnp.where(s < slots.live, slots.index[0, 0, s], zeros)
        pltpu.make_async_copy(dense.at[place], out.at[s], sem).start()

    pltpu.make_async_copy(out, out, sem).wait()


def down_first(pieces, hidden, f_blocks):
    _, tokens, block = hidden.shape
    blocks = f_blocks * (pieces[0].shape[1] // block) + 1
    return pl.pallas_call(
        down_first_body,
        out_shape=pltpu.VMEM((blocks, block, block), BF16),
        in_specs=[WHOLE] * (1 + len(pieces)),
        out_specs=WHOLE,
        scratch_shapes=[pltpu.VMEM((hidden.shape[0] * block, tokens), BF16)],
        compiler_params=params(),
        cost_estimate=cost(blocks * block * block * tokens, 2 * blocks * block * block),
        name="down_first",
    )(hidden, *pieces)


def down_second(index, count, pieces, hidden, dense, slots):
    far_blocks, tokens, block = hidden.shape
    d_blocks = pieces[0].shape[1] // block
    first = (dense.shape[0] - 1) // d_blocks - far_blocks
    out, _ = pl.pallas_call(
        functools.partial(down_second_body, first),
        out_shape=(
            jax.ShapeDtypeStruct((slots, block, block), BF16),
            pltpu.VMEM(dense.shape, BF16),
        ),
        in_specs=[IN_HBM, SCALARS] + [WHOLE] * (2 + len(pieces)),
        out_specs=(IN_HBM, WHOLE),
        scratch_shapes=[
            *Slots.scratch(index),
            pltpu.VMEM((far_blocks * block, tokens), BF16),
            pltpu.SemaphoreType.DMA,
        ],
        input_output_aliases={3: 1},
        compiler_params=params(),
        cost_estimate=cost(slots * block * block * tokens, 2 * slots * block * block),
        name="down_second",
    )(in_hbm(index), count, hidden, resident(dense), *pieces)
    return out


def on_device(
    tokens, cotangent, gate_vals, up_vals, gu_index, gu_count, down_vals, down_index, down_count
):
    block = gate_vals.shape[-1]
    slots = gate_vals.shape[2]
    wide = lax.axis_size("wide")
    narrow = lax.axis_size("narrow")
    chips = wide // 2
    rows = tokens.shape[0]
    d_blocks = tokens.shape[1] // block
    f_blocks = FF // (block * wide)

    def exchange(array):
        return [swap(array, "narrow", narrow, k) for k in range(1, narrow)]

    flips = [chips >> hop for hop in range(1, chips.bit_length())]
    vals = (gate_vals, up_vals)
    x, y, index = tokens, cotangent, gu_index
    weights = []
    for hop, flip in enumerate(flips):
        if hop > 0:
            x = jnp.concatenate([x, x_recv], axis=0)
            y = jnp.concatenate([y, y_recv], axis=0)
            x, y, weights, index = lax.optimization_barrier((x, y, weights, index))
        x_recv = swap(x, "wide", wide, 2 * flip)
        if hop < len(flips) - 1:
            y_recv = swap(y, "wide", wide, 2 * flip)
        if hop < 2:
            early = (down_count,) if hop == 0 else ()
            weights.append(fill(index, gu_count, vals[hop], d_blocks, f_blocks, early))
    index, _ = lax.optimization_barrier((down_index, x))
    down_w = fill(index, down_count, down_vals, f_blocks, d_blocks)
    x, down_w = lax.optimization_barrier((x, down_w))
    x_pieces = [x, x_recv, swap(x, "wide", wide, 1), swap(x_recv, "wide", wide, 1)]
    y, _ = lax.optimization_barrier((y, x_recv))
    y_recv = swap(y, "wide", wide, 2 * flips[-1])

    near_own, near_send = gate_up(x_pieces, *weights, 0)
    near_recv = exchange(near_send)
    late, _ = lax.optimization_barrier((x, near_send))
    far_own, far_send = gate_up([late, *x_pieces[1:]], *weights, 1)
    far_recv = exchange(far_send)
    y, y_recv, _ = lax.optimization_barrier((y, y_recv, far_send))
    y_pieces = [y, y_recv, swap(y, "wide", wide, 1), swap(y_recv, "wide", wide, 1)]
    near_hidden, near_coef = activate(near_own, near_recv)
    down_w, near_hidden = lax.optimization_barrier((down_w, near_hidden))
    dh_own, dh_send, turned = d_hidden(y_pieces, x_pieces, down_w)
    y_pieces, dh_send = lax.optimization_barrier((y_pieces, dh_send))
    dh_recv = exchange(dh_send)
    dense = down_first(y_pieces, near_hidden, f_blocks)
    far_own, dense = lax.optimization_barrier((far_own, dense))
    far_hidden, far_coef = activate(far_own, far_recv)
    down_grad = down_second(down_index, down_count, y_pieces, far_hidden, dense, slots)
    down_grad, far_coef = lax.optimization_barrier((down_grad, far_coef))
    halves, d_pair = d_tokens_parts((near_coef, far_coef), dh_own, dh_recv, *weights)

    halves = [own + swap(send, "wide", wide, 1).astype(F32) for own, send in halves]
    kept = chips // 2 * rows
    far = [own[kept:].astype(BF16) for own in halves]
    cut = slots * 2 // 3 if slots % 3 == 0 else slots
    far[1], d_pair = lax.optimization_barrier((far[1], d_pair))
    grads = gu_grads(gu_index, gu_count, d_pair, turned, slots, 0, cut, ())
    halves = [
        own[:kept] + swap(part, "wide", wide, 2 * flips[-1]).astype(F32)
        for own, part in zip(halves, far)
    ]
    own = jnp.concatenate(halves, axis=1)
    sends = [own[p * rows : (p + 1) * rows].astype(BF16) for p in range(1, chips // 2)]
    if cut < slots:
        sends, d_pair, grads = lax.optimization_barrier((sends, d_pair, grads))
        grads = gu_grads(gu_index, gu_count, d_pair, turned, slots, cut, slots, grads)
    own = own[:rows]
    for p, part in enumerate(sends, 1):
        flip = sum(flips[bit] for bit in range(len(flips)) if p >> bit & 1)
        own = own + swap(part, "wide", wide, 2 * flip).astype(F32)
    gate_grad, up_grad = grads
    return (
        own.astype(BF16),
        gate_grad[None, None],
        up_grad[None, None],
        down_grad[None, None],
    )


def solution(mesh):
    in_specs = (
        P("wide", "narrow"),
        P("wide", "narrow"),
        P("narrow", "wide", None, None, None),
        P("narrow", "wide", None, None, None),
        P("narrow", "wide", None),
        P("narrow", "wide"),
        P("wide", "narrow", None, None, None),
        P("wide", "narrow", None),
        P("wide", "narrow"),
    )
    out_specs = (
        P("wide", "narrow"),
        P("narrow", "wide", None, None, None),
        P("narrow", "wide", None, None, None),
        P("wide", "narrow", None, None, None),
    )
    return jax.shard_map(
        on_device, mesh=mesh, in_specs=in_specs, out_specs=out_specs, check_vma=False
    )
```

```python
import functools
import math

import jax
import jax.numpy as jnp
from jax import lax
from jax.experimental import pallas as pl
from jax.experimental.pallas import tpu as pltpu
from jax.sharding import PartitionSpec as P

FF = 16384
F32 = jnp.float32
BF16 = jnp.bfloat16
VMEM_LIMIT = 8 * 1024 * 1024

WHOLE = pl.BlockSpec(memory_space=pltpu.VMEM)
SCALARS = pl.BlockSpec(memory_space=pltpu.SMEM)
IN_HBM = pl.BlockSpec(memory_space=pltpu.HBM)


def params(vmem=VMEM_LIMIT):
    return pltpu.CompilerParams(vmem_limit_bytes=vmem)


def cost(flops, bytes_accessed):
    return pl.CostEstimate(flops=int(flops), bytes_accessed=int(bytes_accessed), transcendentals=0)


def resident(array):
    return pltpu.with_memory_space_constraint(array, pltpu.VMEM)


def in_hbm(array):
    return pltpu.with_memory_space_constraint(array, pltpu.HBM)


def swap(array, axis, size, flip):
    return lax.ppermute(array, axis, [(i, i ^ flip) for i in range(size)])


def split_index(number, size):
    if size & (size - 1):
        return number // size, number % size
    return number >> (size.bit_length() - 1), number & (size - 1)


class Slots:
    def __init__(self, index_from, count, index, sem):
        self.copy = pltpu.make_async_copy(index_from, index, sem)
        self.index, self.live = index, count[0, 0]

    @staticmethod
    def scratch(index):
        return [pltpu.SMEM(index.shape, index.dtype), pltpu.SemaphoreType.DMA]

    def place(self, slot, size):
        return split_index(self.index[0, 0, slot], size)


def fill_body(index, count, source, *refs):
    target, index_here, slots_sem, sem = refs[-4:]
    slots = Slots(index, count, index_here, slots_sem)
    slots.copy.start()
    outer, inner = target.shape[:2]
    chunk = min(inner, 8)

    @pl.loop(0, outer)
    def _(high):
        target[high] = jnp.zeros(target.shape[1:], target.dtype)

    slots.copy.wait()

    @pl.loop(0, slots.live)
    def _(s):
        high, low = slots.place(s, inner)
        pltpu.make_async_copy(source.at[0, 0, s], target.at[high, low], sem).start()

    many, few = split_index(slots.live, chunk)

    @pl.loop(0, many)
    def _(_):
        blocks = pl.ds(0, chunk)
        pltpu.make_async_copy(source.at[0, 0, blocks], target.at[0, blocks], sem).wait()

    @pl.loop(0, few)
    def _(_):
        pltpu.make_async_copy(source.at[0, 0, 0], target.at[0, 0], sem).wait()


def fill(index, count, slots, outer, inner, early=()):
    block = slots.shape[-1]
    return pl.pallas_call(
        fill_body,
        out_shape=pltpu.VMEM((outer, inner, block, block), BF16),
        in_specs=[IN_HBM, SCALARS, IN_HBM] + [SCALARS] * len(early),
        out_specs=WHOLE,
        scratch_shapes=[*Slots.scratch(index), pltpu.SemaphoreType.DMA],
        compiler_params=params(),
        cost_estimate=cost(0, slots.size * 2),
        name="fill",
    )(in_hbm(index), count, in_hbm(slots), *early)


def stack(pieces):
    return jnp.concatenate([piece[...] for piece in pieces], axis=0)


def gate_up_body(first, *refs):
    *pieces, gate_w, up_w, own, send = refs
    d_blocks, _, block, _ = gate_w.shape
    x = stack(pieces)
    for c in range(own.shape[0]):
        weights = jnp.concatenate(
            [
                gate_w[:, first + c].reshape(d_blocks * block, block),
                up_w[:, first + c].reshape(d_blocks * block, block),
            ],
            axis=1,
        )
        result = jnp.dot(x, weights, preferred_element_type=F32)
        own[c] = result
        send[c] = result.astype(BF16)


def gate_up(pieces, gate_w, up_w, half):
    d_blocks, f_blocks, block, _ = gate_w.shape
    tokens = sum(piece.shape[0] for piece in pieces)
    shape = (f_blocks // 2, tokens, 2 * block)
    return pl.pallas_call(
        functools.partial(gate_up_body, half * f_blocks // 2),
        out_shape=(jax.ShapeDtypeStruct(shape, F32), jax.ShapeDtypeStruct(shape, BF16)),
        in_specs=[WHOLE] * (len(pieces) + 2),
        out_specs=(WHOLE,) * 2,
        compiler_params=params(),
        cost_estimate=cost(2 * tokens * gate_w.size, 2 * gate_w.size),
        name="gate_up",
    )(*pieces, resident(gate_w), resident(up_w))


def d_hidden_body(group, pieces_count, *refs):
    y_pieces, x_pieces = refs[:pieces_count], refs[pieces_count:-5]
    down_w, own, send, x_turned, y_turned = refs[-5:]
    f_blocks, d_blocks, block, _ = down_w.shape
    for d in range(d_blocks):
        at = slice(d * block, (d + 1) * block)
        y_turned[at, :] = jnp.concatenate([piece[:, at] for piece in y_pieces], axis=0).T
    y = y_turned[...]
    for f in range(0, f_blocks, group):
        weights = jnp.concatenate(
            [
                down_w[f : f + group, d].reshape(group * block, block)
                for d in range(d_blocks)
            ],
            axis=1,
        )
        result = jnp.dot(weights, y, preferred_element_type=F32).T
        for side in range(group):
            part = result[:, side * block : (side + 1) * block]
            own[f + side] = part
            send[f + side] = part.astype(BF16)
    for d in range(d_blocks):
        at = slice(d * block, (d + 1) * block)
        x_turned[d] = jnp.concatenate([piece[:, at] for piece in x_pieces], axis=0).T


def d_hidden(y_pieces, x_pieces, down_w):
    f_blocks, d_blocks, block, _ = down_w.shape
    tokens = sum(piece.shape[0] for piece in y_pieces)
    shape = (f_blocks, tokens, block)
    group = max(n for n in (1, 2, 4, 8) if f_blocks % n == 0)
    return pl.pallas_call(
        functools.partial(d_hidden_body, group, len(y_pieces)),
        out_shape=(
            jax.ShapeDtypeStruct(shape, F32),
            jax.ShapeDtypeStruct(shape, BF16),
            jax.ShapeDtypeStruct((d_blocks, block, tokens), BF16),
        ),
        in_specs=[WHOLE] * (len(y_pieces) + len(x_pieces) + 1),
        out_specs=(WHOLE,) * 3,
        scratch_shapes=[pltpu.VMEM((d_blocks * block, tokens), BF16)],
        compiler_params=params(),
        cost_estimate=cost(2 * tokens * down_w.size, 2 * down_w.size),
        name="d_hidden",
    )(*y_pieces, *x_pieces, resident(down_w))


def d_tokens_columns(group, begin, grads, gate_w, up_w, own, send):
    f_blocks, block = gate_w.shape[1:3]
    half = own.shape[0]
    for at in range(0, own.shape[1] // block, group):
        rows = slice(begin + at, begin + at + group)
        weights = jnp.concatenate(
            [
                ref[rows, c].reshape(group * block, block)
                for c in range(f_blocks)
                for ref in (gate_w, up_w)
            ],
            axis=1,
        )
        result = jnp.dot(weights, grads, preferred_element_type=F32).T
        columns = slice(at * block, (at + group) * block)
        own[:, columns] = result[:half]
        send[:, columns] = result[half:].astype(BF16)


def d_tokens_first_body(group, *refs):
    *coef, dh_own = refs[:3]
    *dh_recv, gate_w, up_w, own, send, d_pair, turned = refs[3:]
    f_blocks, block = gate_w.shape[1:3]
    for c in range(f_blocks):
        dh = dh_own[c]
        for part in dh_recv:
            dh = dh + part[c].astype(F32)
        side, at = divmod(c, f_blocks // 2)
        both = (jnp.concatenate([dh, dh], axis=1) * coef[side][at]).astype(BF16)
        d_pair[c] = both
        for side in range(2):
            turned[pl.ds((2 * c + side) * block, block), :] = both[
                :, side * block : (side + 1) * block
            ].T
    d_tokens_columns(group, 0, turned[...], gate_w, up_w, own, send)


def d_tokens_second_body(group, turned, gate_w, up_w, own, send):
    d_blocks = gate_w.shape[0]
    d_tokens_columns(group, d_blocks // 2, turned[...], gate_w, up_w, own, send)


def d_tokens_parts(coef, dh_own, dh_recv, gate_w, up_w):
    d_blocks, f_blocks, block, _ = gate_w.shape
    tokens = dh_own.shape[1]
    half = (tokens // 2, d_blocks // 2 * block)
    group = max(n for n in (1, 2, 4, 8) if d_blocks // 2 % n == 0)
    halves = (jax.ShapeDtypeStruct(half, F32), jax.ShapeDtypeStruct(half, BF16))
    common = dict(
        compiler_params=params(),
        cost_estimate=cost(2 * tokens * gate_w.size, 2 * gate_w.size),
    )
    weights = resident(gate_w), resident(up_w)
    own, send, d_pair, turned = pl.pallas_call(
        functools.partial(d_tokens_first_body, group),
        out_shape=(
            *halves,
            jax.ShapeDtypeStruct((f_blocks, tokens, 2 * block), BF16),
            jax.ShapeDtypeStruct((f_blocks * 2 * block, tokens), BF16),
        ),
        in_specs=[WHOLE] * (5 + len(dh_recv)),
        out_specs=(WHOLE,) * 4,
        name="d_tokens_first",
        **common,
    )(*coef, dh_own, *dh_recv, *weights)
    second = pl.pallas_call(
        functools.partial(d_tokens_second_body, group),
        out_shape=halves,
        in_specs=[WHOLE] * 3,
        out_specs=(WHOLE,) * 2,
        name="d_tokens_second",
        **common,
    )(turned, *weights)
    return ((own, send), second), d_pair


def step_slots(slots):
    return max(n for n in range(1, 33) if slots % n == 0)


def gu_grad_body(first, given, index, count, d_pair, turned, *refs):
    gate_out, up_out, *scalars = refs[given:]
    slots = Slots(index, count, *scalars)
    f_blocks = d_pair.shape[0]
    block = turned.shape[1]
    step = pl.program_id(0)

    @pl.when(step == 0)
    def _():
        slots.copy.start()
        slots.copy.wait()

    chunk = gate_out.shape[0]
    begin = (step + first) * chunk

    def work(masked):
        for j in range(chunk):
            d, f = slots.place(begin + j, f_blocks)
            result = jnp.dot(turned[d], d_pair[f], preferred_element_type=F32)
            if masked:
                result = jnp.where(begin + j < slots.live, result, 0.0)
            result = result.astype(BF16)
            gate_out[j] = result[:, :block]
            up_out[j] = result[:, block:]

    @pl.when(begin + chunk <= slots.live)
    def _():
        work(False)

    @pl.when((begin + chunk > slots.live) & (begin < slots.live))
    def _():
        work(True)

    @pl.when(begin >= slots.live)
    def _():
        gate_out[...] = jnp.zeros(gate_out.shape, gate_out.dtype)
        up_out[...] = jnp.zeros(up_out.shape, up_out.dtype)


def gu_grads(index, count, d_pair, turned, total, begin, end, before):
    block, tokens = turned.shape[1:]
    chunk = step_slots(math.gcd(begin, end))
    first = begin // chunk
    shape = jax.ShapeDtypeStruct((total, block, block), BF16)
    out = pl.BlockSpec((chunk, block, block), lambda i: (i + first, 0, 0))
    size = (end - begin) * block * block
    return pl.pallas_call(
        functools.partial(gu_grad_body, first, len(before)),
        out_shape=(shape,) * 2,
        grid=((end - begin) // chunk,),
        in_specs=[IN_HBM, SCALARS] + [WHOLE] * 2 + [pl.BlockSpec(memory_space=pl.ANY)] * len(before),
        out_specs=(out,) * 2,
        scratch_shapes=Slots.scratch(index),
        input_output_aliases={4 + at: at for at in range(len(before))},
        compiler_params=params(),
        cost_estimate=cost(4 * size * tokens, 4 * size),
        name="gu_grads",
    )(in_hbm(index), count, d_pair, turned, *before)


def activate_body(*refs):
    own, *recv, hidden, coef = refs
    block = hidden.shape[2]
    for f in range(hidden.shape[0]):
        both = own[f]
        for part in recv:
            both = both + part[f].astype(F32)
        gate, up = both[:, :block], both[:, block:]
        sig = jax.nn.sigmoid(gate)
        silu = gate * sig
        hidden[f] = (silu * up).astype(BF16)
        coef[f, :, :block] = up * sig * (1.0 + gate * (1.0 - sig))
        coef[f, :, block:] = silu


def activate(own, recv):
    f_blocks, tokens, pair = own.shape
    return pl.pallas_call(
        activate_body,
        out_shape=(
            jax.ShapeDtypeStruct((f_blocks, tokens, pair // 2), BF16),
            jax.ShapeDtypeStruct(own.shape, F32),
        ),
        in_specs=[WHOLE] * (1 + len(recv)),
        out_specs=(WHOLE,) * 2,
        compiler_params=params(),
        cost_estimate=cost(20 * own.size, 8 * own.size),
        name="activate",
    )(own, *recv)


def down_blocks(first, hidden, pieces, dense, turned):
    f_blocks, tokens, block = hidden.shape
    d_blocks = pieces[0].shape[1] // block
    group = 2 if f_blocks % 2 == 0 else 1
    for f in range(f_blocks):
        turned[f * block : (f + 1) * block, :] = hidden[f].T
    for d in range(0, d_blocks, 2):
        y = jnp.concatenate([piece[:, d * block : (d + 2) * block] for piece in pieces], axis=0)
        for f in range(0, f_blocks, group):
            rows = turned[f * block : (f + group) * block, :]
            result = jnp.dot(rows, y, preferred_element_type=F32).astype(BF16)
            for row in range(group):
                for side in range(2):
                    dense[(first + f + row) * d_blocks + d + side] = result[
                        row * block : (row + 1) * block, side * block : (side + 1) * block
                    ]


def down_first_body(hidden, *refs):
    *pieces, dense, turned = refs
    dense[dense.shape[0] - 1] = jnp.zeros(dense.shape[1:], dense.dtype)
    down_blocks(0, hidden, pieces, dense, turned)


def down_second_body(first, index, count, hidden, _, *refs):
    *pieces, out, dense, index_here, slots_sem, turned, sem = refs
    slots = Slots(index, count, index_here, slots_sem)
    slots.copy.start()
    down_blocks(first, hidden, pieces, dense, turned)
    slots.copy.wait()
    zeros = dense.shape[0] - 1
    total = out.shape[0]

    @pl.loop(0, total, unroll=max(n for n in (1, 2, 4, 8) if total % n == 0))
    def _(s):
        place = jnp.where(s < slots.live, slots.index[0, 0, s], zeros)
        pltpu.make_async_copy(dense.at[place], out.at[s], sem).start()

    pltpu.make_async_copy(out, out, sem).wait()


def down_first(pieces, hidden, f_blocks):
    _, tokens, block = hidden.shape
    blocks = f_blocks * (pieces[0].shape[1] // block) + 1
    return pl.pallas_call(
        down_first_body,
        out_shape=pltpu.VMEM((blocks, block, block), BF16),
        in_specs=[WHOLE] * (1 + len(pieces)),
        out_specs=WHOLE,
        scratch_shapes=[pltpu.VMEM((hidden.shape[0] * block, tokens), BF16)],
        compiler_params=params(),
        cost_estimate=cost(blocks * block * block * tokens, 2 * blocks * block * block),
        name="down_first",
    )(hidden, *pieces)


def down_second(index, count, pieces, hidden, dense, slots):
    far_blocks, tokens, block = hidden.shape
    d_blocks = pieces[0].shape[1] // block
    first = (dense.shape[0] - 1) // d_blocks - far_blocks
    out, _ = pl.pallas_call(
        functools.partial(down_second_body, first),
        out_shape=(
            jax.ShapeDtypeStruct((slots, block, block), BF16),
            pltpu.VMEM(dense.shape, BF16),
        ),
        in_specs=[IN_HBM, SCALARS] + [WHOLE] * (2 + len(pieces)),
        out_specs=(IN_HBM, WHOLE),
        scratch_shapes=[
            *Slots.scratch(index),
            pltpu.VMEM((far_blocks * block, tokens), BF16),
            pltpu.SemaphoreType.DMA,
        ],
        input_output_aliases={3: 1},
        compiler_params=params(),
        cost_estimate=cost(slots * block * block * tokens, 2 * slots * block * block),
        name="down_second",
    )(in_hbm(index), count, hidden, resident(dense), *pieces)
    return out


def on_device(
    tokens, cotangent, gate_vals, up_vals, gu_index, gu_count, down_vals, down_index, down_count
):
    block = gate_vals.shape[-1]
    slots = gate_vals.shape[2]
    wide = lax.axis_size("wide")
    narrow = lax.axis_size("narrow")
    chips = wide // 2
    rows = tokens.shape[0]
    d_blocks = tokens.shape[1] // block
    f_blocks = FF // (block * wide)

    def exchange(array):
        return [swap(array, "narrow", narrow, k) for k in range(1, narrow)]

    flips = [chips >> hop for hop in range(1, chips.bit_length())]
    vals = (gate_vals, up_vals)
    x, index = tokens, gu_index
    weights = []
    for hop, flip in enumerate(flips):
        if hop > 0:
            x = jnp.concatenate([x, x_recv], axis=0)
            x, weights, index = lax.optimization_barrier((x, weights, index))
        x_recv = swap(x, "wide", wide, 2 * flip)
        if hop < 2:
            early = (down_count,) if hop == 0 else ()
            weights.append(fill(index, gu_count, vals[hop], d_blocks, f_blocks, early))
    y, index, _ = lax.optimization_barrier((cotangent, down_index, x))
    down_w = fill(index, down_count, down_vals, f_blocks, d_blocks)
    for flip in flips[:-1]:
        y = jnp.concatenate([y, swap(y, "wide", wide, 2 * flip)], axis=0)
    x, down_w = lax.optimization_barrier((x, down_w))
    x_pieces = [x, x_recv, swap(x, "wide", wide, 1), swap(x_recv, "wide", wide, 1)]
    y, _ = lax.optimization_barrier((y, x_recv))
    y_recv = swap(y, "wide", wide, 2 * flips[-1])

    near_own, near_send = gate_up(x_pieces, *weights, 0)
    near_recv = exchange(near_send)
    late, _ = lax.optimization_barrier((x, near_send))
    far_own, far_send = gate_up([late, *x_pieces[1:]], *weights, 1)
    far_recv = exchange(far_send)
    y, y_recv, _ = lax.optimization_barrier((y, y_recv, far_send))
    y_pieces = [y, y_recv, swap(y, "wide", wide, 1), swap(y_recv, "wide", wide, 1)]
    near_hidden, near_coef = activate(near_own, near_recv)
    down_w, near_hidden = lax.optimization_barrier((down_w, near_hidden))
    dh_own, dh_send, turned = d_hidden(y_pieces, x_pieces, down_w)
    y_pieces, dh_send = lax.optimization_barrier((y_pieces, dh_send))
    dh_recv = exchange(dh_send)
    dense = down_first(y_pieces, near_hidden, f_blocks)
    far_own, dense = lax.optimization_barrier((far_own, dense))
    far_hidden, far_coef = activate(far_own, far_recv)
    down_grad = down_second(down_index, down_count, y_pieces, far_hidden, dense, slots)
    down_grad, far_coef = lax.optimization_barrier((down_grad, far_coef))
    halves, d_pair = d_tokens_parts((near_coef, far_coef), dh_own, dh_recv, *weights)

    halves = [own + swap(send, "wide", wide, 1).astype(F32) for own, send in halves]
    kept = chips // 2 * rows
    far = [own[kept:].astype(BF16) for own in halves]
    cut = slots * 2 // 3 if slots % 3 == 0 else slots
    far[1], d_pair = lax.optimization_barrier((far[1], d_pair))
    grads = gu_grads(gu_index, gu_count, d_pair, turned, slots, 0, cut, ())
    halves = [
        own[:kept] + swap(part, "wide", wide, 2 * flips[-1]).astype(F32)
        for own, part in zip(halves, far)
    ]
    own = jnp.concatenate(halves, axis=1)
    sends = [own[p * rows : (p + 1) * rows].astype(BF16) for p in range(1, chips // 2)]
    if cut < slots:
        sends, d_pair, grads = lax.optimization_barrier((sends, d_pair, grads))
        grads = gu_grads(gu_index, gu_count, d_pair, turned, slots, cut, slots, grads)
    own = own[:rows]
    for p, part in enumerate(sends, 1):
        flip = sum(flips[bit] for bit in range(len(flips)) if p >> bit & 1)
        own = own + swap(part, "wide", wide, 2 * flip).astype(F32)
    gate_grad, up_grad = grads
    return (
        own.astype(BF16),
        gate_grad[None, None],
        up_grad[None, None],
        down_grad[None, None],
    )


def solution(mesh):
    in_specs = (
        P("wide", "narrow"),
        P("wide", "narrow"),
        P("narrow", "wide", None, None, None),
        P("narrow", "wide", None, None, None),
        P("narrow", "wide", None),
        P("narrow", "wide"),
        P("wide", "narrow", None, None, None),
        P("wide", "narrow", None),
        P("wide", "narrow"),
    )
    out_specs = (
        P("wide", "narrow"),
        P("narrow", "wide", None, None, None),
        P("narrow", "wide", None, None, None),
        P("wide", "narrow", None, None, None),
    )
    return jax.shard_map(
        on_device, mesh=mesh, in_specs=in_specs, out_specs=out_specs, check_vma=False
    )
```

```python
import functools
import math

import jax
import jax.numpy as jnp
from jax import lax
from jax.experimental import pallas as pl
from jax.experimental.pallas import tpu as pltpu
from jax.sharding import PartitionSpec as P

FF = 16384
F32 = jnp.float32
BF16 = jnp.bfloat16
VMEM_LIMIT = 8 * 1024 * 1024

WHOLE = pl.BlockSpec(memory_space=pltpu.VMEM)
SCALARS = pl.BlockSpec(memory_space=pltpu.SMEM)
IN_HBM = pl.BlockSpec(memory_space=pltpu.HBM)


def params(vmem=VMEM_LIMIT):
    return pltpu.CompilerParams(vmem_limit_bytes=vmem)


def cost(flops, bytes_accessed):
    return pl.CostEstimate(flops=int(flops), bytes_accessed=int(bytes_accessed), transcendentals=0)


def resident(array):
    return pltpu.with_memory_space_constraint(array, pltpu.VMEM)


def in_hbm(array):
    return pltpu.with_memory_space_constraint(array, pltpu.HBM)


def swap(array, axis, size, flip):
    return lax.ppermute(array, axis, [(i, i ^ flip) for i in range(size)])


def split_index(number, size):
    if size & (size - 1):
        return number // size, number % size
    return number >> (size.bit_length() - 1), number & (size - 1)


class Slots:
    def __init__(self, index_from, count, index, sem):
        self.copy = pltpu.make_async_copy(index_from, index, sem)
        self.index, self.live = index, count[0, 0]

    @staticmethod
    def scratch(index):
        return [pltpu.SMEM(index.shape, index.dtype), pltpu.SemaphoreType.DMA]

    def place(self, slot, size):
        return split_index(self.index[0, 0, slot], size)


def fill_body(index, count, source, *refs):
    target, index_here, slots_sem, sem = refs[-4:]
    slots = Slots(index, count, index_here, slots_sem)
    slots.copy.start()
    outer, inner = target.shape[:2]
    chunk = min(inner, 8)

    @pl.loop(0, outer)
    def _(high):
        target[high] = jnp.zeros(target.shape[1:], target.dtype)

    slots.copy.wait()

    def start(s):
        high, low = slots.place(s, inner)
        pltpu.make_async_copy(source.at[0, 0, s], target.at[high, low], sem).start()

    eights, rest = split_index(slots.live, 8)

    @pl.loop(0, eights)
    def _(eight):
        for s in range(8):
            start(eight * 8 + s)

    @pl.loop(0, rest)
    def _(s):
        start(eights * 8 + s)

    many, few = split_index(slots.live, chunk)

    @pl.loop(0, many)
    def _(_):
        blocks = pl.ds(0, chunk)
        pltpu.make_async_copy(source.at[0, 0, blocks], target.at[0, blocks], sem).wait()

    @pl.loop(0, few)
    def _(_):
        pltpu.make_async_copy(source.at[0, 0, 0], target.at[0, 0], sem).wait()


def fill(index, count, slots, outer, inner, early=()):
    block = slots.shape[-1]
    return pl.pallas_call(
        fill_body,
        out_shape=pltpu.VMEM((outer, inner, block, block), BF16),
        in_specs=[IN_HBM, SCALARS, IN_HBM] + [SCALARS] * len(early),
        out_specs=WHOLE,
        scratch_shapes=[*Slots.scratch(index), pltpu.SemaphoreType.DMA],
        compiler_params=params(),
        cost_estimate=cost(0, slots.size * 2),
        name="fill",
    )(in_hbm(index), count, in_hbm(slots), *early)


def stack(pieces):
    return jnp.concatenate([piece[...] for piece in pieces], axis=0)


def gate_up_body(first, *refs):
    *pieces, gate_w, up_w, own, send = refs
    d_blocks, _, block, _ = gate_w.shape
    x = stack(pieces)
    for c in range(own.shape[0]):
        weights = jnp.concatenate(
            [
                gate_w[:, first + c].reshape(d_blocks * block, block),
                up_w[:, first + c].reshape(d_blocks * block, block),
            ],
            axis=1,
        )
        result = jnp.dot(x, weights, preferred_element_type=F32)
        own[c] = result
        send[c] = result.astype(BF16)


def gate_up(pieces, gate_w, up_w, half):
    d_blocks, f_blocks, block, _ = gate_w.shape
    tokens = sum(piece.shape[0] for piece in pieces)
    shape = (f_blocks // 2, tokens, 2 * block)
    return pl.pallas_call(
        functools.partial(gate_up_body, half * f_blocks // 2),
        out_shape=(jax.ShapeDtypeStruct(shape, F32), jax.ShapeDtypeStruct(shape, BF16)),
        in_specs=[WHOLE] * (len(pieces) + 2),
        out_specs=(WHOLE,) * 2,
        compiler_params=params(),
        cost_estimate=cost(2 * tokens * gate_w.size, 2 * gate_w.size),
        name="gate_up",
    )(*pieces, resident(gate_w), resident(up_w))


def d_hidden_body(group, pieces_count, *refs):
    y_pieces, x_pieces = refs[:pieces_count], refs[pieces_count:-5]
    down_w, own, send, x_turned, y_turned = refs[-5:]
    f_blocks, d_blocks, block, _ = down_w.shape
    for d in range(d_blocks):
        at = slice(d * block, (d + 1) * block)
        y_turned[at, :] = jnp.concatenate([piece[:, at] for piece in y_pieces], axis=0).T
    y = y_turned[...]
    for f in range(0, f_blocks, group):
        weights = jnp.concatenate(
            [
                down_w[f : f + group, d].reshape(group * block, block)
                for d in range(d_blocks)
            ],
            axis=1,
        )
        result = jnp.dot(weights, y, preferred_element_type=F32).T
        for side in range(group):
            part = result[:, side * block : (side + 1) * block]
            own[f + side] = part
            send[f + side] = part.astype(BF16)
    for d in range(d_blocks):
        at = slice(d * block, (d + 1) * block)
        x_turned[d] = jnp.concatenate([piece[:, at] for piece in x_pieces], axis=0).T


def d_hidden(y_pieces, x_pieces, down_w):
    f_blocks, d_blocks, block, _ = down_w.shape
    tokens = sum(piece.shape[0] for piece in y_pieces)
    shape = (f_blocks, tokens, block)
    group = max(n for n in (1, 2, 4, 8) if f_blocks % n == 0)
    return pl.pallas_call(
        functools.partial(d_hidden_body, group, len(y_pieces)),
        out_shape=(
            jax.ShapeDtypeStruct(shape, F32),
            jax.ShapeDtypeStruct(shape, BF16),
            jax.ShapeDtypeStruct((d_blocks, block, tokens), BF16),
        ),
        in_specs=[WHOLE] * (len(y_pieces) + len(x_pieces) + 1),
        out_specs=(WHOLE,) * 3,
        scratch_shapes=[pltpu.VMEM((d_blocks * block, tokens), BF16)],
        compiler_params=params(),
        cost_estimate=cost(2 * tokens * down_w.size, 2 * down_w.size),
        name="d_hidden",
    )(*y_pieces, *x_pieces, resident(down_w))


def d_tokens_columns(group, begin, grads, gate_w, up_w, own, send):
    f_blocks, block = gate_w.shape[1:3]
    half = own.shape[0]
    for at in range(0, own.shape[1] // block, group):
        rows = slice(begin + at, begin + at + group)
        weights = jnp.concatenate(
            [
                ref[rows, c].reshape(group * block, block)
                for c in range(f_blocks)
                for ref in (gate_w, up_w)
            ],
            axis=1,
        )
        result = jnp.dot(weights, grads, preferred_element_type=F32).T
        columns = slice(at * block, (at + group) * block)
        own[:, columns] = result[:half]
        send[:, columns] = result[half:].astype(BF16)


def d_tokens_first_body(group, *refs):
    *coef, dh_own = refs[:3]
    *dh_recv, gate_w, up_w, own, send, d_pair, turned = refs[3:]
    f_blocks, block = gate_w.shape[1:3]
    for c in range(f_blocks):
        dh = dh_own[c]
        for part in dh_recv:
            dh = dh + part[c].astype(F32)
        side, at = divmod(c, f_blocks // 2)
        both = (jnp.concatenate([dh, dh], axis=1) * coef[side][at]).astype(BF16)
        d_pair[c] = both
        for side in range(2):
            turned[pl.ds((2 * c + side) * block, block), :] = both[
                :, side * block : (side + 1) * block
            ].T
    d_tokens_columns(group, 0, turned[...], gate_w, up_w, own, send)


def d_tokens_second_body(group, turned, gate_w, up_w, own, send):
    d_blocks = gate_w.shape[0]
    d_tokens_columns(group, d_blocks // 2, turned[...], gate_w, up_w, own, send)


def d_tokens_parts(coef, dh_own, dh_recv, gate_w, up_w):
    d_blocks, f_blocks, block, _ = gate_w.shape
    tokens = dh_own.shape[1]
    half = (tokens // 2, d_blocks // 2 * block)
    group = max(n for n in (1, 2, 4, 8) if d_blocks // 2 % n == 0)
    halves = (jax.ShapeDtypeStruct(half, F32), jax.ShapeDtypeStruct(half, BF16))
    common = dict(
        compiler_params=params(),
        cost_estimate=cost(2 * tokens * gate_w.size, 2 * gate_w.size),
    )
    weights = resident(gate_w), resident(up_w)
    own, send, d_pair, turned = pl.pallas_call(
        functools.partial(d_tokens_first_body, group),
        out_shape=(
            *halves,
            jax.ShapeDtypeStruct((f_blocks, tokens, 2 * block), BF16),
            jax.ShapeDtypeStruct((f_blocks * 2 * block, tokens), BF16),
        ),
        in_specs=[WHOLE] * (5 + len(dh_recv)),
        out_specs=(WHOLE,) * 4,
        name="d_tokens_first",
        **common,
    )(*coef, dh_own, *dh_recv, *weights)
    second = pl.pallas_call(
        functools.partial(d_tokens_second_body, group),
        out_shape=halves,
        in_specs=[WHOLE] * 3,
        out_specs=(WHOLE,) * 2,
        name="d_tokens_second",
        **common,
    )(turned, *weights)
    return ((own, send), second), d_pair


def step_slots(slots):
    return max(n for n in range(1, 33) if slots % n == 0)


def gu_grad_body(first, given, index, count, d_pair, turned, *refs):
    gate_out, up_out, *scalars = refs[given:]
    slots = Slots(index, count, *scalars)
    f_blocks = d_pair.shape[0]
    block = turned.shape[1]
    step = pl.program_id(0)

    @pl.when(step == 0)
    def _():
        slots.copy.start()
        slots.copy.wait()

    chunk = gate_out.shape[0]
    begin = (step + first) * chunk

    def work(masked):
        for j in range(chunk):
            d, f = slots.place(begin + j, f_blocks)
            result = jnp.dot(turned[d], d_pair[f], preferred_element_type=F32)
            if masked:
                result = jnp.where(begin + j < slots.live, result, 0.0)
            result = result.astype(BF16)
            gate_out[j] = result[:, :block]
            up_out[j] = result[:, block:]

    @pl.when(begin + chunk <= slots.live)
    def _():
        work(False)

    @pl.when((begin + chunk > slots.live) & (begin < slots.live))
    def _():
        work(True)

    @pl.when(begin >= slots.live)
    def _():
        gate_out[...] = jnp.zeros(gate_out.shape, gate_out.dtype)
        up_out[...] = jnp.zeros(up_out.shape, up_out.dtype)


def gu_grads(index, count, d_pair, turned, total, begin, end, before):
    block, tokens = turned.shape[1:]
    chunk = step_slots(math.gcd(begin, end))
    first = begin // chunk
    shape = jax.ShapeDtypeStruct((total, block, block), BF16)
    out = pl.BlockSpec((chunk, block, block), lambda i: (i + first, 0, 0))
    size = (end - begin) * block * block
    return pl.pallas_call(
        functools.partial(gu_grad_body, first, len(before)),
        out_shape=(shape,) * 2,
        grid=((end - begin) // chunk,),
        in_specs=[IN_HBM, SCALARS] + [WHOLE] * 2 + [pl.BlockSpec(memory_space=pl.ANY)] * len(before),
        out_specs=(out,) * 2,
        scratch_shapes=Slots.scratch(index),
        input_output_aliases={4 + at: at for at in range(len(before))},
        compiler_params=params(),
        cost_estimate=cost(4 * size * tokens, 4 * size),
        name="gu_grads",
    )(in_hbm(index), count, d_pair, turned, *before)


def activate_body(*refs):
    own, *recv, hidden, coef = refs
    block = hidden.shape[2]
    for f in range(hidden.shape[0]):
        both = own[f]
        for part in recv:
            both = both + part[f].astype(F32)
        gate, up = both[:, :block], both[:, block:]
        sig = jax.nn.sigmoid(gate)
        silu = gate * sig
        hidden[f] = (silu * up).astype(BF16)
        coef[f, :, :block] = up * sig * (1.0 + gate * (1.0 - sig))
        coef[f, :, block:] = silu


def activate(own, recv):
    f_blocks, tokens, pair = own.shape
    return pl.pallas_call(
        activate_body,
        out_shape=(
            jax.ShapeDtypeStruct((f_blocks, tokens, pair // 2), BF16),
            jax.ShapeDtypeStruct(own.shape, F32),
        ),
        in_specs=[WHOLE] * (1 + len(recv)),
        out_specs=(WHOLE,) * 2,
        compiler_params=params(),
        cost_estimate=cost(20 * own.size, 8 * own.size),
        name="activate",
    )(own, *recv)


def down_blocks(first, hidden, pieces, dense, turned):
    f_blocks, tokens, block = hidden.shape
    d_blocks = pieces[0].shape[1] // block
    group = 2 if f_blocks % 2 == 0 else 1
    for f in range(f_blocks):
        turned[f * block : (f + 1) * block, :] = hidden[f].T
    for d in range(0, d_blocks, 2):
        y = jnp.concatenate([piece[:, d * block : (d + 2) * block] for piece in pieces], axis=0)
        for f in range(0, f_blocks, group):
            rows = turned[f * block : (f + group) * block, :]
            result = jnp.dot(rows, y, preferred_element_type=F32).astype(BF16)
            for row in range(group):
                for side in range(2):
                    dense[(first + f + row) * d_blocks + d + side] = result[
                        row * block : (row + 1) * block, side * block : (side + 1) * block
                    ]


def down_first_body(hidden, *refs):
    *pieces, dense, turned = refs
    dense[dense.shape[0] - 1] = jnp.zeros(dense.shape[1:], dense.dtype)
    down_blocks(0, hidden, pieces, dense, turned)


def down_second_body(first, index, count, hidden, _, *refs):
    *pieces, out, dense, index_here, slots_sem, turned, sem = refs
    slots = Slots(index, count, index_here, slots_sem)
    slots.copy.start()
    down_blocks(first, hidden, pieces, dense, turned)
    slots.copy.wait()
    zeros = dense.shape[0] - 1
    total = out.shape[0]

    @pl.loop(0, total, unroll=max(n for n in (1, 2, 4, 8) if total % n == 0))
    def _(s):
        place = jnp.where(s < slots.live, slots.index[0, 0, s], zeros)
        pltpu.make_async_copy(dense.at[place], out.at[s], sem).start()

    pltpu.make_async_copy(out, out, sem).wait()


def down_first(pieces, hidden, f_blocks):
    _, tokens, block = hidden.shape
    blocks = f_blocks * (pieces[0].shape[1] // block) + 1
    return pl.pallas_call(
        down_first_body,
        out_shape=pltpu.VMEM((blocks, block, block), BF16),
        in_specs=[WHOLE] * (1 + len(pieces)),
        out_specs=WHOLE,
        scratch_shapes=[pltpu.VMEM((hidden.shape[0] * block, tokens), BF16)],
        compiler_params=params(),
        cost_estimate=cost(blocks * block * block * tokens, 2 * blocks * block * block),
        name="down_first",
    )(hidden, *pieces)


def down_second(index, count, pieces, hidden, dense, slots):
    far_blocks, tokens, block = hidden.shape
    d_blocks = pieces[0].shape[1] // block
    first = (dense.shape[0] - 1) // d_blocks - far_blocks
    out, _ = pl.pallas_call(
        functools.partial(down_second_body, first),
        out_shape=(
            jax.ShapeDtypeStruct((slots, block, block), BF16),
            pltpu.VMEM(dense.shape, BF16),
        ),
        in_specs=[IN_HBM, SCALARS] + [WHOLE] * (2 + len(pieces)),
        out_specs=(IN_HBM, WHOLE),
        scratch_shapes=[
            *Slots.scratch(index),
            pltpu.VMEM((far_blocks * block, tokens), BF16),
            pltpu.SemaphoreType.DMA,
        ],
        input_output_aliases={3: 1},
        compiler_params=params(),
        cost_estimate=cost(slots * block * block * tokens, 2 * slots * block * block),
        name="down_second",
    )(in_hbm(index), count, hidden, resident(dense), *pieces)
    return out


def on_device(
    tokens, cotangent, gate_vals, up_vals, gu_index, gu_count, down_vals, down_index, down_count
):
    block = gate_vals.shape[-1]
    slots = gate_vals.shape[2]
    wide = lax.axis_size("wide")
    narrow = lax.axis_size("narrow")
    chips = wide // 2
    rows = tokens.shape[0]
    d_blocks = tokens.shape[1] // block
    f_blocks = FF // (block * wide)

    def exchange(array):
        return [swap(array, "narrow", narrow, k) for k in range(1, narrow)]

    flips = [chips >> hop for hop in range(1, chips.bit_length())]
    vals = (gate_vals, up_vals)
    x, index = tokens, gu_index
    weights = []
    for hop, flip in enumerate(flips):
        if hop > 0:
            x = jnp.concatenate([x, x_recv], axis=0)
            x, weights, index = lax.optimization_barrier((x, weights, index))
        x_recv = swap(x, "wide", wide, 2 * flip)
        if hop < 2:
            early = (down_count,) if hop == 1 else ()
            weights.append(fill(index, gu_count, vals[hop], d_blocks, f_blocks, early))
    y, index, _ = lax.optimization_barrier((cotangent, down_index, x))
    down_w = fill(index, down_count, down_vals, f_blocks, d_blocks)
    for flip in flips[:-1]:
        y = jnp.concatenate([y, swap(y, "wide", wide, 2 * flip)], axis=0)
    x, down_w = lax.optimization_barrier((x, down_w))
    x_pieces = [x, x_recv, swap(x, "wide", wide, 1), swap(x_recv, "wide", wide, 1)]
    y, _ = lax.optimization_barrier((y, x_recv))
    y_recv = swap(y, "wide", wide, 2 * flips[-1])

    near_own, near_send = gate_up(x_pieces, *weights, 0)
    near_recv = exchange(near_send)
    late, _ = lax.optimization_barrier((x, near_send))
    far_own, far_send = gate_up([late, *x_pieces[1:]], *weights, 1)
    far_recv = exchange(far_send)
    y, y_recv, _ = lax.optimization_barrier((y, y_recv, far_send))
    y_pieces = [y, y_recv, swap(y, "wide", wide, 1), swap(y_recv, "wide", wide, 1)]
    near_hidden, near_coef = activate(near_own, near_recv)
    down_w, near_hidden = lax.optimization_barrier((down_w, near_hidden))
    dh_own, dh_send, turned = d_hidden(y_pieces, x_pieces, down_w)
    y_pieces, dh_send = lax.optimization_barrier((y_pieces, dh_send))
    dh_recv = exchange(dh_send)
    dense = down_first(y_pieces, near_hidden, f_blocks)
    far_own, dense = lax.optimization_barrier((far_own, dense))
    far_hidden, far_coef = activate(far_own, far_recv)
    down_grad = down_second(down_index, down_count, y_pieces, far_hidden, dense, slots)
    down_grad, far_coef = lax.optimization_barrier((down_grad, far_coef))
    halves, d_pair = d_tokens_parts((near_coef, far_coef), dh_own, dh_recv, *weights)

    halves = [own + swap(send, "wide", wide, 1).astype(F32) for own, send in halves]
    kept = chips // 2 * rows
    far = [own[kept:].astype(BF16) for own in halves]
    cut = slots * 2 // 3 if slots % 3 == 0 else slots
    far[1], d_pair = lax.optimization_barrier((far[1], d_pair))
    grads = gu_grads(gu_index, gu_count, d_pair, turned, slots, 0, cut, ())
    halves = [
        own[:kept] + swap(part, "wide", wide, 2 * flips[-1]).astype(F32)
        for own, part in zip(halves, far)
    ]
    own = jnp.concatenate(halves, axis=1)
    sends = [own[p * rows : (p + 1) * rows].astype(BF16) for p in range(1, chips // 2)]
    if cut < slots:
        sends, d_pair, grads = lax.optimization_barrier((sends, d_pair, grads))
        grads = gu_grads(gu_index, gu_count, d_pair, turned, slots, cut, slots, grads)
    own = own[:rows]
    for p, part in enumerate(sends, 1):
        flip = sum(flips[bit] for bit in range(len(flips)) if p >> bit & 1)
        own = own + swap(part, "wide", wide, 2 * flip).astype(F32)
    gate_grad, up_grad = grads
    return (
        own.astype(BF16),
        gate_grad[None, None],
        up_grad[None, None],
        down_grad[None, None],
    )


def solution(mesh):
    in_specs = (
        P("wide", "narrow"),
        P("wide", "narrow"),
        P("narrow", "wide", None, None, None),
        P("narrow", "wide", None, None, None),
        P("narrow", "wide", None),
        P("narrow", "wide"),
        P("wide", "narrow", None, None, None),
        P("wide", "narrow", None),
        P("wide", "narrow"),
    )
    out_specs = (
        P("wide", "narrow"),
        P("narrow", "wide", None, None, None),
        P("narrow", "wide", None, None, None),
        P("wide", "narrow", None, None, None),
    )
    return jax.shard_map(
        on_device, mesh=mesh, in_specs=in_specs, out_specs=out_specs, check_vma=False
    )
```

```python
import functools
import math

import jax
import jax.numpy as jnp
from jax import lax
from jax.experimental import pallas as pl
from jax.experimental.pallas import tpu as pltpu
from jax.sharding import PartitionSpec as P

FF = 16384
F32 = jnp.float32
BF16 = jnp.bfloat16
VMEM_LIMIT = 8 * 1024 * 1024

WHOLE = pl.BlockSpec(memory_space=pltpu.VMEM)
SCALARS = pl.BlockSpec(memory_space=pltpu.SMEM)
IN_HBM = pl.BlockSpec(memory_space=pltpu.HBM)


def params(vmem=VMEM_LIMIT):
    return pltpu.CompilerParams(vmem_limit_bytes=vmem)


def cost(flops, bytes_accessed):
    return pl.CostEstimate(flops=int(flops), bytes_accessed=int(bytes_accessed), transcendentals=0)


def resident(array):
    return pltpu.with_memory_space_constraint(array, pltpu.VMEM)


def in_hbm(array):
    return pltpu.with_memory_space_constraint(array, pltpu.HBM)


def swap(array, axis, size, flip):
    return lax.ppermute(array, axis, [(i, i ^ flip) for i in range(size)])


def split_index(number, size):
    if size & (size - 1):
        return number // size, number % size
    return number >> (size.bit_length() - 1), number & (size - 1)


class Slots:
    def __init__(self, index_from, count, index, sem):
        self.copy = pltpu.make_async_copy(index_from, index, sem)
        self.index, self.live = index, count[0, 0]

    @staticmethod
    def scratch(index):
        return [pltpu.SMEM(index.shape, index.dtype), pltpu.SemaphoreType.DMA]

    def place(self, slot, size):
        return split_index(self.index[0, 0, slot], size)


def fill_body(index, count, source, *refs):
    target, index_here, slots_sem, sem = refs[-4:]
    slots = Slots(index, count, index_here, slots_sem)
    slots.copy.start()
    outer, inner = target.shape[:2]
    chunk = min(inner, 8)

    @pl.loop(0, outer)
    def _(high):
        target[high] = jnp.zeros(target.shape[1:], target.dtype)

    slots.copy.wait()

    @pl.loop(0, slots.live)
    def _(s):
        high, low = slots.place(s, inner)
        pltpu.make_async_copy(source.at[0, 0, s], target.at[high, low], sem).start()

    many, few = split_index(slots.live, chunk)

    @pl.loop(0, many)
    def _(_):
        blocks = pl.ds(0, chunk)
        pltpu.make_async_copy(source.at[0, 0, blocks], target.at[0, blocks], sem).wait()

    @pl.loop(0, few)
    def _(_):
        pltpu.make_async_copy(source.at[0, 0, 0], target.at[0, 0], sem).wait()


def fill(index, count, slots, outer, inner, early=()):
    block = slots.shape[-1]
    return pl.pallas_call(
        fill_body,
        out_shape=pltpu.VMEM((outer, inner, block, block), BF16),
        in_specs=[IN_HBM, SCALARS, IN_HBM] + [SCALARS] * len(early),
        out_specs=WHOLE,
        scratch_shapes=[*Slots.scratch(index), pltpu.SemaphoreType.DMA],
        compiler_params=params(),
        cost_estimate=cost(0, slots.size * 2),
        name="fill",
    )(in_hbm(index), count, in_hbm(slots), *early)


def stack(pieces):
    return jnp.concatenate([piece[...] for piece in pieces], axis=0)


def gate_up_body(first, *refs):
    *pieces, gate_w, up_w, own, send = refs
    d_blocks, _, block, _ = gate_w.shape
    x = stack(pieces)
    for c in range(own.shape[0]):
        weights = jnp.concatenate(
            [
                gate_w[:, first + c].reshape(d_blocks * block, block),
                up_w[:, first + c].reshape(d_blocks * block, block),
            ],
            axis=1,
        )
        result = jnp.dot(x, weights, preferred_element_type=F32)
        own[c] = result
        send[c] = result.astype(BF16)


def gate_up(pieces, gate_w, up_w, half):
    d_blocks, f_blocks, block, _ = gate_w.shape
    tokens = sum(piece.shape[0] for piece in pieces)
    shape = (f_blocks // 2, tokens, 2 * block)
    return pl.pallas_call(
        functools.partial(gate_up_body, half * f_blocks // 2),
        out_shape=(jax.ShapeDtypeStruct(shape, F32), jax.ShapeDtypeStruct(shape, BF16)),
        in_specs=[WHOLE] * (len(pieces) + 2),
        out_specs=(WHOLE,) * 2,
        compiler_params=params(),
        cost_estimate=cost(2 * tokens * gate_w.size, 2 * gate_w.size),
        name="gate_up",
    )(*pieces, resident(gate_w), resident(up_w))


def d_hidden_body(group, pieces_count, *refs):
    y_pieces, x_pieces = refs[:pieces_count], refs[pieces_count:-5]
    down_w, own, send, x_turned, y_turned = refs[-5:]
    f_blocks, d_blocks, block, _ = down_w.shape
    for d in range(d_blocks):
        at = slice(d * block, (d + 1) * block)
        y_turned[at, :] = jnp.concatenate([piece[:, at] for piece in y_pieces], axis=0).T
    y = y_turned[...]
    for f in range(0, f_blocks, group):
        weights = jnp.concatenate(
            [
                down_w[f : f + group, d].reshape(group * block, block)
                for d in range(d_blocks)
            ],
            axis=1,
        )
        result = jnp.dot(weights, y, preferred_element_type=F32).T
        for side in range(group):
            part = result[:, side * block : (side + 1) * block]
            own[f + side] = part
            send[f + side] = part.astype(BF16)
    for d in range(d_blocks):
        at = slice(d * block, (d + 1) * block)
        x_turned[d] = jnp.concatenate([piece[:, at] for piece in x_pieces], axis=0).T


def d_hidden(y_pieces, x_pieces, down_w):
    f_blocks, d_blocks, block, _ = down_w.shape
    tokens = sum(piece.shape[0] for piece in y_pieces)
    shape = (f_blocks, tokens, block)
    group = max(n for n in (1, 2, 4, 8) if f_blocks % n == 0)
    return pl.pallas_call(
        functools.partial(d_hidden_body, group, len(y_pieces)),
        out_shape=(
            jax.ShapeDtypeStruct(shape, F32),
            jax.ShapeDtypeStruct(shape, BF16),
            jax.ShapeDtypeStruct((d_blocks, block, tokens), BF16),
        ),
        in_specs=[WHOLE] * (len(y_pieces) + len(x_pieces) + 1),
        out_specs=(WHOLE,) * 3,
        scratch_shapes=[pltpu.VMEM((d_blocks * block, tokens), BF16)],
        compiler_params=params(),
        cost_estimate=cost(2 * tokens * down_w.size, 2 * down_w.size),
        name="d_hidden",
    )(*y_pieces, *x_pieces, resident(down_w))


def d_tokens_columns(group, begin, grads, gate_w, up_w, own, send):
    f_blocks, block = gate_w.shape[1:3]
    half = own.shape[0]
    for at in range(0, own.shape[1] // block, group):
        rows = slice(begin + at, begin + at + group)
        weights = jnp.concatenate(
            [
                ref[rows, c].reshape(group * block, block)
                for c in range(f_blocks)
                for ref in (gate_w, up_w)
            ],
            axis=1,
        )
        result = jnp.dot(weights, grads, preferred_element_type=F32).T
        columns = slice(at * block, (at + group) * block)
        own[:, columns] = result[:half]
        send[:, columns] = result[half:].astype(BF16)


def d_tokens_first_body(group, *refs):
    *coef, dh_own = refs[:3]
    *dh_recv, gate_w, up_w, own, send, d_pair, turned = refs[3:]
    f_blocks, block = gate_w.shape[1:3]
    for c in range(f_blocks):
        dh = dh_own[c]
        for part in dh_recv:
            dh = dh + part[c].astype(F32)
        side, at = divmod(c, f_blocks // 2)
        both = (jnp.concatenate([dh, dh], axis=1) * coef[side][at]).astype(BF16)
        d_pair[c] = both
        for side in range(2):
            turned[pl.ds((2 * c + side) * block, block), :] = both[
                :, side * block : (side + 1) * block
            ].T
    d_tokens_columns(group, 0, turned[...], gate_w, up_w, own, send)


def d_tokens_second_body(group, turned, gate_w, up_w, own, send):
    d_blocks = gate_w.shape[0]
    d_tokens_columns(group, d_blocks // 2, turned[...], gate_w, up_w, own, send)


def d_tokens_parts(coef, dh_own, dh_recv, gate_w, up_w):
    d_blocks, f_blocks, block, _ = gate_w.shape
    tokens = dh_own.shape[1]
    half = (tokens // 2, d_blocks // 2 * block)
    group = max(n for n in (1, 2, 4, 8) if d_blocks // 2 % n == 0)
    halves = (jax.ShapeDtypeStruct(half, F32), jax.ShapeDtypeStruct(half, BF16))
    common = dict(
        compiler_params=params(),
        cost_estimate=cost(2 * tokens * gate_w.size, 2 * gate_w.size),
    )
    weights = resident(gate_w), resident(up_w)
    own, send, d_pair, turned = pl.pallas_call(
        functools.partial(d_tokens_first_body, group),
        out_shape=(
            *halves,
            jax.ShapeDtypeStruct((f_blocks, tokens, 2 * block), BF16),
            jax.ShapeDtypeStruct((f_blocks * 2 * block, tokens), BF16),
        ),
        in_specs=[WHOLE] * (5 + len(dh_recv)),
        out_specs=(WHOLE,) * 4,
        name="d_tokens_first",
        **common,
    )(*coef, dh_own, *dh_recv, *weights)
    second = pl.pallas_call(
        functools.partial(d_tokens_second_body, group),
        out_shape=halves,
        in_specs=[WHOLE] * 3,
        out_specs=(WHOLE,) * 2,
        name="d_tokens_second",
        **common,
    )(turned, *weights)
    return ((own, send), second), d_pair


def step_slots(slots):
    return max(n for n in range(1, 33) if slots % n == 0)


def gu_grad_body(first, given, index, count, d_pair, turned, *refs):
    gate_out, up_out, *scalars = refs[given:]
    slots = Slots(index, count, *scalars)
    f_blocks = d_pair.shape[0]
    block = turned.shape[1]
    step = pl.program_id(0)

    @pl.when(step == 0)
    def _():
        slots.copy.start()
        slots.copy.wait()

    chunk = gate_out.shape[0]
    begin = (step + first) * chunk

    def work(masked):
        for j in range(chunk):
            d, f = slots.place(begin + j, f_blocks)
            result = jnp.dot(turned[d], d_pair[f], preferred_element_type=F32)
            if masked:
                result = jnp.where(begin + j < slots.live, result, 0.0)
            result = result.astype(BF16)
            gate_out[j] = result[:, :block]
            up_out[j] = result[:, block:]

    @pl.when(begin + chunk <= slots.live)
    def _():
        work(False)

    @pl.when((begin + chunk > slots.live) & (begin < slots.live))
    def _():
        work(True)

    @pl.when(begin >= slots.live)
    def _():
        gate_out[...] = jnp.zeros(gate_out.shape, gate_out.dtype)
        up_out[...] = jnp.zeros(up_out.shape, up_out.dtype)


def gu_grads(index, count, d_pair, turned, total, begin, end, before):
    block, tokens = turned.shape[1:]
    chunk = step_slots(math.gcd(begin, end))
    first = begin // chunk
    shape = jax.ShapeDtypeStruct((total, block, block), BF16)
    out = pl.BlockSpec((chunk, block, block), lambda i: (i + first, 0, 0))
    size = (end - begin) * block * block
    return pl.pallas_call(
        functools.partial(gu_grad_body, first, len(before)),
        out_shape=(shape,) * 2,
        grid=((end - begin) // chunk,),
        in_specs=[IN_HBM, SCALARS] + [WHOLE] * 2 + [pl.BlockSpec(memory_space=pl.ANY)] * len(before),
        out_specs=(out,) * 2,
        scratch_shapes=Slots.scratch(index),
        input_output_aliases={4 + at: at for at in range(len(before))},
        compiler_params=params(),
        cost_estimate=cost(4 * size * tokens, 4 * size),
        name="gu_grads",
    )(in_hbm(index), count, d_pair, turned, *before)


def activate_body(*refs):
    own, *recv, hidden, coef = refs
    block = hidden.shape[2]
    for f in range(hidden.shape[0]):
        both = own[f]
        for part in recv:
            both = both + part[f].astype(F32)
        gate, up = both[:, :block], both[:, block:]
        sig = jax.nn.sigmoid(gate)
        silu = gate * sig
        hidden[f] = (silu * up).astype(BF16)
        coef[f, :, :block] = up * sig * (1.0 + gate * (1.0 - sig))
        coef[f, :, block:] = silu


def activate(own, recv):
    f_blocks, tokens, pair = own.shape
    return pl.pallas_call(
        activate_body,
        out_shape=(
            jax.ShapeDtypeStruct((f_blocks, tokens, pair // 2), BF16),
            jax.ShapeDtypeStruct(own.shape, F32),
        ),
        in_specs=[WHOLE] * (1 + len(recv)),
        out_specs=(WHOLE,) * 2,
        compiler_params=params(),
        cost_estimate=cost(20 * own.size, 8 * own.size),
        name="activate",
    )(own, *recv)


def down_blocks(first, hidden, pieces, dense, turned):
    f_blocks, tokens, block = hidden.shape
    d_blocks = pieces[0].shape[1] // block
    group = 2 if f_blocks % 2 == 0 else 1
    for f in range(f_blocks):
        turned[f * block : (f + 1) * block, :] = hidden[f].T
    for d in range(0, d_blocks, 2):
        y = jnp.concatenate([piece[:, d * block : (d + 2) * block] for piece in pieces], axis=0)
        for f in range(0, f_blocks, group):
            rows = turned[f * block : (f + group) * block, :]
            result = jnp.dot(rows, y, preferred_element_type=F32).astype(BF16)
            for row in range(group):
                for side in range(2):
                    dense[(first + f + row) * d_blocks + d + side] = result[
                        row * block : (row + 1) * block, side * block : (side + 1) * block
                    ]


def down_first_body(hidden, *refs):
    *pieces, dense, turned = refs
    dense[dense.shape[0] - 1] = jnp.zeros(dense.shape[1:], dense.dtype)
    down_blocks(0, hidden, pieces, dense, turned)


def down_second_body(first, index, count, hidden, _, *refs):
    *pieces, out, dense, index_here, slots_sem, turned, sem = refs
    slots = Slots(index, count, index_here, slots_sem)
    slots.copy.start()
    down_blocks(first, hidden, pieces, dense, turned)
    slots.copy.wait()
    zeros = dense.shape[0] - 1
    total = out.shape[0]

    @pl.loop(0, total, unroll=max(n for n in (1, 2, 4, 8) if total % n == 0))
    def _(s):
        place = jnp.where(s < slots.live, slots.index[0, 0, s], zeros)
        pltpu.make_async_copy(dense.at[place], out.at[s], sem).start()

    pltpu.make_async_copy(out, out, sem).wait()


def down_first(pieces, hidden, f_blocks):
    _, tokens, block = hidden.shape
    blocks = f_blocks * (pieces[0].shape[1] // block) + 1
    return pl.pallas_call(
        down_first_body,
        out_shape=pltpu.VMEM((blocks, block, block), BF16),
        in_specs=[WHOLE] * (1 + len(pieces)),
        out_specs=WHOLE,
        scratch_shapes=[pltpu.VMEM((hidden.shape[0] * block, tokens), BF16)],
        compiler_params=params(),
        cost_estimate=cost(blocks * block * block * tokens, 2 * blocks * block * block),
        name="down_first",
    )(hidden, *pieces)


def down_second(index, count, pieces, hidden, dense, slots):
    far_blocks, tokens, block = hidden.shape
    d_blocks = pieces[0].shape[1] // block
    first = (dense.shape[0] - 1) // d_blocks - far_blocks
    out, _ = pl.pallas_call(
        functools.partial(down_second_body, first),
        out_shape=(
            jax.ShapeDtypeStruct((slots, block, block), BF16),
            pltpu.VMEM(dense.shape, BF16),
        ),
        in_specs=[IN_HBM, SCALARS] + [WHOLE] * (2 + len(pieces)),
        out_specs=(IN_HBM, WHOLE),
        scratch_shapes=[
            *Slots.scratch(index),
            pltpu.VMEM((far_blocks * block, tokens), BF16),
            pltpu.SemaphoreType.DMA,
        ],
        input_output_aliases={3: 1},
        compiler_params=params(),
        cost_estimate=cost(slots * block * block * tokens, 2 * slots * block * block),
        name="down_second",
    )(in_hbm(index), count, hidden, resident(dense), *pieces)
    return out


def on_device(
    tokens, cotangent, gate_vals, up_vals, gu_index, gu_count, down_vals, down_index, down_count
):
    block = gate_vals.shape[-1]
    slots = gate_vals.shape[2]
    wide = lax.axis_size("wide")
    narrow = lax.axis_size("narrow")
    chips = wide // 2
    rows = tokens.shape[0]
    d_blocks = tokens.shape[1] // block
    f_blocks = FF // (block * wide)

    def exchange(array):
        return [swap(array, "narrow", narrow, k) for k in range(1, narrow)]

    flips = [chips >> hop for hop in range(1, chips.bit_length())]
    vals = (gate_vals, up_vals)
    x, index = tokens, gu_index
    weights = []
    for hop, flip in enumerate(flips):
        if hop > 0:
            x = jnp.concatenate([x, x_recv], axis=0)
            x, weights, index = lax.optimization_barrier((x, weights, index))
        x_recv = swap(x, "wide", wide, 2 * flip)
        if hop < 2:
            early = (down_count,) if hop == 0 else ()
            weights.append(fill(index, gu_count, vals[hop], d_blocks, f_blocks, early))
    y, index, _ = lax.optimization_barrier((cotangent, down_index, x))
    down_w = fill(index, down_count, down_vals, f_blocks, d_blocks)
    for flip in flips[:-1]:
        y = jnp.concatenate([y, swap(y, "wide", wide, 2 * flip)], axis=0)
    x, down_w = lax.optimization_barrier((x, down_w))
    x_pieces = [x, x_recv, swap(x, "wide", wide, 1), swap(x_recv, "wide", wide, 1)]

    near_own, near_send = gate_up(x_pieces, *weights, 0)
    near_recv = exchange(near_send)
    late, y, _ = lax.optimization_barrier((x, y, near_send))
    y_recv = swap(y, "wide", wide, 2 * flips[-1])
    far_own, far_send = gate_up([late, *x_pieces[1:]], *weights, 1)
    far_recv = exchange(far_send)
    y, y_recv, _ = lax.optimization_barrier((y, y_recv, far_send))
    y_pieces = [y, y_recv, swap(y, "wide", wide, 1), swap(y_recv, "wide", wide, 1)]
    near_hidden, near_coef = activate(near_own, near_recv)
    down_w, near_hidden = lax.optimization_barrier((down_w, near_hidden))
    dh_own, dh_send, turned = d_hidden(y_pieces, x_pieces, down_w)
    y_pieces, dh_send = lax.optimization_barrier((y_pieces, dh_send))
    dh_recv = exchange(dh_send)
    dense = down_first(y_pieces, near_hidden, f_blocks)
    far_own, dense = lax.optimization_barrier((far_own, dense))
    far_hidden, far_coef = activate(far_own, far_recv)
    down_grad = down_second(down_index, down_count, y_pieces, far_hidden, dense, slots)
    down_grad, far_coef = lax.optimization_barrier((down_grad, far_coef))
    halves, d_pair = d_tokens_parts((near_coef, far_coef), dh_own, dh_recv, *weights)

    halves = [own + swap(send, "wide", wide, 1).astype(F32) for own, send in halves]
    kept = chips // 2 * rows
    far = [own[kept:].astype(BF16) for own in halves]
    cut = slots * 2 // 3 if slots % 3 == 0 else slots
    far[1], d_pair = lax.optimization_barrier((far[1], d_pair))
    grads = gu_grads(gu_index, gu_count, d_pair, turned, slots, 0, cut, ())
    halves = [
        own[:kept] + swap(part, "wide", wide, 2 * flips[-1]).astype(F32)
        for own, part in zip(halves, far)
    ]
    own = jnp.concatenate(halves, axis=1)
    sends = [own[p * rows : (p + 1) * rows].astype(BF16) for p in range(1, chips // 2)]
    if cut < slots:
        sends, d_pair, grads = lax.optimization_barrier((sends, d_pair, grads))
        grads = gu_grads(gu_index, gu_count, d_pair, turned, slots, cut, slots, grads)
    own = own[:rows]
    for p, part in enumerate(sends, 1):
        flip = sum(flips[bit] for bit in range(len(flips)) if p >> bit & 1)
        own = own + swap(part, "wide", wide, 2 * flip).astype(F32)
    gate_grad, up_grad = grads
    return (
        own.astype(BF16),
        gate_grad[None, None],
        up_grad[None, None],
        down_grad[None, None],
    )


def solution(mesh):
    in_specs = (
        P("wide", "narrow"),
        P("wide", "narrow"),
        P("narrow", "wide", None, None, None),
        P("narrow", "wide", None, None, None),
        P("narrow", "wide", None),
        P("narrow", "wide"),
        P("wide", "narrow", None, None, None),
        P("wide", "narrow", None),
        P("wide", "narrow"),
    )
    out_specs = (
        P("wide", "narrow"),
        P("narrow", "wide", None, None, None),
        P("narrow", "wide", None, None, None),
        P("wide", "narrow", None, None, None),
    )
    return jax.shard_map(
        on_device, mesh=mesh, in_specs=in_specs, out_specs=out_specs, check_vma=False
    )
```

```python
import functools
import math

import jax
import jax.numpy as jnp
from jax import lax
from jax.experimental import pallas as pl
from jax.experimental.pallas import tpu as pltpu
from jax.sharding import PartitionSpec as P

FF = 16384
F32 = jnp.float32
BF16 = jnp.bfloat16
VMEM_LIMIT = 8 * 1024 * 1024

WHOLE = pl.BlockSpec(memory_space=pltpu.VMEM)
SCALARS = pl.BlockSpec(memory_space=pltpu.SMEM)
IN_HBM = pl.BlockSpec(memory_space=pltpu.HBM)


def params(vmem=VMEM_LIMIT):
    return pltpu.CompilerParams(vmem_limit_bytes=vmem)


def cost(flops, bytes_accessed):
    return pl.CostEstimate(flops=int(flops), bytes_accessed=int(bytes_accessed), transcendentals=0)


def resident(array):
    return pltpu.with_memory_space_constraint(array, pltpu.VMEM)


def in_hbm(array):
    return pltpu.with_memory_space_constraint(array, pltpu.HBM)


def swap(array, axis, size, flip):
    return lax.ppermute(array, axis, [(i, i ^ flip) for i in range(size)])


def split_index(number, size):
    if size & (size - 1):
        return number // size, number % size
    return number >> (size.bit_length() - 1), number & (size - 1)


class Slots:
    def __init__(self, index_from, count, index, sem):
        self.copy = pltpu.make_async_copy(index_from, index, sem)
        self.index, self.live = index, count[0, 0]

    @staticmethod
    def scratch(index):
        return [pltpu.SMEM(index.shape, index.dtype), pltpu.SemaphoreType.DMA]

    def place(self, slot, size):
        return split_index(self.index[0, 0, slot], size)


def fill_body(index, count, source, *refs):
    target, index_here, slots_sem, sem = refs[-4:]
    slots = Slots(index, count, index_here, slots_sem)
    slots.copy.start()
    outer, inner = target.shape[:2]
    chunk = min(inner, 8)

    @pl.loop(0, outer)
    def _(high):
        target[high] = jnp.zeros(target.shape[1:], target.dtype)

    slots.copy.wait()

    @pl.loop(0, slots.live)
    def _(s):
        high, low = slots.place(s, inner)
        pltpu.make_async_copy(source.at[0, 0, s], target.at[high, low], sem).start()

    many, few = split_index(slots.live, chunk)

    @pl.loop(0, many)
    def _(_):
        blocks = pl.ds(0, chunk)
        pltpu.make_async_copy(source.at[0, 0, blocks], target.at[0, blocks], sem).wait()

    @pl.loop(0, few)
    def _(_):
        pltpu.make_async_copy(source.at[0, 0, 0], target.at[0, 0], sem).wait()


def fill(index, count, slots, outer, inner, early=()):
    block = slots.shape[-1]
    return pl.pallas_call(
        fill_body,
        out_shape=pltpu.VMEM((outer, inner, block, block), BF16),
        in_specs=[IN_HBM, SCALARS, IN_HBM] + [SCALARS] * len(early),
        out_specs=WHOLE,
        scratch_shapes=[*Slots.scratch(index), pltpu.SemaphoreType.DMA],
        compiler_params=params(),
        cost_estimate=cost(0, slots.size * 2),
        name="fill",
    )(in_hbm(index), count, in_hbm(slots), *early)


def stack(pieces):
    return jnp.concatenate([piece[...] for piece in pieces], axis=0)


def gate_up_body(first, *refs):
    *pieces, gate_w, up_w, own, send = refs
    d_blocks, _, block, _ = gate_w.shape
    x = stack(pieces)
    for c in range(own.shape[0]):
        weights = jnp.concatenate(
            [
                gate_w[:, first + c].reshape(d_blocks * block, block),
                up_w[:, first + c].reshape(d_blocks * block, block),
            ],
            axis=1,
        )
        result = jnp.dot(x, weights, preferred_element_type=F32)
        own[c] = result
        send[c] = result.astype(BF16)


def gate_up(pieces, gate_w, up_w, half):
    d_blocks, f_blocks, block, _ = gate_w.shape
    tokens = sum(piece.shape[0] for piece in pieces)
    shape = (f_blocks // 2, tokens, 2 * block)
    return pl.pallas_call(
        functools.partial(gate_up_body, half * f_blocks // 2),
        out_shape=(jax.ShapeDtypeStruct(shape, F32), jax.ShapeDtypeStruct(shape, BF16)),
        in_specs=[WHOLE] * (len(pieces) + 2),
        out_specs=(WHOLE,) * 2,
        compiler_params=params(),
        cost_estimate=cost(2 * tokens * gate_w.size, 2 * gate_w.size),
        name="gate_up",
    )(*pieces, resident(gate_w), resident(up_w))


def d_hidden_body(group, pieces_count, *refs):
    y_pieces, x_pieces = refs[:pieces_count], refs[pieces_count:-5]
    down_w, own, send, x_turned, y_turned = refs[-5:]
    f_blocks, d_blocks, block, _ = down_w.shape
    for d in range(d_blocks):
        at = slice(d * block, (d + 1) * block)
        y_turned[at, :] = jnp.concatenate([piece[:, at] for piece in y_pieces], axis=0).T
    y = y_turned[...]
    for f in range(0, f_blocks, group):
        weights = jnp.concatenate(
            [
                down_w[f : f + group, d].reshape(group * block, block)
                for d in range(d_blocks)
            ],
            axis=1,
        )
        result = jnp.dot(weights, y, preferred_element_type=F32).T
        for side in range(group):
            part = result[:, side * block : (side + 1) * block]
            own[f + side] = part
            send[f + side] = part.astype(BF16)
    for d in range(d_blocks):
        at = slice(d * block, (d + 1) * block)
        x_turned[d] = jnp.concatenate([piece[:, at] for piece in x_pieces], axis=0).T


def d_hidden(y_pieces, x_pieces, down_w):
    f_blocks, d_blocks, block, _ = down_w.shape
    tokens = sum(piece.shape[0] for piece in y_pieces)
    shape = (f_blocks, tokens, block)
    group = max(n for n in (1, 2, 4, 8) if f_blocks % n == 0)
    return pl.pallas_call(
        functools.partial(d_hidden_body, group, len(y_pieces)),
        out_shape=(
            jax.ShapeDtypeStruct(shape, F32),
            jax.ShapeDtypeStruct(shape, BF16),
            jax.ShapeDtypeStruct((d_blocks, block, tokens), BF16),
        ),
        in_specs=[WHOLE] * (len(y_pieces) + len(x_pieces) + 1),
        out_specs=(WHOLE,) * 3,
        scratch_shapes=[pltpu.VMEM((d_blocks * block, tokens), BF16)],
        compiler_params=params(),
        cost_estimate=cost(2 * tokens * down_w.size, 2 * down_w.size),
        name="d_hidden",
    )(*y_pieces, *x_pieces, resident(down_w))


def d_tokens_columns(group, begin, grads, gate_w, up_w, own, send):
    f_blocks, block = gate_w.shape[1:3]
    half = own.shape[0]
    for at in range(0, own.shape[1] // block, group):
        rows = slice(begin + at, begin + at + group)
        weights = jnp.concatenate(
            [
                ref[rows, c].reshape(group * block, block)
                for c in range(f_blocks)
                for ref in (gate_w, up_w)
            ],
            axis=1,
        )
        result = jnp.dot(weights, grads, preferred_element_type=F32).T
        columns = slice(at * block, (at + group) * block)
        own[:, columns] = result[:half]
        send[:, columns] = result[half:].astype(BF16)


def d_tokens_first_body(group, *refs):
    *coef, dh_own = refs[:3]
    *dh_recv, gate_w, up_w, own, send, d_pair, turned = refs[3:]
    f_blocks, block = gate_w.shape[1:3]
    for c in range(f_blocks):
        dh = dh_own[c]
        for part in dh_recv:
            dh = dh + part[c].astype(F32)
        side, at = divmod(c, f_blocks // 2)
        both = (jnp.concatenate([dh, dh], axis=1) * coef[side][at]).astype(BF16)
        d_pair[c] = both
        for side in range(2):
            turned[pl.ds((2 * c + side) * block, block), :] = both[
                :, side * block : (side + 1) * block
            ].T
    d_tokens_columns(group, 0, turned[...], gate_w, up_w, own, send)


def d_tokens_second_body(group, turned, gate_w, up_w, own, send):
    d_blocks = gate_w.shape[0]
    d_tokens_columns(group, d_blocks // 2, turned[...], gate_w, up_w, own, send)


def d_tokens_parts(coef, dh_own, dh_recv, gate_w, up_w):
    d_blocks, f_blocks, block, _ = gate_w.shape
    tokens = dh_own.shape[1]
    half = (tokens // 2, d_blocks // 2 * block)
    group = max(n for n in (1, 2, 4, 8) if d_blocks // 2 % n == 0)
    halves = (jax.ShapeDtypeStruct(half, F32), jax.ShapeDtypeStruct(half, BF16))
    common = dict(
        compiler_params=params(),
        cost_estimate=cost(2 * tokens * gate_w.size, 2 * gate_w.size),
    )
    weights = resident(gate_w), resident(up_w)
    own, send, d_pair, turned = pl.pallas_call(
        functools.partial(d_tokens_first_body, group),
        out_shape=(
            *halves,
            jax.ShapeDtypeStruct((f_blocks, tokens, 2 * block), BF16),
            jax.ShapeDtypeStruct((f_blocks * 2 * block, tokens), BF16),
        ),
        in_specs=[WHOLE] * (5 + len(dh_recv)),
        out_specs=(WHOLE,) * 4,
        name="d_tokens_first",
        **common,
    )(*coef, dh_own, *dh_recv, *weights)
    second = pl.pallas_call(
        functools.partial(d_tokens_second_body, group),
        out_shape=halves,
        in_specs=[WHOLE] * 3,
        out_specs=(WHOLE,) * 2,
        name="d_tokens_second",
        **common,
    )(turned, *weights)
    return ((own, send), second), d_pair


def step_slots(slots):
    return max(n for n in range(1, 33) if slots % n == 0)


def gu_grad_body(first, given, index, count, d_pair, turned, *refs):
    gate_out, up_out, *scalars = refs[given:]
    slots = Slots(index, count, *scalars)
    f_blocks = d_pair.shape[0]
    block = turned.shape[1]
    step = pl.program_id(0)

    @pl.when(step == 0)
    def _():
        slots.copy.start()
        slots.copy.wait()

    chunk = gate_out.shape[0]
    begin = (step + first) * chunk

    def work(masked):
        for j in range(chunk):
            d, f = slots.place(begin + j, f_blocks)
            result = jnp.dot(turned[d], d_pair[f], preferred_element_type=F32)
            if masked:
                result = jnp.where(begin + j < slots.live, result, 0.0)
            result = result.astype(BF16)
            gate_out[j] = result[:, :block]
            up_out[j] = result[:, block:]

    @pl.when(begin + chunk <= slots.live)
    def _():
        work(False)

    @pl.when((begin + chunk > slots.live) & (begin < slots.live))
    def _():
        work(True)

    @pl.when(begin >= slots.live)
    def _():
        gate_out[...] = jnp.zeros(gate_out.shape, gate_out.dtype)
        up_out[...] = jnp.zeros(up_out.shape, up_out.dtype)


def gu_grads(index, count, d_pair, turned, total, begin, end, before):
    block, tokens = turned.shape[1:]
    chunk = step_slots(math.gcd(begin, end))
    first = begin // chunk
    shape = jax.ShapeDtypeStruct((total, block, block), BF16)
    out = pl.BlockSpec((chunk, block, block), lambda i: (i + first, 0, 0))
    size = (end - begin) * block * block
    return pl.pallas_call(
        functools.partial(gu_grad_body, first, len(before)),
        out_shape=(shape,) * 2,
        grid=((end - begin) // chunk,),
        in_specs=[IN_HBM, SCALARS] + [WHOLE] * 2 + [pl.BlockSpec(memory_space=pl.ANY)] * len(before),
        out_specs=(out,) * 2,
        scratch_shapes=Slots.scratch(index),
        input_output_aliases={4 + at: at for at in range(len(before))},
        compiler_params=params(),
        cost_estimate=cost(4 * size * tokens, 4 * size),
        name="gu_grads",
    )(in_hbm(index), count, d_pair, turned, *before)


def activate_body(*refs):
    own, *recv, hidden, coef = refs
    block = hidden.shape[2]
    for f in range(hidden.shape[0]):
        both = own[f]
        for part in recv:
            both = both + part[f].astype(F32)
        gate, up = both[:, :block], both[:, block:]
        sig = jax.nn.sigmoid(gate)
        silu = gate * sig
        hidden[f] = (silu * up).astype(BF16)
        coef[f, :, :block] = up * sig * (1.0 + gate * (1.0 - sig))
        coef[f, :, block:] = silu


def activate(own, recv):
    f_blocks, tokens, pair = own.shape
    return pl.pallas_call(
        activate_body,
        out_shape=(
            jax.ShapeDtypeStruct((f_blocks, tokens, pair // 2), BF16),
            jax.ShapeDtypeStruct(own.shape, F32),
        ),
        in_specs=[WHOLE] * (1 + len(recv)),
        out_specs=(WHOLE,) * 2,
        compiler_params=params(),
        cost_estimate=cost(20 * own.size, 8 * own.size),
        name="activate",
    )(own, *recv)


def down_blocks(first, hidden, pieces, dense, turned):
    f_blocks, tokens, block = hidden.shape
    d_blocks = pieces[0].shape[1] // block
    group = 2 if f_blocks % 2 == 0 else 1
    for f in range(f_blocks):
        turned[f * block : (f + 1) * block, :] = hidden[f].T
    for d in range(0, d_blocks, 2):
        y = jnp.concatenate([piece[:, d * block : (d + 2) * block] for piece in pieces], axis=0)
        for f in range(0, f_blocks, group):
            rows = turned[f * block : (f + group) * block, :]
            result = jnp.dot(rows, y, preferred_element_type=F32).astype(BF16)
            for row in range(group):
                for side in range(2):
                    dense[(first + f + row) * d_blocks + d + side] = result[
                        row * block : (row + 1) * block, side * block : (side + 1) * block
                    ]


def down_first_body(hidden, *refs):
    *pieces, dense, turned = refs
    dense[dense.shape[0] - 1] = jnp.zeros(dense.shape[1:], dense.dtype)
    down_blocks(0, hidden, pieces, dense, turned)


def down_second_body(first, index, count, hidden, _, *refs):
    *pieces, out, dense, index_here, slots_sem, turned, sem = refs
    slots = Slots(index, count, index_here, slots_sem)
    slots.copy.start()
    down_blocks(first, hidden, pieces, dense, turned)
    slots.copy.wait()
    zeros = dense.shape[0] - 1
    total = out.shape[0]

    @pl.loop(0, total, unroll=max(n for n in (1, 2, 4, 8) if total % n == 0))
    def _(s):
        place = jnp.where(s < slots.live, slots.index[0, 0, s], zeros)
        pltpu.make_async_copy(dense.at[place], out.at[s], sem).start()

    pltpu.make_async_copy(out, out, sem).wait()


def down_first(pieces, hidden, f_blocks):
    _, tokens, block = hidden.shape
    blocks = f_blocks * (pieces[0].shape[1] // block) + 1
    return pl.pallas_call(
        down_first_body,
        out_shape=pltpu.VMEM((blocks, block, block), BF16),
        in_specs=[WHOLE] * (1 + len(pieces)),
        out_specs=WHOLE,
        scratch_shapes=[pltpu.VMEM((hidden.shape[0] * block, tokens), BF16)],
        compiler_params=params(),
        cost_estimate=cost(blocks * block * block * tokens, 2 * blocks * block * block),
        name="down_first",
    )(hidden, *pieces)


def down_second(index, count, pieces, hidden, dense, slots):
    far_blocks, tokens, block = hidden.shape
    d_blocks = pieces[0].shape[1] // block
    first = (dense.shape[0] - 1) // d_blocks - far_blocks
    out, _ = pl.pallas_call(
        functools.partial(down_second_body, first),
        out_shape=(
            jax.ShapeDtypeStruct((slots, block, block), BF16),
            pltpu.VMEM(dense.shape, BF16),
        ),
        in_specs=[IN_HBM, SCALARS] + [WHOLE] * (2 + len(pieces)),
        out_specs=(IN_HBM, WHOLE),
        scratch_shapes=[
            *Slots.scratch(index),
            pltpu.VMEM((far_blocks * block, tokens), BF16),
            pltpu.SemaphoreType.DMA,
        ],
        input_output_aliases={3: 1},
        compiler_params=params(),
        cost_estimate=cost(slots * block * block * tokens, 2 * slots * block * block),
        name="down_second",
    )(in_hbm(index), count, hidden, resident(dense), *pieces)
    return out


def on_device(
    tokens, cotangent, gate_vals, up_vals, gu_index, gu_count, down_vals, down_index, down_count
):
    block = gate_vals.shape[-1]
    slots = gate_vals.shape[2]
    wide = lax.axis_size("wide")
    narrow = lax.axis_size("narrow")
    chips = wide // 2
    rows = tokens.shape[0]
    d_blocks = tokens.shape[1] // block
    f_blocks = FF // (block * wide)

    def exchange(array):
        return [swap(array, "narrow", narrow, k) for k in range(1, narrow)]

    flips = [chips >> hop for hop in range(1, chips.bit_length())]
    vals = (gate_vals, up_vals)
    x, index = tokens, gu_index
    weights = []
    for hop, flip in enumerate(flips):
        if hop > 0:
            x = jnp.concatenate([x, x_recv], axis=0)
            x, weights, index = lax.optimization_barrier((x, weights, index))
        x_recv = swap(x, "wide", wide, 2 * flip)
        if hop < 2:
            early = (down_count,) if hop == 0 else ()
            weights.append(fill(index, gu_count, vals[hop], d_blocks, f_blocks, early))
    y, index, _ = lax.optimization_barrier((cotangent, down_index, x))
    down_w = fill(index, down_count, down_vals, f_blocks, d_blocks)
    for flip in flips[:-1]:
        y = jnp.concatenate([y, swap(y, "wide", wide, 2 * flip)], axis=0)
    x, down_w = lax.optimization_barrier((x, down_w))
    x = jnp.concatenate([x, x_recv], axis=0)
    x_pieces = [x, swap(x, "wide", wide, 1)]
    y, _ = lax.optimization_barrier((y, x_recv))
    y_recv = swap(y, "wide", wide, 2 * flips[-1])

    near_own, near_send = gate_up(x_pieces, *weights, 0)
    near_recv = exchange(near_send)
    late, _ = lax.optimization_barrier((x, near_send))
    far_own, far_send = gate_up([late, *x_pieces[1:]], *weights, 1)
    far_recv = exchange(far_send)
    y, y_recv, _ = lax.optimization_barrier((y, y_recv, far_send))
    y_pieces = [y, y_recv, swap(y, "wide", wide, 1), swap(y_recv, "wide", wide, 1)]
    near_hidden, near_coef = activate(near_own, near_recv)
    down_w, near_hidden = lax.optimization_barrier((down_w, near_hidden))
    dh_own, dh_send, turned = d_hidden(y_pieces, x_pieces, down_w)
    y_pieces, dh_send = lax.optimization_barrier((y_pieces, dh_send))
    dh_recv = exchange(dh_send)
    dense = down_first(y_pieces, near_hidden, f_blocks)
    far_own, dense = lax.optimization_barrier((far_own, dense))
    far_hidden, far_coef = activate(far_own, far_recv)
    down_grad = down_second(down_index, down_count, y_pieces, far_hidden, dense, slots)
    down_grad, far_coef = lax.optimization_barrier((down_grad, far_coef))
    halves, d_pair = d_tokens_parts((near_coef, far_coef), dh_own, dh_recv, *weights)

    halves = [own + swap(send, "wide", wide, 1).astype(F32) for own, send in halves]
    kept = chips // 2 * rows
    far = [own[kept:].astype(BF16) for own in halves]
    cut = slots * 2 // 3 if slots % 3 == 0 else slots
    far[1], d_pair = lax.optimization_barrier((far[1], d_pair))
    grads = gu_grads(gu_index, gu_count, d_pair, turned, slots, 0, cut, ())
    halves = [
        own[:kept] + swap(part, "wide", wide, 2 * flips[-1]).astype(F32)
        for own, part in zip(halves, far)
    ]
    own = jnp.concatenate(halves, axis=1)
    sends = [own[p * rows : (p + 1) * rows].astype(BF16) for p in range(1, chips // 2)]
    if cut < slots:
        sends, d_pair, grads = lax.optimization_barrier((sends, d_pair, grads))
        grads = gu_grads(gu_index, gu_count, d_pair, turned, slots, cut, slots, grads)
    own = own[:rows]
    for p, part in enumerate(sends, 1):
        flip = sum(flips[bit] for bit in range(len(flips)) if p >> bit & 1)
        own = own + swap(part, "wide", wide, 2 * flip).astype(F32)
    gate_grad, up_grad = grads
    return (
        own.astype(BF16),
        gate_grad[None, None],
        up_grad[None, None],
        down_grad[None, None],
    )


def solution(mesh):
    in_specs = (
        P("wide", "narrow"),
        P("wide", "narrow"),
        P("narrow", "wide", None, None, None),
        P("narrow", "wide", None, None, None),
        P("narrow", "wide", None),
        P("narrow", "wide"),
        P("wide", "narrow", None, None, None),
        P("wide", "narrow", None),
        P("wide", "narrow"),
    )
    out_specs = (
        P("wide", "narrow"),
        P("narrow", "wide", None, None, None),
        P("narrow", "wide", None, None, None),
        P("wide", "narrow", None, None, None),
    )
    return jax.shard_map(
        on_device, mesh=mesh, in_specs=in_specs, out_specs=out_specs, check_vma=False
    )
```
